32 devices in a mesh: dp: 8 (over z, y), mp: 4 (over x, core).
Axes of the slice: x: 2, y: 2, z: 4, core: 2. Of those that a mesh axis runs over, the one named last changes fastest.
Arguments:
- tokens: bfloat16 [64, 512, 768], P(('dp', 'mp')), may hold values from -6 to 6
- segment_ids: int32 [64, 512], P(('dp', 'mp')), may hold values from 0 to 31, as said below
- cotangent: bfloat16 [64, 512, 768], P(('dp', 'mp')), may hold values from -6 to 6
- norm1_gain: bfloat16 [768], replicated, may hold values from 0.25 to 1.75
- norm1_shift: bfloat16 [768], replicated, may hold values from -1.25 to 1.25
- w_qkv: bfloat16 [768, 3, 768], P(None, None, 'mp'), may hold values from -0.21875 to 0.21875
- qv_bias: bfloat16 [2, 768], P(None, 'mp'), may hold values from -1.25 to 1.25
- w_out: bfloat16 [768, 768], P('mp'), may hold values from -1.25 to 1.25
- out_bias: bfloat16 [768], replicated, may hold values from -1.25 to 1.25
- norm2_gain: bfloat16 [768], replicated, may hold values from 0.25 to 1.75
- norm2_shift: bfloat16 [768], replicated, may hold values from -1.25 to 1.25
- w_up: bfloat16 [768, 3072], P(None, 'mp'), may hold values from -0.21875 to 0.21875
- up_bias: bfloat16 [3072], P('mp'), may hold values from -1.25 to 1.25
- w_down: bfloat16 [3072, 768], P('mp'), may hold values from -0.109375 to 0.109375
- down_bias: bfloat16 [768], replicated, may hold values from -1.25 to 1.25
Outputs:
- mixed: bfloat16 [64, 512, 768], P(('dp', 'mp'))
- input_grad: bfloat16 [64, 512, 768], P(('dp', 'mp'))
- grad_norm1_gain: float32 [768], replicated
- grad_norm1_shift: float32 [768], replicated
- grad_w_qkv: float32 [768, 3, 768], P(None, None, 'mp')
- grad_qv_bias: float32 [2, 768], P(None, 'mp')
- grad_w_out: float32 [768, 768], P('mp')
- grad_out_bias: float32 [768], replicated
- grad_norm2_gain: float32 [768], replicated
- grad_norm2_shift: float32 [768], replicated
- grad_w_up: float32 [768, 3072], P(None, 'mp')
- grad_up_bias: float32 [3072], P('mp')
- grad_w_down: float32 [3072, 768], P('mp')
- grad_down_bias: float32 [768], replicated
The draws below stay inside these ranges and needn't reach their ends.
Inputs may be any that keep to these rules, and one draw needn't show every extreme that they name: `segment_ids`: within each row the ids start at 0 and never fall, rising by one at each new caption; each row holds exactly 32 captions, positions with equal ids in one row forming one caption.
All inputs are finite; a program needn't handle non-finite values.
Results may differ from the reference program's by a relative error of at most 0.019.
Values may be sent and summed in bfloat16 or wider, within the bound.
A program may use at most 192 MiB of HBM per device.

```python
import math
import jax
import jax.numpy as jnp
from jax import lax

D = 768
HEADS = 12
HEAD = 64
FF = 3072
SEQ = 512
ROWS = 64


def draw_segment_ids(key, part):
    key = jax.random.fold_in(key, 11)
    caption_count = SEQ // 16
    row_keys = jax.random.split(key, ROWS)

    def one_row(row_key):
        order = jax.random.permutation(row_key, SEQ - 1).astype(jnp.int32) + 1
        picks = order[:caption_count - 1]
        place = lax.broadcasted_iota(jnp.int32, (caption_count - 1, SEQ), 1)
        starts = jnp.sum((place == picks[:, None]).astype(jnp.int32), axis=0)
        return jnp.cumsum(starts).astype(jnp.int32)
    return jax.vmap(one_row)(row_keys).astype(jnp.int32)


def shard_levels(rng, extent, cuts, low, high):
    gain, own = 1.0, jax.random.fold_in(rng, 6)
    for position, parts in cuts:
        steps = jnp.exp(jax.random.uniform(jax.random.fold_in(own, position), (parts,), jnp.float32, low / len(cuts), high / len(cuts)))
        gain = gain * jnp.repeat(steps, extent[position] // parts).reshape([-1 if axis == position else 1 for axis in range(len(extent))])
    return gain


def bell_draw(stream_key, extent, spread, most, cuts=(), held_as=jnp.bfloat16):
    values = jax.random.normal(stream_key, extent, jnp.float32) * spread
    if len(cuts) > 0:
        values = shard_levels(stream_key, extent, cuts, -0.22, 0.18) * values
    return jnp.clip(values, min=-most, max=most).astype(held_as)


def setup_inputs(seed: int = 0) -> dict:
    seeds = jax.random.split(jax.random.key(seed), 16)
    tokens = bell_draw(seeds[0], (ROWS, SEQ, D), 1.0, 6.0, ((0, 32),))
    segment_ids = draw_segment_ids(jax.random.fold_in(seeds[15], 71), 0)
    cotangent = bell_draw(seeds[2], (ROWS, SEQ, D), 1.0, 6.0, ((0, 32),))
    norm1_gain = jnp.clip(1.0 + 0.15 * jax.random.normal(seeds[3], (D,), jnp.float32), 0.25, 1.75).astype(jnp.bfloat16)
    norm1_shift = bell_draw(seeds[4], (D,), 0.2, 1.25)
    w_qkv = bell_draw(seeds[5], (D, 3, D), D ** -0.5, 0.21875, ((2, 4),))
    qv_bias = bell_draw(seeds[6], (2, D), 0.2, 1.25, ((1, 4),))
    w_out = bell_draw(seeds[7], (D, D), (D // 32) ** -0.5, 1.25, ((0, 4),))
    out_bias = bell_draw(seeds[8], (D,), 0.2, 1.25)
    norm2_gain = jnp.clip(1.0 + 0.15 * jax.random.normal(seeds[9], (D,), jnp.float32), 0.25, 1.75).astype(jnp.bfloat16)
    norm2_shift = bell_draw(seeds[10], (D,), 0.2, 1.25)
    w_up = bell_draw(seeds[11], (D, FF), D ** -0.5, 0.21875, ((1, 4),))
    up_bias = bell_draw(seeds[12], (FF,), 0.2, 1.25, ((0, 4),))
    w_down = bell_draw(seeds[13], (FF, D), FF ** -0.5, 0.109375, ((0, 4),))
    down_bias = bell_draw(seeds[14], (D,), 0.2, 1.25)
    return dict(tokens=tokens, segment_ids=segment_ids, cotangent=cotangent, norm1_gain=norm1_gain, norm1_shift=norm1_shift, w_qkv=w_qkv, qv_bias=qv_bias, w_out=w_out, out_bias=out_bias, norm2_gain=norm2_gain, norm2_shift=norm2_shift, w_up=w_up, up_bias=up_bias, w_down=w_down, down_bias=down_bias)


EPS = 1e-06
MASKED = -1e+30
HIGH = lax.Precision.HIGHEST

@jax.custom_vjp
def low(v):
    return lax.optimization_barrier(v.astype(jnp.bfloat16)).astype(jnp.float32)

@jax.custom_vjp
def low_back(v):
    return v

def low_keep(v):
    return (low(v), None)

def low_pass(kept, grad):
    return (grad,)

def back_keep(v):
    return (v, None)

def back_low(kept, grad):
    return (low(grad),)
low.defvjp(low_keep, low_pass)
low_back.defvjp(back_keep, back_low)

def layer_norm(values, gain_f, shift_f):
    average = lax.optimization_barrier(jnp.mean(values, axis=-1, keepdims=True))
    centred = values - average
    inv_std = lax.rsqrt(lax.optimization_barrier(jnp.mean(centred * centred, axis=-1, keepdims=True)) + EPS)
    return centred * inv_std * gain_f + shift_f

def attend_row(row_items):
    queries, key_rows, values, seg_ids = row_items
    scores = jnp.einsum('qhe,khe->hqk', queries, key_rows, precision=HIGH) * HEAD ** (-0.5)
    same_doc = (seg_ids[:, None] == seg_ids[None, :])[None]
    scores = low_back(jnp.where(same_doc, scores, MASKED))
    attn_prob = low(jax.nn.softmax(scores, axis=-1))
    return jnp.einsum('hqk,khe->qhe', attn_prob, values, precision=HIGH)

def forward(inputs, seg_rows, params):
    gain_one, shift_one, w_qkv, qv_bias, w_out, out_bias, gain_two, shift_two, w_up, up_bias, w_down, down_bias = params
    row_count = inputs.shape[0]
    norm_one = low(layer_norm(inputs, gain_one, shift_one))
    projected = jnp.einsum('bsd,dcf->bscf', norm_one, w_qkv, precision=HIGH)
    proj_bias = jnp.stack([qv_bias[0], jnp.zeros_like(qv_bias[0]), qv_bias[1]])
    projected = low(low_back(projected + proj_bias))
    heads_view = projected.reshape(row_count, SEQ, 3, HEADS, HEAD)
    mixed_rows = lax.map(jax.checkpoint(attend_row), (heads_view[:, :, 0], heads_view[:, :, 1], heads_view[:, :, 2], seg_rows))
    mixed_rows = low(low_back(mixed_rows.reshape(row_count, SEQ, D)))
    attn_out = low_back(jnp.einsum('bsf,fd->bsd', mixed_rows, w_out, precision=HIGH) + out_bias)
    middle = inputs + attn_out
    norm_two = low(layer_norm(middle, gain_two, shift_two))
    pre_act = low_back(jnp.einsum('bsd,df->bsf', norm_two, w_up, precision=HIGH) + up_bias)
    hidden = low(jax.nn.gelu(pre_act, approximate=False))
    expert_out = low_back(jnp.einsum('bsf,fd->bsd', hidden, w_down, precision=HIGH) + down_bias)
    return middle + expert_out

def reference(tokens, segment_ids, cotangent, norm1_gain, norm1_shift, w_qkv, qv_bias, w_out, out_bias, norm2_gain, norm2_shift, w_up, up_bias, w_down, down_bias):
    params = tuple((param.astype(jnp.float32) for param in (norm1_gain, norm1_shift, w_qkv, qv_bias, w_out, out_bias, norm2_gain, norm2_shift, w_up, up_bias, w_down, down_bias)))
    row_count = tokens.shape[0]
    block_rows = math.gcd(row_count, 8)
    block_count = row_count // block_rows
    blocks = (tokens.reshape(block_count, block_rows, SEQ, D), segment_ids.reshape(block_count, block_rows, SEQ), cotangent.reshape(block_count, block_rows, SEQ, D))

    def advance(totals, row_items):
        part_input, part_seg, part_cot = row_items

        def run_layer(values, weights):
            return forward(values, part_seg, weights)
        result, pull_back = jax.vjp(run_layer, part_input.astype(jnp.float32), params)
        grad_input, grad_params = pull_back(part_cot.astype(jnp.float32))
        return (jax.tree.map(jnp.add, totals, grad_params), (result.astype(jnp.bfloat16), grad_input.astype(jnp.bfloat16)))
    start = jax.tree.map(jnp.zeros_like, params)
    totals, (mixed, input_grad) = lax.scan(advance, start, blocks)
    return (mixed.reshape(row_count, SEQ, D), input_grad.reshape(row_count, SEQ, D), totals[0], totals[1], totals[2], totals[3], totals[4], totals[5], totals[6], totals[7], totals[8], totals[9], totals[10], totals[11])
```

```python
import jax
import jax.numpy as jnp
from jax import lax
from jax.sharding import PartitionSpec as P

HEAD = 64


EPS = 1e-06
MASKED = -1e30


def flat_dot(left_side, right_side):
    result = jnp.dot(
        left_side.reshape(-1, left_side.shape[-1]), right_side, preferred_element_type=jnp.float32
    )
    return result.reshape(left_side.shape[:-1] + (right_side.shape[-1],))


def back_dot(grad_in, weight):
    result = lax.dot_general(
        grad_in.reshape(-1, grad_in.shape[-1]),
        weight,
        (((1,), (1,)), ((), ())),
        preferred_element_type=jnp.float32,
    )
    return result.reshape(grad_in.shape[:-1] + (weight.shape[0],))


def cross_dot(left_side, right_side):
    return lax.dot_general(
        left_side.reshape(-1, left_side.shape[-1]),
        right_side.reshape(-1, right_side.shape[-1]),
        (((0,), (0,)), ((), ())),
        preferred_element_type=jnp.float32,
    )


def norm_forward(values, gain_f, shift_f):
    average = jnp.mean(values, axis=-1, keepdims=True)
    centred = values - average
    inv_std = lax.rsqrt(jnp.mean(centred * centred, axis=-1, keepdims=True) + EPS)
    normed = centred * inv_std
    return (normed * gain_f + shift_f, normed, inv_std)


def norm_backward(grad_in, normed, inv_std, gain_f):
    scaled = grad_in * gain_f
    inner = (
        scaled
        - jnp.mean(scaled, axis=-1, keepdims=True)
        - normed * jnp.mean(scaled * normed, axis=-1, keepdims=True)
    )
    return (inner * inv_std, jnp.sum(grad_in * normed, axis=(0, 1)), jnp.sum(grad_in, axis=(0, 1)))


def gelu_slope(pre_act):
    cumul = 0.5 * (1.0 + lax.erf(pre_act * 0.7071067811865476))
    return cumul + pre_act * jnp.exp(-0.5 * pre_act * pre_act) * 0.3989422804014327


def masked_scores(queries, key_rows, seg_ids, score_scale):
    scores = (
        jnp.einsum("bqhe,bkhe->bhqk", queries, key_rows, preferred_element_type=jnp.float32)
        * score_scale
    )
    same_doc = (seg_ids[:, :, None] == seg_ids[:, None, :])[:, None]
    return jnp.where(same_doc, scores, MASKED)


def attention_forward(queries, key_rows, values, seg_ids, score_scale):
    scores = masked_scores(queries, key_rows, seg_ids, score_scale)
    highest = jnp.max(scores, axis=-1, keepdims=True)
    log_total = highest + jnp.log(jnp.sum(jnp.exp(scores - highest), axis=-1, keepdims=True))
    attn_prob = jnp.exp(scores - log_total).astype(jnp.bfloat16)
    mixed_heads = jnp.einsum(
        "bhqk,bkhe->bqhe", attn_prob, values, preferred_element_type=jnp.float32
    )
    return (mixed_heads.astype(jnp.bfloat16), log_total)


def attention_backward(queries, key_rows, values, seg_ids, log_total, grad_mixed, score_scale):
    attn_prob = jnp.exp(masked_scores(queries, key_rows, seg_ids, score_scale) - log_total)
    grad_values = jnp.einsum(
        "bhqk,bqhe->bkhe",
        attn_prob.astype(jnp.bfloat16),
        grad_mixed,
        preferred_element_type=jnp.float32,
    )
    grad_prob = jnp.einsum(
        "bqhe,bkhe->bhqk", grad_mixed, values, preferred_element_type=jnp.float32
    )
    grad_scores = (
        attn_prob * (grad_prob - jnp.sum(attn_prob * grad_prob, axis=-1, keepdims=True))
    ).astype(jnp.bfloat16)
    grad_queries = (
        jnp.einsum("bhqk,bkhe->bqhe", grad_scores, key_rows, preferred_element_type=jnp.float32)
        * score_scale
    )
    grad_keys = (
        jnp.einsum("bhqk,bqhe->bkhe", grad_scores, queries, preferred_element_type=jnp.float32)
        * score_scale
    )
    return (grad_queries, grad_keys, grad_values)


def on_device(
    tokens,
    segment_ids,
    cotangent,
    norm1_gain,
    norm1_shift,
    w_qkv,
    qv_bias,
    w_out,
    out_bias,
    norm2_gain,
    norm2_shift,
    w_up,
    up_bias,
    w_down,
    down_bias,
):
    score_scale = HEAD ** (-0.5)
    f32, bf16 = jnp.float32, jnp.bfloat16
    width = tokens.shape[-1]
    qkv_all = lax.all_gather(w_qkv, "mp", axis=2, tiled=True).reshape(width, 3 * width)
    qv_all = lax.all_gather(qv_bias, "mp", axis=1, tiled=True).astype(f32)
    out_all = lax.all_gather(w_out, "mp", axis=0, tiled=True)
    up_all = lax.all_gather(w_up, "mp", axis=1, tiled=True)
    upb_all = lax.all_gather(up_bias, "mp", axis=0, tiled=True).astype(f32)
    down_all = lax.all_gather(w_down, "mp", axis=0, tiled=True)
    proj_bias = jnp.stack([qv_all[0], jnp.zeros_like(qv_all[0]), qv_all[1]])
    gain_one = norm1_gain.astype(f32)
    shift_one = norm1_shift.astype(f32)
    gain_two = norm2_gain.astype(f32)
    shift_two = norm2_shift.astype(f32)
    rows, seq = tokens.shape[:2]
    heads = width // HEAD

    x_own = tokens.astype(f32)
    norm_one, hat_one, inv_one = norm_forward(x_own, gain_one, shift_one)
    low_one = norm_one.astype(bf16)
    projected = (
        flat_dot(low_one, qkv_all).reshape(rows, seq, 3, width) + proj_bias
    ).astype(bf16)
    heads_view = projected.reshape(rows, seq, 3, heads, HEAD)
    queries = heads_view[:, :, 0]
    key_rows = heads_view[:, :, 1]
    values = heads_view[:, :, 2]
    mixed_heads, log_total = attention_forward(queries, key_rows, values, segment_ids, score_scale)
    mixed_rows = mixed_heads.reshape(rows, seq, width)
    middle = x_own + flat_dot(mixed_rows, out_all) + out_bias.astype(f32)
    norm_two, hat_two, inv_two = norm_forward(middle, gain_two, shift_two)
    low_two = norm_two.astype(bf16)
    pre_act = flat_dot(low_two, up_all) + upb_all
    hidden = jax.nn.gelu(pre_act, approximate=False).astype(bf16)
    mixed = (middle + flat_dot(hidden, down_all) + down_bias.astype(f32)).astype(bf16)
    grad_top = cotangent.astype(f32)
    grad_downb = jnp.sum(grad_top, axis=(0, 1))
    grad_wdown = cross_dot(hidden, cotangent)
    grad_pre = (back_dot(cotangent, down_all) * gelu_slope(pre_act)).astype(bf16)
    grad_upb = jnp.sum(grad_pre, axis=(0, 1), dtype=f32)
    grad_wup = cross_dot(low_two, grad_pre)
    grad_two = back_dot(grad_pre, up_all)
    grad_norm_two, grad_gain_two, grad_shift_two = norm_backward(
        grad_two, hat_two, inv_two, gain_two
    )
    grad_middle = grad_top + grad_norm_two
    grad_mid_low = grad_middle.astype(bf16)
    grad_outb = jnp.sum(grad_mid_low, axis=(0, 1), dtype=f32)
    grad_wout = cross_dot(mixed_rows, grad_mid_low)
    grad_mixed = back_dot(grad_mid_low, out_all).astype(bf16).reshape(rows, seq, heads, HEAD)
    grad_queries, grad_keys, grad_values = attention_backward(
        queries, key_rows, values, segment_ids, log_total, grad_mixed, score_scale
    )
    grad_proj = jnp.stack(
        [
            grad_queries.reshape(rows, seq, width),
            grad_keys.reshape(rows, seq, width),
            grad_values.reshape(rows, seq, width),
        ],
        axis=2,
    ).astype(bf16)
    proj_sums = jnp.sum(grad_proj, axis=(0, 1), dtype=f32)
    grad_qv = jnp.stack([proj_sums[0], proj_sums[2]])
    grad_proj_flat = grad_proj.reshape(rows, seq, 3 * width)
    grad_qkv = cross_dot(low_one, grad_proj_flat).reshape(width, 3, width)
    grad_one = back_dot(grad_proj_flat, qkv_all)
    grad_norm_one, grad_gain_one, grad_shift_one = norm_backward(
        grad_one, hat_one, inv_one, gain_one
    )
    input_grad = (grad_middle + grad_norm_one).astype(bf16)

    def spread(value, axis):
        return lax.psum_scatter(
            value.astype(bf16), "mp", scatter_dimension=axis, tiled=True
        )

    grad_qkv, grad_wout, grad_wup, grad_wdown = lax.psum(
        (spread(grad_qkv, 2), spread(grad_wout, 0), spread(grad_wup, 1), spread(grad_wdown, 0)),
        "dp",
    )
    parts = [
        grad_gain_one, grad_shift_one, grad_outb, grad_gain_two, grad_shift_two, grad_downb,
        grad_qv.reshape(-1), grad_upb,
    ]
    sizes = [part.shape[0] for part in parts]
    total = lax.psum(jnp.concatenate(parts), ("dp", "mp"))
    pieces, start = [], 0
    for size in sizes:
        pieces.append(total[start : start + size])
        start += size
    me = lax.axis_index("mp")
    qv_here = qv_bias.shape[1]
    grad_qv = lax.dynamic_slice_in_dim(pieces[6].reshape(2, width), me * qv_here, qv_here, 1)
    up_here = up_bias.shape[0]
    grad_upb = lax.dynamic_slice_in_dim(pieces[7], me * up_here, up_here, 0)
    return (
        mixed,
        input_grad,
        pieces[0],
        pieces[1],
        grad_qkv.astype(f32),
        grad_qv,
        grad_wout.astype(f32),
        pieces[2],
        pieces[3],
        pieces[4],
        grad_wup.astype(f32),
        grad_upb,
        grad_wdown.astype(f32),
        pieces[5],
    )


def solution(mesh):
    placed = (
        P(("dp", "mp"), None, None),
        P(("dp", "mp"), None),
        P(("dp", "mp"), None, None),
        P(),
        P(),
        P(None, None, "mp"),
        P(None, "mp"),
        P("mp", None),
        P(),
        P(),
        P(),
        P(None, "mp"),
        P("mp"),
        P("mp", None),
        P(),
    )
    return jax.shard_map(
        on_device,
        mesh=mesh,
        in_specs=placed,
        out_specs=(
            P(("dp", "mp"), None, None),
            P(("dp", "mp"), None, None),
            P(),
            P(),
            P(None, None, "mp"),
            P(None, "mp"),
            P("mp", None),
            P(),
            P(),
            P(),
            P(None, "mp"),
            P("mp"),
            P("mp", None),
            P(),
        ),
        check_vma=False,
    )
```

```python
import functools

import jax
import jax.numpy as jnp
from jax import lax
from jax.experimental import pallas as pl
from jax.experimental.pallas import tpu as pltpu
from jax.sharding import PartitionSpec as P

HEAD = 64
EPS = 1e-06
MASKED = -1e30
UNIT = 256
SPLIT = 2
INV_LANE = 32
F32, BF16 = jnp.float32, jnp.bfloat16

GAIN1, SHIFT1, OUTB, GAIN2, SHIFT2, DOWNB, QUERYB, VALUEB, UPB = range(9)

BETWEEN, FIRST_HEADS, LAST_NORM, STEPS = 12, 13, 19, 27
FAR_PAIRS = (0, 1, 0, 1, 1, 0)

WHEN = {
    "pass_x": {0: 4, 1: 5, 3: 6},
    "pass_z": {1: 4, 3: 5, 5: 6},
    "pass_y": {2: 4, 5: 5, 7: 6},
    "pass_done": {2: 4, 6: 5, 8: 6},
    "mate_done": {0: 4, 4: 5, 10: 6},
    "pair_send": {1: 0, 3: 1, 5: 2, 7: 3, 9: 4, 11: 5},
    "pair_add": {2: 0, 4: 1, 6: 2, 8: 3, 10: 4, 12: 5},
    "far_send": {14: 0, 15: 1, 16: 2},
    "far_add": {15: 0, 16: 1, 17: 2},
    "near_send": {17: 0, 18: 1, 19: 2},
    "near_add": {18: 0, 19: 1, 20: 2},
    "add_x": {8: 0, 11: 1, 13: 2, 15: 3, 17: 4, 18: 5, 20: 6, 21: 7, 22: 8},
    "add_y": {10: 0, 13: 1, 15: 2, 16: 3, 18: 4, 20: 5, 21: 6, 22: 7, 23: 8},
    "add_z": {12: 0, 14: 1, 16: 2, 17: 3, 19: 4, 21: 5, 22: 6, 23: 7, 24: 8},
    "give_y": {13: 0, 15: 1, 17: 2, 18: 3, 20: 4, 22: 5, 23: 6, 24: 7, 25: 8},
    "finish": {15: 0, 17: 1, 18: 2, 19: 3, 21: 4, 23: 5, 24: 6, 25: 7, 26: 8},
    "sums": {20: 0, 21: 1, 22: 2, 23: 3, 24: 4},
}


def dot(left, right, left_dim, right_dim):
    return lax.dot_general(
        left, right, (((left_dim,), (right_dim,)), ((), ())), preferred_element_type=F32
    )


def column_sum(values):
    return jnp.sum(values, axis=0, keepdims=True)


def gelu_parts(pre):
    size = jnp.abs(pre) * 0.7071067811865476
    part = 1.0 / (1.0 + 0.3275911 * size)
    tail = jnp.exp(-0.5 * pre * pre)
    poly = part * (
        0.254829592
        + part * (-0.284496736 + part * (1.421413741 + part * (-1.453152027 + part * 1.061405429)))
    )
    half = 0.5 * poly * tail
    return jnp.where(pre >= 0, 1.0 - half, half), tail * 0.3989422804014327


def kernel(
    x_in, g_in, seg_ref, small_ref, bias_in, qkv_in, out_in, up_in, down_in,
    mixed_out, input_out, grads_out, sums_out,
    wq, wo, wm, wb, grad, mate_buf, x_buf, y_buf, z_buf,
    x_ref, g_ref, a1_ref, proj_ref, o_ref, x1_ref, hat2_ref, a2_ref, da2_ref,
    hid_ref, low_ref, lse_ref, aug_q, aug_k, sums, sums_recv,
    local_sem, wm_s, wm_r, wx_s, wx_r, wy_s, wy_r, wz_s, wz_r, wf_s, wf_r, wb_s, wb_r,
    pair_s, pair_r, ex_s, ex_r, ey_s, ey_r, ez_s, ez_r, fz_s, fz_r, fy_s, fy_r, sums_s, sums_r,
    *, rows, seq,
):
    tokens, width = x_ref.shape
    dp, mp = lax.axis_index("dp"), lax.axis_index("mp")
    c, x = mp % 2, mp // 2
    y, z = dp % 2, (dp // 2) % 4
    block = dp - dp % 8
    zb = z % 2
    nx, nc, ny = 1 - x, 1 - c, 1 - y

    def device(zz, yy, xx, cc):
        return (block + zz * 2 + yy, xx * 2 + cc)

    mate = device(z, y, x, nc)
    x_peer = device(z, y, nx, c)
    y_peer = device(z, ny, x, c)
    z_peers = [device((z + step) % 4, y, x, c) for step in (1, 2, 3)]
    z_pair = device(z + 1 - 2 * zb, y, x, c)
    cross = device(z, y, nx, nc)

    def remote(src, dst, send, recv, where):
        return pltpu.make_async_remote_copy(
            src_ref=src, dst_ref=dst, send_sem=send, recv_sem=recv,
            device_id=where, device_id_type=pl.DeviceIdType.MESH,
        )

    up_stage = grad.at[0, 0, pl.ds(0, width)]
    locals_ = [
        pltpu.make_async_copy(qkv_in, wq.at[x, :, :, c], local_sem.at[0]),
        pltpu.make_async_copy(x_in, x_ref, local_sem.at[1]),
        pltpu.make_async_copy(bias_in, wb.at[x, c], local_sem.at[2]),
        pltpu.make_async_copy(out_in, wo.at[x, :, c], local_sem.at[3]),
        pltpu.make_async_copy(up_in, up_stage, local_sem.at[4]),
        pltpu.make_async_copy(down_in, wm.at[x, c, :, pl.ds(UNIT, UNIT)], local_sem.at[5]),
        pltpu.make_async_copy(g_in, g_ref, local_sem.at[6]),
    ]
    for copy in locals_:
        copy.start()

    barrier = pltpu.get_barrier_semaphore()
    everyone = [mate, x_peer, cross, y_peer] + z_peers
    for peer in everyone:
        pl.semaphore_signal(barrier, inc=1, device_id=peer, device_id_type=pl.DeviceIdType.MESH)
    pl.semaphore_wait(barrier, len(everyone))

    third = width // 3

    def piece(kind, index, xx, cc, lanes=slice(None)):
        if kind == "q":
            return wq.at[xx, index, :, cc, :, lanes]
        if kind == "o":
            return wo.at[xx, :, cc, :, lanes]
        return wm.at[xx, cc, index, :, lanes]

    def lanes_of(part):
        return pl.ds(pl.multiple_of(part * third, third), third)

    part_x = jnp.where(zb == 1, 2, y)
    part_z = jnp.where(zb == 1, y, 2)

    def kinds(number, run):
        if isinstance(number, int):
            run("q" if number < 3 else "o" if number == 3 else "m", number - 4 if number > 3 else number)
            return
        pl.when(number < 3)(lambda: run("q", number))
        pl.when(number == 3)(lambda: run("o", number))
        pl.when(number > 3)(lambda: run("m", number - 4))

    def to_mate(number, kind, index):
        own = piece(kind, index, x, c)
        return remote(own, own, wm_s.at[number], wm_r.at[number], mate)

    def to_x(number, kind, index):
        own = piece(kind, index, x, c, lanes_of(part_x))
        return remote(own, own, wx_s.at[number], wx_r.at[number], x_peer)

    def on_z(number, kind, index, part):
        held = piece(kind, index, nx, c, lanes_of(part))
        return remote(held, held, wz_s.at[number], wz_r.at[number], z_pair)

    def on_y(number, kind, index, part):
        held = piece(kind, index, nx, c, lanes_of(part))
        return remote(held, held, wy_s.at[number], wy_r.at[number], y_peer)

    def forward(number, kind, index):
        held = piece(kind, index, nx, c)
        return remote(held, held, wf_s.at[number], wf_r.at[number], mate)

    def mate_done(number):
        kinds(number, lambda kind, index: to_mate(number, kind, index).wait_recv())

    def start_x(number):
        kinds(number, lambda kind, index: to_x(number, kind, index).start())

    def pass_x(number):
        def run(kind, index):
            to_x(number, kind, index).wait_recv()
            on_z(number, kind, index, part_x).start()
            pl.when(zb == 0)(lambda: on_y(number, kind, index, part_x).start())

        kinds(number, run)
        pl.when(number < 5)(lambda: start_x(number + 2))

    def pass_z(number):
        def run(kind, index):
            on_z(number, kind, index, part_x).wait_recv()
            pl.when(zb == 1)(lambda: on_y(number, kind, index, part_z).start())

        kinds(number, run)

    def pass_y(number):
        def run(kind, index):
            on_y(number, kind, index, part_x).wait_recv()
            forward(number, kind, index).start()

        kinds(number, run)

    def pass_done(number):
        kinds(number, lambda kind, index: forward(number, kind, index).wait_recv())

    biases = [
        remote(wb.at[x, c], wb.at[x, c], wb_s.at[i], wb_r.at[i], peer)
        for i, peer in enumerate((mate, x_peer, cross))
    ]
    locals_[0].wait()
    start_x(0)
    for number in range(3):
        to_mate(number, "q", number).start()
    locals_[2].wait()
    for copy in biases:
        copy.start()
    start_x(1)
    locals_[3].wait()
    to_mate(3, "o", 3).start()

    chunk = 128
    locals_[1].wait()

    def small(row):
        return small_ref[row : row + 1, :]

    def norm(values):
        centred = values - jnp.mean(values, axis=-1, keepdims=True)
        inv = lax.rsqrt(jnp.mean(centred * centred, axis=-1, keepdims=True) + EPS)
        return centred * inv, inv

    def at_chunk(step):
        return pl.ds(pl.multiple_of(step * chunk, chunk), chunk)

    def first_norm(step, carry):
        where = at_chunk(step)
        hat, _ = norm(x_ref[where, :].astype(F32))
        a1_ref[where, :] = (small(0) * hat + small(1)).astype(BF16)
        return carry

    lax.fori_loop(0, tokens // chunk, first_norm, 0)

    lane = lax.broadcasted_iota(jnp.int32, (seq, 128), 1)
    for row in range(rows):
        ids = jnp.broadcast_to(seg_ref[row : row + 1, :].astype(F32), (128, seq)).T
        spot = lane % 64
        same = spot == ids.astype(jnp.int32)
        inside = spot < 32
        where = pl.ds(row * seq, seq)
        aug_q[where, :] = jnp.where(same, 1.0, 0.0).astype(BF16)
        aug_k[where, :] = jnp.where(jnp.logical_and(inside, jnp.logical_not(same)), MASKED, 0.0).astype(BF16)

    even = lane < 64

    def pick(values, others):
        return jnp.where(even, values, others), jnp.where(even, others, values)

    def attend_forward(step):
        xx, t = jnp.where(step < 3, x, nx), step % 3
        weights = wq[xx, t].reshape(3 * 128, width)
        biasq = wb[xx, 0, 1:2, :].astype(F32) + wb[xx, 1, 1:2, :].astype(F32)
        biasv = wb[xx, 0, 2:3, :].astype(F32) + wb[xx, 1, 2:3, :].astype(F32)
        pq = jnp.where(t == 0, biasq[:, :128], jnp.where(t == 1, biasq[:, 128:256], biasq[:, 256:384]))
        pv = jnp.where(t == 0, biasv[:, :128], jnp.where(t == 1, biasv[:, 128:256], biasv[:, 256:384]))
        for row in range(rows):
            where = pl.ds(row * seq, seq)
            value = dot(a1_ref[where, :], weights, 1, 1)
            proj_ref[xx, t, where, 0:128] = ((value[:, :128] + pq).astype(BF16) * 0.125).astype(BF16)
            proj_ref[xx, t, where, 128:256] = value[:, 128:256].astype(BF16)
            proj_ref[xx, t, where, 256:384] = (value[:, 256:] + pv).astype(BF16)
        group = xx * 3 + t
        for row in range(rows):
            where = pl.ds(row * seq, seq)
            qs = pick(proj_ref[xx, t, where, 0:128], aug_q[where, :])
            ks = pick(proj_ref[xx, t, where, 128:256], aug_k[where, :])
            vs = pick(proj_ref[xx, t, where, 256:384], jnp.ones((seq, 128), BF16))
            highest, result = [], []
            for q, k, v in zip(qs, ks, vs):
                scores = dot(q, k, 1, 1)
                top = jnp.max(scores, axis=-1, keepdims=True)
                highest.append(top)
                result.append(dot(jnp.exp(scores - top).astype(BF16), v, 1, 0))
            total = pltpu.roll(jnp.where(even, result[1], result[0]), 64, 1)
            mixed = jnp.where(even, result[0], result[1]) / total
            o_ref[where, pl.ds(pl.multiple_of(group * 128, 128), 128)] = mixed.astype(BF16)
            log_total = jnp.where(even, highest[0], highest[1]) + jnp.log(total)
            lse_ref[where, :] = jnp.where(lane % 64 == group, log_total, lse_ref[where, :])

    lse_ref[...] = jnp.zeros_like(lse_ref)

    def forward_step(step, carry):
        @pl.when(step == 0)
        def _():
            biases[0].wait_recv()

        @pl.when(step == 3)
        def _():
            biases[1].wait_recv()
            biases[2].wait_recv()

        pl.when(jnp.logical_and(step >= 1, step < 5))(lambda: pass_x(step - 1))
        pl.when(step >= 2)(lambda: pass_z(step - 2))
        pl.when(step >= 3)(lambda: pass_y(step - 3))
        pl.when(step >= 3)(lambda: pass_done(step - 3))
        pl.when(step < 3)(lambda: mate_done(step))
        attend_forward(step)

        @pl.when(step == 0)
        def _():
            locals_[4].wait()
            locals_[5].wait()
            for index in range(3):
                wm[x, c, index, pl.ds(0, UNIT), :] = up_stage[:, index * UNIT : (index + 1) * UNIT].T
                to_mate(4 + index, "m", index).start()

        return carry

    lax.fori_loop(0, 6, forward_step, 0)
    pass_y(3)
    mate_done(3)
    pass_done(3)

    def second_norm(step, carry):
        where = pl.ds(pl.multiple_of(step * 256, 256), 256)
        value = x_ref[where, :].astype(F32) + dot(o_ref[where, :], wo[...].reshape(width, width), 1, 0) + small(2)
        hat, inv = norm(value)
        hat2_ref[where, :] = hat.astype(BF16)
        spot = lax.broadcasted_iota(jnp.int32, (256, 128), 1)
        lse_ref[where, :] = jnp.where(spot == INV_LANE, inv, lse_ref[where, :])
        a2_ref[where, :] = (small(3) * hat + small(4)).astype(BF16)
        x1_ref[where, :] = value + small(5)
        da2_ref[where, :] = jnp.zeros_like(value)
        return carry

    lax.fori_loop(0, tokens // 256, second_norm, 0)
    sums[...] = jnp.zeros_like(sums)
    locals_[6].wait()

    def pair_place(pair):
        far = sum(jnp.where(pair == p, 1, 0) for p, flag in enumerate(FAR_PAIRS) if flag)
        return jnp.where(far == 1, nx, x), pair // 2

    def expert_tile(step):
        xx, index = pair_place(step // 2)
        cc = jnp.where(step % 2 == 0, nc, c)
        w_up = wm[xx, cc, index, pl.ds(0, UNIT), :]
        w_down = wm[xx, cc, index, pl.ds(UNIT, UNIT), :]
        lanes = pl.ds(pl.multiple_of(index * UNIT, UNIT), UNIT)
        bias = wb[xx, cc, 0:1, lanes].astype(F32)
        upb_sum = None
        part_rows = tokens // SPLIT
        for part in range(SPLIT):
            where = pl.ds(part * part_rows, part_rows)
            pre = dot(a2_ref[where, :], w_up, 1, 1) + bias
            back = dot(g_ref[where, :], w_down, 1, 1)
            cumul, density = gelu_parts(pre)
            hidden = (pre * cumul).astype(BF16)
            low = (back * (cumul + pre * density)).astype(BF16)
            hid_ref[where, :] = hidden
            low_ref[where, :] = low
            one = column_sum(low.astype(F32))
            upb_sum = one if upb_sum is None else upb_sum + one
            x1_ref[where, :] += dot(hidden, w_down, 1, 0)
            da2_ref[where, :] += dot(low, w_up, 1, 0)
        sums[pl.ds(UPB + xx * 2 + cc, 1), lanes] = upb_sum
        base = pl.multiple_of(index * 2 * UNIT, UNIT)
        grad[xx, cc, pl.ds(base, UNIT), :] = dot(low_ref[...], a2_ref[...], 0, 0).astype(BF16)
        grad[xx, cc, pl.ds(base + UNIT, UNIT), :] = dot(hid_ref[...], g_ref[...], 0, 0).astype(BF16)

    def norm_back(grad_in, hat, inv, gain):
        scaled = grad_in * gain
        return inv * (
            scaled
            - jnp.mean(scaled, axis=-1, keepdims=True)
            - hat * jnp.mean(scaled * hat, axis=-1, keepdims=True)
        )

    def add_sum(row, values):
        sums[row : row + 1, :] += column_sum(values)

    heads_rows = 6 * UNIT

    def between():
        def one(step, carry):
            where = at_chunk(step)
            da2, hat = da2_ref[where, :], hat2_ref[where, :].astype(F32)
            top = g_ref[where, :].astype(F32)
            add_sum(GAIN2, da2 * hat)
            add_sum(SHIFT2, da2)
            add_sum(DOWNB, top)
            middle = top + norm_back(da2, hat, lse_ref[where, INV_LANE : INV_LANE + 1], small(3))
            da2_ref[where, :] = middle
            low = middle.astype(BF16)
            add_sum(OUTB, low.astype(F32))
            a2_ref[where, :] = low
            hat2_ref[where, :] = x1_ref[where, :].astype(BF16)
            return carry

        lax.fori_loop(0, tokens // chunk, one, 0)
        mixed_copy.start()
        for xx in range(2):
            half = dot(o_ref[:, xx * 384 : (xx + 1) * 384], a2_ref[...], 0, 0).astype(BF16)
            for t in range(3):
                for cc in range(2):
                    start = (t * 2 + cc) * 64
                    grad[xx, cc, pl.ds(heads_rows + t * 64, 64), :] = half[start : start + 64]

        def back(step, carry):
            where = pl.ds(pl.multiple_of(step * 256, 256), 256)
            a2_ref[where, :] = dot(a2_ref[where, :], wo[...].reshape(width, width), 1, 1).astype(BF16)
            return carry

        lax.fori_loop(0, tokens // 256, back, 0)

    def attend_backward(step):
        xx, t = jnp.where(step < 3, nx, x), step % 3
        group = xx * 3 + t
        lanes = pl.ds(pl.multiple_of(group * 128, 128), 128)

        def one_row(row, carry):
            where = pl.ds(pl.multiple_of(row * seq, seq), seq)
            query, key, value = (proj_ref[xx, t, where, i * 128 : (i + 1) * 128] for i in range(3))
            out, back = o_ref[where, lanes], a2_ref[where, lanes]
            none = jnp.zeros((seq, 128), BF16)
            product = out.astype(F32) * back.astype(F32)
            log_total = lse_ref[where, :]
            spot = lane % 64
            tops = [
                jnp.sum(jnp.where(lane == group + shift, log_total, 0.0), axis=-1, keepdims=True)
                for shift in (0, 64)
            ]
            deltas = [jnp.sum(item, axis=-1, keepdims=True) for item in pick(product, jnp.zeros_like(product))]
            q_aug, k_aug = pick(query, aug_q[where, :]), pick(key, aug_k[where, :])
            q_own, k_own, b_own = pick(query, none), pick(key, none), pick(back, none)
            v_aug = pick(value, jnp.where(spot < 3, 1.0, 0.0).astype(BF16))
            splits = []
            for delta in deltas:
                first = (-delta).astype(BF16).astype(F32)
                second = (-delta - first).astype(BF16).astype(F32)
                last = -delta - first - second
                splits.append(
                    jnp.where(spot == 0, first, jnp.where(spot == 1, second, jnp.where(spot == 2, last, 0.0)))
                )
            b_aug = (
                jnp.where(even, back, splits[0].astype(BF16)),
                jnp.where(even, splits[1].astype(BF16), back),
            )
            d_query = d_key = d_value = None
            for i in range(2):
                prob = jnp.exp(dot(q_aug[i], k_aug[i], 1, 1) - tops[i])
                low = prob.astype(BF16)
                inner = dot(b_aug[i], v_aug[i], 1, 1)
                d_score = (prob * inner).astype(BF16)
                parts = (dot(d_score, k_own[i], 1, 0), dot(d_score, q_own[i], 0, 0), dot(low, b_own[i], 0, 0))
                if i == 0:
                    d_query, d_key, d_value = parts
                else:
                    d_query, d_key, d_value = d_query + parts[0], d_key + parts[1], d_value + parts[2]
            low_query = (d_query * 0.125).astype(BF16)
            low_value = d_value.astype(BF16)
            proj_ref[xx, t, where, 0:128] = low_query
            proj_ref[xx, t, where, 128:256] = d_key.astype(BF16)
            proj_ref[xx, t, where, 256:384] = low_value
            sums[QUERYB : QUERYB + 1, lanes] += column_sum(low_query.astype(F32))
            sums[VALUEB : VALUEB + 1, lanes] += column_sum(low_value.astype(F32))
            return carry

        lax.fori_loop(0, rows, one_row, 0)
        whole = proj_ref[xx, t]
        weight_grad = dot(whole, a1_ref[...], 0, 0).astype(BF16)
        for part in range(3):
            for cc in range(2):
                start = part * 128 + cc * 64
                place = pl.multiple_of(heads_rows + 192 + t * 192 + part * 64, 64)
                grad[xx, cc, pl.ds(place, 64), :] = weight_grad[start : start + 64]
        part = dot(whole, wq[xx, t].reshape(3 * 128, width), 1, 0)

        @pl.when(step == 0)
        def _():
            x1_ref[...] = part

        @pl.when(step > 0)
        def _():
            x1_ref[...] += part

    def last_norm():
        def one(step, carry):
            where = at_chunk(step)
            hat, inv = norm(x_ref[where, :].astype(F32))
            da1 = x1_ref[where, :]
            add_sum(GAIN1, da1 * hat)
            add_sum(SHIFT1, da1)
            g_ref[where, :] = (da2_ref[where, :] + norm_back(da1, hat, inv, small(0))).astype(BF16)
            return carry

        lax.fori_loop(0, tokens // chunk, one, 0)
        input_copy.start()

    mixed_copy = pltpu.make_async_copy(hat2_ref, mixed_out, local_sem.at[7])
    input_copy = pltpu.make_async_copy(g_ref, input_out, local_sem.at[8])

    def add_into(xx, start, count, other, other_start):
        def one(step, carry):
            mine = pl.ds(pl.multiple_of(start + step * 32, 32), 32)
            theirs = pl.ds(pl.multiple_of(other_start + step * 32, 32), 32)
            grad[xx, c, mine, :] = (grad[xx, c, mine, :].astype(F32) + other[theirs, :].astype(F32)).astype(BF16)
            return carry

        lax.fori_loop(0, count // 32, one, 0)

    def pair_copy(xx, granule, start, count):
        return remote(
            grad.at[xx, nc, pl.ds(start, count)],
            mate_buf.at[granule % 2, pl.ds(0, count)],
            pair_s.at[granule], pair_r.at[granule], mate,
        )

    def x_copy(unit):
        where = pl.ds(pl.multiple_of(unit * UNIT, UNIT), UNIT)
        return remote(grad.at[nx, c, where], x_buf.at[where], ex_s.at[unit], ex_r.at[unit], x_peer)

    def granule_add(xx, granule, start, count):
        pair_copy(xx, granule, start, count).wait_recv()
        add_into(xx, start, count, mate_buf.at[granule % 2], 0)

    def tile_start(index):
        return pl.multiple_of(index * 2 * UNIT, 2 * UNIT)

    def pair_send(pair):
        xx, index = pair_place(pair)
        pair_copy(xx, pair, tile_start(index), 2 * UNIT).start()

    def pair_add(pair):
        xx, index = pair_place(pair)
        granule_add(xx, pair, tile_start(index), 2 * UNIT)

        @pl.when(xx == nx)
        def _():
            x_copy(2 * index).start()
            x_copy(2 * index + 1).start()

    def heads_start(number):
        return pl.multiple_of(heads_rows + number * UNIT, UNIT)

    def far_send(number):
        pair_copy(nx, 6 + number, heads_start(number), UNIT).start()

    def far_add(number):
        granule_add(nx, 6 + number, heads_start(number), UNIT)
        x_copy(6 + number).start()

    def near_send(number):
        pair_copy(x, 9 + number, heads_start(number), UNIT).start()

    def near_add(number):
        granule_add(x, 9 + number, heads_start(number), UNIT)

    half = UNIT // 2
    share = half // 4

    def y_copy(unit):
        return remote(
            grad.at[x, c, pl.ds(pl.multiple_of(unit * UNIT + ny * half, half), half)],
            y_buf.at[pl.ds(pl.multiple_of(unit * half, half), half)],
            ey_s.at[unit], ey_r.at[unit], y_peer,
        )

    def share_rows(unit, yy, zz):
        return pl.ds(pl.multiple_of(unit * UNIT + yy * half + zz * share, share), share)

    def z_copy(unit, step):
        return remote(
            grad.at[x, c, share_rows(unit, y, (z + step) % 4)],
            z_buf.at[unit, step - 1], ez_s.at[unit, step - 1], ez_r.at[unit, step - 1], z_peers[step - 1],
        )

    def back_z_copy(unit, step):
        where = share_rows(unit, y, z)
        return remote(
            x_buf.at[where], x_buf.at[where], fz_s.at[unit, step - 1], fz_r.at[unit, step - 1], z_peers[step - 1]
        )

    def back_y_copy(unit):
        where = pl.ds(pl.multiple_of(unit * UNIT + y * half, half), half)
        return remote(x_buf.at[where], x_buf.at[where], fy_s.at[unit], fy_r.at[unit], y_peer)

    def add_x(unit):
        x_copy(unit).wait_recv()
        start = pl.multiple_of(unit * UNIT, UNIT)
        add_into(x, start, UNIT, x_buf, start)
        y_copy(unit).start()

    def add_y(unit):
        y_copy(unit).wait_recv()
        add_into(x, pl.multiple_of(unit * UNIT + y * half, half), half, y_buf, pl.multiple_of(unit * half, half))
        for step in (1, 2, 3):
            z_copy(unit, step).start()

    def add_z(unit):
        for step in (1, 2, 3):
            z_copy(unit, step).wait_recv()
        where = share_rows(unit, y, z)
        total = grad[x, c, where, :].astype(F32)
        for step in range(3):
            total += z_buf[unit, step].astype(F32)
        x_buf[where, :] = total.astype(BF16)
        for step in (1, 2, 3):
            back_z_copy(unit, step).start()

    def give_y(unit):
        for step in (1, 2, 3):
            back_z_copy(unit, step).wait_recv()
        back_y_copy(unit).start()

    def out_copy(unit):
        where = pl.ds(pl.multiple_of(unit * UNIT, UNIT), UNIT)
        return pltpu.make_async_copy(x_buf.at[where], grads_out.at[where], local_sem.at[9 + unit])

    def finish(unit):
        back_y_copy(unit).wait_recv()
        out_copy(unit).start()

    def sums_copy(slot, source, peer):
        return remote(sums_recv.at[6 + source], sums_recv.at[slot], sums_s.at[slot], sums_r.at[slot], peer)

    small_peers = [(0, 0, mate), (1, 1, x_peer), (2, 2, y_peer)]

    def sums_step(number):
        @pl.when(number == 0)
        def _():
            sums_recv[6] = sums[...]
            sums_copy(*small_peers[0]).start()

        for index in (1, 2):
            @pl.when(number == index)
            def _(index=index):
                sums_copy(*small_peers[index - 1]).wait_recv()
                sums_recv[6 + index] = sums_recv[5 + index] + sums_recv[index - 1]
                sums_copy(*small_peers[index]).start()

        @pl.when(number == 3)
        def _():
            sums_copy(*small_peers[2]).wait_recv()
            sums_recv[9] = sums_recv[8] + sums_recv[2]
            for step in (1, 2, 3):
                sums_copy(2 + step, 3, z_peers[step - 1]).start()

        @pl.when(number == 4)
        def _():
            for step in (1, 2, 3):
                sums_copy(2 + step, 3, z_peers[step - 1]).wait_recv()
            total = None
            for zz in range(4):
                behind = (z - zz + 4) % 4
                value = jnp.where(
                    behind == 0,
                    sums_recv[9],
                    jnp.where(behind == 1, sums_recv[3], jnp.where(behind == 2, sums_recv[4], sums_recv[5])),
                )
                total = value if total is None else total + value
            sums_out[...] = total

    events = {
        "pair_add": pair_add, "far_add": far_add, "near_add": near_add,
        "pair_send": pair_send, "far_send": far_send, "near_send": near_send,
        "pass_x": pass_x, "pass_z": pass_z, "pass_y": pass_y, "pass_done": pass_done, "mate_done": mate_done,
        "add_x": add_x, "add_y": add_y, "add_z": add_z, "give_y": give_y, "finish": finish,
        "sums": sums_step,
    }

    def main_step(step, carry):
        for name, run in events.items():
            number = jnp.int32(-1)
            for at, which in WHEN[name].items():
                number = jnp.where(step == at, which, number)
            pl.when(number >= 0)(functools.partial(run, number))
        pl.when(step < BETWEEN)(lambda: expert_tile(step))
        pl.when(step == BETWEEN)(between)
        pl.when(jnp.logical_and(step >= FIRST_HEADS, step < LAST_NORM))(
            lambda: attend_backward(step - FIRST_HEADS)
        )
        pl.when(step == LAST_NORM)(last_norm)
        return carry

    lax.fori_loop(0, STEPS, main_step, 0)

    mixed_copy.wait()
    input_copy.wait()
    for copy in biases:
        copy.wait_send()

    def piece_sends(number):
        def run(kind, index):
            to_mate(number, kind, index).wait_send()
            to_x(number, kind, index).wait_send()
            on_z(number, kind, index, part_x).wait_send()
            on_y(number, kind, index, part_x).wait_send()
            forward(number, kind, index).wait_send()

        kinds(number, run)

    def last_waits(unit, carry):
        x_copy(unit).wait_send()
        y_copy(unit).wait_send()
        for step in (1, 2, 3):
            z_copy(unit, step).wait_send()
            back_z_copy(unit, step).wait_send()
        back_y_copy(unit).wait_send()
        out_copy(unit).wait()
        pl.when(unit < 7)(lambda: piece_sends(unit))
        @pl.when(unit < 6)
        def _():
            xx, index = pair_place(unit)
            pair_copy(xx, unit, tile_start(index), 2 * UNIT).wait_send()

        @pl.when(unit < 3)
        def _():
            pair_copy(nx, 6 + unit, heads_start(unit), UNIT).wait_send()
            pair_copy(x, 9 + unit, heads_start(unit), UNIT).wait_send()

        return carry

    lax.fori_loop(0, 9, last_waits, 0)
    for slot, source, peer in small_peers:
        sums_copy(slot, source, peer).wait_send()
    for step in (1, 2, 3):
        sums_copy(2 + step, 3, z_peers[step - 1]).wait_send()


def on_device(
    tokens, segment_ids, cotangent, norm1_gain, norm1_shift, w_qkv, qv_bias, w_out, out_bias,
    norm2_gain, norm2_shift, w_up, up_bias, w_down, down_bias,
):
    rows, seq, width = tokens.shape
    count = rows * seq
    me = lax.axis_index("mp")
    core = me % 2
    shard = w_up.shape[1]
    heads = w_out.shape[0] // HEAD
    tiles = shard // UNIT
    units = 2 * tiles + 3

    small = jnp.stack([norm1_gain, norm1_shift, out_bias, norm2_gain, norm2_shift, down_bias]).astype(F32)
    spread = jnp.zeros((2, heads, 2, HEAD), BF16)
    spread = lax.dynamic_update_slice(spread, qv_bias.reshape(2, heads, 1, HEAD), (0, 0, core, 0))
    spread = spread.reshape(2, heads * 2 * HEAD)
    bias = jnp.concatenate(
        [up_bias[None], jnp.pad(spread, ((0, 0), (0, width - spread.shape[1]))), jnp.zeros((13, width), BF16)]
    )
    qkv_rows = jnp.transpose(w_qkv, (1, 2, 0)).reshape(3, heads, HEAD, width).transpose(1, 0, 2, 3)

    any_space = pl.BlockSpec(memory_space=pl.ANY)
    vmem = pl.BlockSpec(memory_space=pltpu.VMEM)
    dma = pltpu.SemaphoreType.DMA
    vm = pltpu.VMEM
    mixed, input_grad, grads, sums = pl.pallas_call(
        functools.partial(kernel, rows=rows, seq=seq),
        out_shape=(
            jax.ShapeDtypeStruct((count, width), BF16),
            jax.ShapeDtypeStruct((count, width), BF16),
            jax.ShapeDtypeStruct((units * UNIT, width), BF16),
            jax.ShapeDtypeStruct((16, width), F32),
        ),
        in_specs=[any_space, any_space, vmem, vmem, any_space, any_space, any_space, any_space, any_space],
        out_specs=(any_space, any_space, any_space, vmem),
        scratch_shapes=[
            vm((2, heads, 3, 2, HEAD, width), BF16),
            vm((2, heads, 2, HEAD, width), BF16),
            vm((2, 2, tiles, 2 * UNIT, width), BF16),
            vm((2, 2, 16, width), BF16),
            vm((2, 2, units * UNIT, width), BF16),
            vm((2, 2 * UNIT, width), BF16),
            vm((units * UNIT, width), BF16),
            vm((units * UNIT // 2, width), BF16),
            vm((units, 3, UNIT // 8, width), BF16),
            vm((count, width), BF16),
            vm((count, width), BF16),
            vm((count, width), BF16),
            vm((2, heads, count, 3 * 128), BF16),
            vm((count, width), BF16),
            vm((count, width), F32),
            vm((count, width), BF16),
            vm((count, width), BF16),
            vm((count, width), F32),
            vm((count, UNIT), BF16),
            vm((count, UNIT), BF16),
            vm((count, 128), F32),
            vm((count, 128), BF16),
            vm((count, 128), BF16),
            vm((16, width), F32),
            vm((10, 16, width), F32),
            dma((9 + units,)),
            dma((7,)), dma((7,)), dma((7,)), dma((7,)), dma((7,)), dma((7,)),
            dma((7,)), dma((7,)), dma((7,)), dma((7,)), dma((3,)), dma((3,)),
            dma((12,)), dma((12,)),
            dma((units,)), dma((units,)), dma((units,)), dma((units,)),
            dma((units, 3)), dma((units, 3)), dma((units, 3)), dma((units, 3)),
            dma((units,)), dma((units,)), dma((6,)), dma((6,)),
        ],
        compiler_params=pltpu.CompilerParams(
            collective_id=0, has_side_effects=True, vmem_limit_bytes=64 * 2**20 - 2**16
        ),
    )(
        tokens.reshape(count, width), cotangent.reshape(count, width), segment_ids, small, bias,
        qkv_rows, w_out.reshape(heads, HEAD, width), w_up, w_down.reshape(tiles, UNIT, width),
    )

    groups = lax.axis_size("dp") // 8
    if groups > 1:
        grads, sums = lax.psum((grads.astype(F32) * 0.125, sums * 0.125), "dp")
    grads = grads.astype(F32)
    split = 2 * tiles * UNIT
    expert = grads[:split].reshape(tiles, 2, UNIT, width)
    grad_up = expert[:, 0].reshape(shard, width).T
    grad_down = expert[:, 1].reshape(shard, width)
    grad_out = grads[split : split + heads * HEAD]
    grad_qkv = grads[split + heads * HEAD :].reshape(heads, 3, HEAD, width)
    grad_qkv = grad_qkv.transpose(3, 1, 0, 2).reshape(width, 3, heads * HEAD)
    grad_qv = sums[QUERYB : VALUEB + 1].reshape(2, 2, heads, 2, HEAD)
    grad_qv = lax.dynamic_slice(grad_qv, (0, me // 2, 0, core, 0), (2, 1, heads, 1, HEAD)).reshape(2, heads * HEAD)
    grad_upb = lax.dynamic_slice(sums, (UPB + me, 0), (1, width))[0]
    return (
        mixed.reshape(rows, seq, width),
        input_grad.reshape(rows, seq, width),
        sums[GAIN1],
        sums[SHIFT1],
        grad_qkv,
        grad_qv,
        grad_out,
        sums[OUTB],
        sums[GAIN2],
        sums[SHIFT2],
        grad_up,
        grad_upb,
        grad_down,
        sums[DOWNB],
    )


def solution(mesh):
    tall = P(("dp", "mp"), None, None)
    return jax.shard_map(
        on_device,
        mesh=mesh,
        in_specs=(
            tall, P(("dp", "mp"), None), tall, P(), P(), P(None, None, "mp"), P(None, "mp"), P("mp", None),
            P(), P(), P(), P(None, "mp"), P("mp"), P("mp", None), P(),
        ),
        out_specs=(
            tall, tall, P(), P(), P(None, None, "mp"), P(None, "mp"), P("mp", None), P(), P(), P(),
            P(None, "mp"), P("mp"), P("mp", None), P(),
        ),
        check_vma=False,
    )
```

```python
import functools

import jax
import jax.numpy as jnp
from jax import lax
from jax.experimental import pallas as pl
from jax.experimental.pallas import tpu as pltpu
from jax.sharding import PartitionSpec as P

HEAD = 64
EPS = 1e-06
MASKED = -1e30
UNIT = 256
SPLIT = 2
INV_LANE = 32
OWN_UP, OWN_QV = 12, 13
F32, BF16 = jnp.float32, jnp.bfloat16

GAIN1, SHIFT1, OUTB, GAIN2, SHIFT2, DOWNB, QUERYB, VALUEB, UPB = range(9)

FAR_PAIRS = (0, 1, 0, 1, 0, 1)
PAIR_TILES = (0, 0, 1, 1, 2, 2)
BETWEEN, FIRST_HEADS, LAST_NORM = 12, 15, 33
PLAN_FORWARD = (
    (("mate_done", 0), ("bias_done", 0),),
    (("pass_x", 0), ("pass_x", 1), ("mate_done", 1),),
    (("mate_done", 2),),
    (("pass_x", 2), ("pass_x", 3), ("pass_z", 0), ("pass_z", 1), ("pass_y", 0), ("pass_done", 0), ("bias_done", 1), ("bias_done", 2),),
    (("pass_x", 4), ("pass_z", 2), ("pass_z", 3), ("pass_y", 1), ("pass_done", 1),),
    (("pass_x", 5), ("pass_y", 2), ("pass_done", 2),),
)
PLAN_SECOND = (("pass_x", 6), ("pass_z", 4), ("pass_y", 3), ("mate_done", 3), ("pass_done", 3), )
PLAN_MAIN = (
    (("pass_z", 5), ("mate_done", 4),),
    (("pass_z", 6), ("pass_y", 4), ("pair_send", 0),),
    (("pass_y", 5), ("pass_done", 4),),
    (("pair_add", 0), ("pair_send", 1),),
    (("pass_y", 6), ("pair_add", 1), ("mate_done", 5),),
    (("pair_send", 2),),
    (("pair_add", 2), ("pass_done", 5),),
    (("pair_send", 3), ("add_x", 0),),
    (("pair_add", 3), ("mate_done", 6),),
    (("pair_send", 4), ("add_x", 1), ("add_y", 0),),
    (("pair_add", 4), ("add_z", 0), ("pass_done", 6),),
    (("pair_send", 5), ("add_x", 2), ("add_y", 1),),
    (("pair_add", 5), ("add_z", 1), ("add_far", 0),),
    (("add_y", 2),),
    (("add_x", 3),),
    (("add_far", 1), ("give_y", 0),),
    (("add_z", 2),),
    (("add_y", 3), ("give_y", 1),),
    (("far_send", 0), ("add_x", 4),),
    (("far_add", 0), ("add_z", 3), ("add_far", 2), ("finish", 0),),
    (),
    (("far_send", 1), ("add_x", 5), ("finish", 1),),
    (("far_add", 1), ("add_far", 3), ("add_y", 4), ("give_y", 2),),
    (),
    (("far_send", 2), ("add_y", 5), ("give_y", 3),),
    (("far_add", 2), ("add_z", 4),),
    (("add_z", 5), ("finish", 2),),
    (("near_send", 0),),
    (("near_add", 0), ("add_x", 6), ("add_far", 4), ("finish", 3),),
    (),
    (("near_send", 1), ("add_far", 5), ("give_y", 4),),
    (("near_add", 1), ("add_x", 7), ("add_y", 6),),
    (("give_y", 5),),
    (("near_send", 2), ("add_z", 6), ("finish", 4),),
)
PLAN_DRAIN = (
    ("near_add", 2),
    ("add_x", 8),
    ("sums", 0),
    ("add_y", 7),
    ("sums", 1),
    ("add_far", 6),
    ("add_z", 7),
    ("finish", 5),
    ("sums", 2),
    ("give_y", 6),
    ("sums", 3),
    ("add_y", 8),
    ("sums", 4),
    ("add_far", 7),
    ("add_z", 8),
    ("sums", 5),
    ("finish", 6),
    ("give_y", 7),
    ("add_far", 8),
    ("finish", 7),
    ("give_y", 8),
    ("finish", 8),
)

def dot(left, right, left_dim, right_dim):
    return lax.dot_general(
        left, right, (((left_dim,), (right_dim,)), ((), ())), preferred_element_type=F32
    )


def column_sum(values):
    return jnp.sum(values, axis=0, keepdims=True)


def gelu_parts(pre):
    size = jnp.abs(pre) * 0.7071067811865476
    base = 1.0 + 0.3275911 * size
    part = pl.reciprocal(base, approx=True)
    part = part * (2.0 - base * part)
    tail = jnp.exp(-0.5 * pre * pre)
    poly = part * (
        0.254829592
        + part * (-0.284496736 + part * (1.421413741 + part * (-1.453152027 + part * 1.061405429)))
    )
    half = 0.5 * poly * tail
    return jnp.where(pre >= 0, 1.0 - half, half), tail * 0.3989422804014327


def kernel(
    x_in, g_in, seg_in, gain1_in, shift1_in, outb_in, gain2_in, shift2_in, downb_in, upb_in, qvb_in,
    qkv_in, out_in, up_in, down_in,
    mixed_out, input_out, grads_out, sums_out,
    wq, wo, wm, wb, grad, mate_buf, x_buf, y_buf, z_buf,
    x_ref, g_ref, a1_ref, proj_ref, o_ref, x1_ref, hat2_ref, a2_ref, da2_ref,
    hid_ref, low_ref, lse_ref, aug_q, aug_k, sums, sums_recv,
    seg_ref, gain1_ref, shift1_ref, outb_ref, gain2_ref, shift2_ref, downb_ref, upb_ref, qvb_ref, small_sem,
    local_sem, wm_s, wm_r, wx_s, wx_r, wy_s, wy_r, wz_s, wz_r, wf_s, wf_r, wb_s, wb_r,
    pair_s, pair_r, ex_s, ex_r, ey_s, ey_r, ez_s, ez_r, ew_s, ew_r, fz_s, fz_r, fy_s, fy_r, sums_s, sums_r,
    *, rows, seq,
):
    tokens, width = x_ref.shape
    dp, mp = lax.axis_index("dp"), lax.axis_index("mp")
    c, x = mp % 2, mp // 2
    y, z = dp % 2, (dp // 2) % 4
    block = dp - dp % 8
    zb = z % 2
    nx, nc, ny = 1 - x, 1 - c, 1 - y

    def device(zz, yy, xx, cc):
        return (block + zz * 2 + yy, xx * 2 + cc)

    mate = device(z, y, x, nc)
    x_peer = device(z, y, nx, c)
    y_peer = device(z, ny, x, c)
    z_far = device((z + 2) % 4, y, x, c)
    z_pair = device(z + 1 - 2 * zb, y, x, c)
    cross = device(z, y, nx, nc)

    def remote(src, dst, send, recv, where):
        return pltpu.make_async_remote_copy(
            src_ref=src, dst_ref=dst, send_sem=send, recv_sem=recv,
            device_id=where, device_id_type=pl.DeviceIdType.MESH,
        )

    barrier = pltpu.get_barrier_semaphore()
    everyone = [mate, x_peer, cross, y_peer, z_pair, z_far]
    for peer in everyone:
        pl.semaphore_signal(barrier, inc=1, device_id=peer, device_id_type=pl.DeviceIdType.MESH)

    up_stage = grad.at[0, 0, pl.ds(0, width)]
    locals_ = [
        pltpu.make_async_copy(qkv_in.at[:, 0], wq.at[x, 0, :, c], local_sem.at[0]),
        pltpu.make_async_copy(qkv_in.at[:, 1], wq.at[x, 1, :, c], local_sem.at[1]),
        pltpu.make_async_copy(qkv_in.at[:, 2], wq.at[x, 2, :, c], local_sem.at[2]),
        pltpu.make_async_copy(x_in, x_ref, local_sem.at[3]),
        pltpu.make_async_copy(out_in, wo.at[x, :, c], local_sem.at[4]),
        pltpu.make_async_copy(up_in, up_stage, local_sem.at[5]),
        pltpu.make_async_copy(down_in, wm.at[x, c, :, pl.ds(UNIT, UNIT)], local_sem.at[6]),
        pltpu.make_async_copy(g_in, g_ref, local_sem.at[7]),
    ]
    small_copies = [
        pltpu.make_async_copy(src, dst, small_sem.at[i])
        for i, (src, dst) in enumerate((
            (seg_in, seg_ref), (upb_in, upb_ref), (qvb_in, qvb_ref), (gain1_in, gain1_ref), (shift1_in, shift1_ref),
            (outb_in, outb_ref), (gain2_in, gain2_ref), (shift2_in, shift2_ref), (downb_in, downb_ref),
        ))
    ]
    for copy in small_copies + locals_:
        copy.start()
    for copy in small_copies:
        copy.wait()

    from_lane = lax.broadcasted_iota(jnp.int32, (qvb_ref.shape[1], 384), 0)
    to_lane = lax.broadcasted_iota(jnp.int32, (qvb_ref.shape[1], 384), 1)
    placed = jnp.logical_and(
        from_lane == (to_lane // 128) * 64 + to_lane % 64, (to_lane // 64) % 2 == c
    )
    place = jnp.where(placed, 1.0, 0.0).astype(BF16)
    qv_rows = dot(qvb_ref[...], place, 1, 0)
    qv_rows = jnp.concatenate([qv_rows, jnp.zeros((2, width - 384), F32)], axis=1)
    tile_row = lax.broadcasted_iota(jnp.int32, (16, width), 0)
    wb[x, c] = jnp.where(
        tile_row == 0,
        upb_ref[...].astype(F32).reshape(1, width),
        jnp.where(tile_row == 1, qv_rows[0:1], jnp.where(tile_row == 2, qv_rows[1:2], 0.0)),
    ).astype(BF16)
    lane = lax.broadcasted_iota(jnp.int32, (seq, 128), 1)
    for row in range(rows):
        ids = jnp.broadcast_to(seg_ref[row : row + 1, :].astype(F32), (128, seq)).T
        spot = lane % 64
        same = spot == ids.astype(jnp.int32)
        inside = spot < 32
        where = pl.ds(row * seq, seq)
        aug_q[where, :] = jnp.where(same, 1.0, 0.0).astype(BF16)
        aug_k[where, :] = jnp.where(jnp.logical_and(inside, jnp.logical_not(same)), MASKED, 0.0).astype(BF16)
    lse_ref[...] = jnp.zeros_like(lse_ref)
    locals_[5].wait()
    locals_[6].wait()
    tiles = up_stage.shape[1] // UNIT
    for index in range(tiles):
        wm[x, c, index, pl.ds(0, UNIT), :] = up_stage[:, index * UNIT : (index + 1) * UNIT].T
    for number in (0, 1, 2, 4):
        locals_[number].wait()
    pl.semaphore_wait(barrier, len(everyone))

    third = width // 3

    def piece(kind, index, xx, cc, lanes=slice(None)):
        if kind == "q":
            return wq.at[xx, index, :, cc, :, lanes]
        if kind == "o":
            return wo.at[xx, :, cc, :, lanes]
        return wm.at[xx, cc, index, :, lanes]

    def lanes_of(part):
        return pl.ds(pl.multiple_of(part * third, third), third)

    part_x = jnp.where(zb == 1, 2, y)
    part_z = jnp.where(zb == 1, y, 2)

    def kinds(number, run):
        if isinstance(number, int):
            run("q" if number < 3 else "o" if number == 3 else "m", number - 4 if number > 3 else number)
            return
        pl.when(number < 3)(lambda: run("q", number))
        pl.when(number == 3)(lambda: run("o", number))
        pl.when(number > 3)(lambda: run("m", number - 4))

    def to_mate(number, kind, index):
        own = piece(kind, index, x, c)
        return remote(own, own, wm_s.at[number], wm_r.at[number], mate)

    def to_x(number, kind, index):
        own = piece(kind, index, x, c, lanes_of(part_x))
        return remote(own, own, wx_s.at[number], wx_r.at[number], x_peer)

    def on_z(number, kind, index, part):
        held = piece(kind, index, nx, c, lanes_of(part))
        return remote(held, held, wz_s.at[number], wz_r.at[number], z_pair)

    def on_y(number, kind, index, part):
        held = piece(kind, index, nx, c, lanes_of(part))
        return remote(held, held, wy_s.at[number], wy_r.at[number], y_peer)

    def forward(number, kind, index):
        held = piece(kind, index, nx, c)
        return remote(held, held, wf_s.at[number], wf_r.at[number], mate)

    def mate_done(number):
        kinds(number, lambda kind, index: to_mate(number, kind, index).wait_recv())

    def start_x(number):
        kinds(number, lambda kind, index: to_x(number, kind, index).start())

    def pass_x(number):
        def run(kind, index):
            to_x(number, kind, index).wait_recv()
            on_z(number, kind, index, part_x).start()
            pl.when(zb == 0)(lambda: on_y(number, kind, index, part_x).start())

        kinds(number, run)
        if number < 5:
            start_x(number + 2)

    def pass_z(number):
        def run(kind, index):
            on_z(number, kind, index, part_x).wait_recv()
            pl.when(zb == 1)(lambda: on_y(number, kind, index, part_z).start())

        kinds(number, run)

    def pass_y(number):
        def run(kind, index):
            on_y(number, kind, index, part_x).wait_recv()
            forward(number, kind, index).start()

        kinds(number, run)

    def bias_done(number):
        biases[number].wait_recv()

    def pass_done(number):
        kinds(number, lambda kind, index: forward(number, kind, index).wait_recv())

    biases = [
        remote(wb.at[x, c], wb.at[x, c], wb_s.at[i], wb_r.at[i], peer)
        for i, peer in enumerate((mate, x_peer, cross))
    ]
    for number in range(2):
        start_x(number)
        to_mate(number, "q", number).start()
    for copy in biases:
        copy.start()
    to_mate(2, "q", 2).start()
    to_mate(3, "o", 3).start()
    for index in range(tiles):
        to_mate(4 + index, "m", index).start()

    chunk = 128
    locals_[3].wait()
    small_refs = (gain1_ref, shift1_ref, outb_ref, gain2_ref, shift2_ref, downb_ref)

    def small(row):
        return small_refs[row][...].astype(F32).reshape(1, width)

    def norm(values):
        centred = values - jnp.mean(values, axis=-1, keepdims=True)
        inv = lax.rsqrt(jnp.mean(centred * centred, axis=-1, keepdims=True) + EPS)
        return centred * inv, inv

    def at_chunk(step):
        return pl.ds(pl.multiple_of(step * chunk, chunk), chunk)

    def first_norm(step, carry):
        where = at_chunk(step)
        hat, _ = norm(x_ref[where, :].astype(F32))
        a1_ref[where, :] = (small(0) * hat + small(1)).astype(BF16)
        return carry

    even = lane < 64

    def pick(values, others):
        return jnp.where(even, values, others), jnp.where(even, others, values)

    def attend_forward(step):
        xx, t = jnp.where(step < 3, x, nx), step % 3
        weights = wq[xx, t].reshape(3 * 128, width)
        biasq = wb[xx, 0, 1:2, :].astype(F32) + wb[xx, 1, 1:2, :].astype(F32)
        biasv = wb[xx, 0, 2:3, :].astype(F32) + wb[xx, 1, 2:3, :].astype(F32)
        pq = jnp.where(t == 0, biasq[:, :128], jnp.where(t == 1, biasq[:, 128:256], biasq[:, 256:384]))
        pv = jnp.where(t == 0, biasv[:, :128], jnp.where(t == 1, biasv[:, 128:256], biasv[:, 256:384]))
        for row in range(rows):
            where = pl.ds(row * seq, seq)
            value = dot(a1_ref[where, :], weights, 1, 1)
            proj_ref[xx, t, where, 0:128] = ((value[:, :128] + pq).astype(BF16) * 0.125).astype(BF16)
            proj_ref[xx, t, where, 128:256] = value[:, 128:256].astype(BF16)
            proj_ref[xx, t, where, 256:384] = (value[:, 256:] + pv).astype(BF16)
        group = xx * 3 + t
        for row in range(rows):
            where = pl.ds(row * seq, seq)
            qs = pick(proj_ref[xx, t, where, 0:128], aug_q[where, :])
            ks = pick(proj_ref[xx, t, where, 128:256], aug_k[where, :])
            vs = pick(proj_ref[xx, t, where, 256:384], jnp.ones((seq, 128), BF16))
            highest, result = [], []
            for q, k, v in zip(qs, ks, vs):
                scores = dot(q, k, 1, 1)
                top = jnp.max(scores, axis=-1, keepdims=True)
                highest.append(top)
                result.append(dot(jnp.exp(scores - top).astype(BF16), v, 1, 0))
            total = pltpu.roll(jnp.where(even, result[1], result[0]), 64, 1)
            mixed = jnp.where(even, result[0], result[1]) / total
            o_ref[where, pl.ds(pl.multiple_of(group * 128, 128), 128)] = mixed.astype(BF16)
            log_total = jnp.where(even, highest[0], highest[1]) + jnp.log(total)
            lse_ref[where, :] = jnp.where(lane % 64 == group, log_total, lse_ref[where, :])

    def second_norm(step, carry):
        where = pl.ds(pl.multiple_of(step * 256, 256), 256)
        value = x_ref[where, :].astype(F32) + dot(o_ref[where, :], wo[...].reshape(width, width), 1, 0) + small(2)
        hat, inv = norm(value)
        hat2_ref[where, :] = hat.astype(BF16)
        spot = lax.broadcasted_iota(jnp.int32, (256, 128), 1)
        lse_ref[where, :] = jnp.where(spot == INV_LANE, inv, lse_ref[where, :])
        a2_ref[where, :] = (small(3) * hat + small(4)).astype(BF16)
        x1_ref[where, :] = value + small(5)
        da2_ref[where, :] = jnp.zeros_like(value)
        return carry

    def pair_place(pair):
        if isinstance(pair, int):
            return (nx if FAR_PAIRS[pair] else x), PAIR_TILES[pair]
        far = sum(jnp.where(pair == p, 1, 0) for p, flag in enumerate(FAR_PAIRS) if flag)
        tile = sum(jnp.where(pair == p, index, 0) for p, index in enumerate(PAIR_TILES))
        return jnp.where(far == 1, nx, x), tile

    def multiple(value, of):
        return value if isinstance(value, int) else pl.multiple_of(value, of)

    def expert_tile(step):
        xx, index = pair_place(step // 2)
        cc = jnp.where(step % 2 == 0, nc, c)
        w_up = wm[xx, cc, index, pl.ds(0, UNIT), :]
        w_down = wm[xx, cc, index, pl.ds(UNIT, UNIT), :]
        lanes = pl.ds(pl.multiple_of(index * UNIT, UNIT), UNIT)
        bias = wb[xx, cc, 0:1, lanes].astype(F32)
        upb_sum = None
        part_rows = tokens // SPLIT
        for part in range(SPLIT):
            where = pl.ds(part * part_rows, part_rows)
            pre = dot(a2_ref[where, :], w_up, 1, 1) + bias
            back = dot(g_ref[where, :], w_down, 1, 1)
            cumul, density = gelu_parts(pre)
            hidden = (pre * cumul).astype(BF16)
            low = (back * (cumul + pre * density)).astype(BF16)
            hid_ref[where, :] = hidden
            low_ref[where, :] = low
            one = column_sum(low.astype(F32))
            upb_sum = one if upb_sum is None else upb_sum + one
            x1_ref[where, :] += dot(hidden, w_down, 1, 0)
            da2_ref[where, :] += dot(low, w_up, 1, 0)
        sums[pl.ds(UPB + xx * 2 + cc, 1), lanes] = upb_sum
        base = pl.multiple_of(index * 2 * UNIT, UNIT)
        grad[xx, cc, pl.ds(base, UNIT), :] = dot(low_ref[...], a2_ref[...], 0, 0).astype(BF16)
        grad[xx, cc, pl.ds(base + UNIT, UNIT), :] = dot(hid_ref[...], g_ref[...], 0, 0).astype(BF16)

    def norm_back(grad_in, hat, inv, gain):
        scaled = grad_in * gain
        return inv * (
            scaled
            - jnp.mean(scaled, axis=-1, keepdims=True)
            - hat * jnp.mean(scaled * hat, axis=-1, keepdims=True)
        )

    def add_sum(row, values):
        sums[row : row + 1, :] += column_sum(values)

    heads_rows = 6 * UNIT

    def between_norm():
        def one(step, carry):
            where = at_chunk(step)
            da2, hat = da2_ref[where, :], hat2_ref[where, :].astype(F32)
            top = g_ref[where, :].astype(F32)
            add_sum(GAIN2, da2 * hat)
            add_sum(SHIFT2, da2)
            add_sum(DOWNB, top)
            middle = top + norm_back(da2, hat, lse_ref[where, INV_LANE : INV_LANE + 1], small(3))
            da2_ref[where, :] = middle
            low = middle.astype(BF16)
            add_sum(OUTB, low.astype(F32))
            a2_ref[where, :] = low
            hat2_ref[where, :] = x1_ref[where, :].astype(BF16)
            return carry

        lax.fori_loop(0, tokens // chunk, one, 0)
        mixed_copy.start()

    def between_out():
        for xx in range(2):
            half = dot(o_ref[:, xx * 384 : (xx + 1) * 384], a2_ref[...], 0, 0).astype(BF16)
            for t in range(3):
                for cc in range(2):
                    start = (t * 2 + cc) * 64
                    grad[xx, cc, pl.ds(heads_rows + t * 64, 64), :] = half[start : start + 64]

    def between_back():
        def back(step, carry):
            where = pl.ds(pl.multiple_of(step * 256, 256), 256)
            a2_ref[where, :] = dot(a2_ref[where, :], wo[...].reshape(width, width), 1, 1).astype(BF16)
            return carry

        lax.fori_loop(0, tokens // 256, back, 0)

    def attend_backward(step):
        xx, t = jnp.where(step < 9, nx, x), (step // 3) % 3
        group = xx * 3 + t
        lanes = pl.ds(pl.multiple_of(group * 128, 128), 128)

        def one_row():
            where = pl.ds(pl.multiple_of((step % 3) * seq, seq), seq)
            query, key, value = (proj_ref[xx, t, where, i * 128 : (i + 1) * 128] for i in range(3))
            out, back = o_ref[where, lanes], a2_ref[where, lanes]
            none = jnp.zeros((seq, 128), BF16)
            product = out.astype(F32) * back.astype(F32)
            log_total = lse_ref[where, :]
            spot = lane % 64
            tops = [
                jnp.sum(jnp.where(lane == group + shift, log_total, 0.0), axis=-1, keepdims=True)
                for shift in (0, 64)
            ]
            deltas = [jnp.sum(item, axis=-1, keepdims=True) for item in pick(product, jnp.zeros_like(product))]
            q_aug, k_aug = pick(query, aug_q[where, :]), pick(key, aug_k[where, :])
            q_own, k_own, b_own = pick(query, none), pick(key, none), pick(back, none)
            v_aug = pick(value, jnp.where(spot < 3, 1.0, 0.0).astype(BF16))
            splits = []
            for delta in deltas:
                first = (-delta).astype(BF16).astype(F32)
                second = (-delta - first).astype(BF16).astype(F32)
                last = -delta - first - second
                splits.append(
                    jnp.where(spot == 0, first, jnp.where(spot == 1, second, jnp.where(spot == 2, last, 0.0)))
                )
            b_aug = (
                jnp.where(even, back, splits[0].astype(BF16)),
                jnp.where(even, splits[1].astype(BF16), back),
            )
            d_query = d_key = d_value = None
            for i in range(2):
                prob = jnp.exp(dot(q_aug[i], k_aug[i], 1, 1) - tops[i])
                low = prob.astype(BF16)
                inner = dot(b_aug[i], v_aug[i], 1, 1)
                d_score = (prob * inner).astype(BF16)
                parts = (dot(d_score, k_own[i], 1, 0), dot(d_score, q_own[i], 0, 0), dot(low, b_own[i], 0, 0))
                if i == 0:
                    d_query, d_key, d_value = parts
                else:
                    d_query, d_key, d_value = d_query + parts[0], d_key + parts[1], d_value + parts[2]
            low_query = (d_query * 0.125).astype(BF16)
            low_value = d_value.astype(BF16)
            proj_ref[xx, t, where, 0:128] = low_query
            proj_ref[xx, t, where, 128:256] = d_key.astype(BF16)
            proj_ref[xx, t, where, 256:384] = low_value
            sums[QUERYB : QUERYB + 1, lanes] += column_sum(low_query.astype(F32))
            sums[VALUEB : VALUEB + 1, lanes] += column_sum(low_value.astype(F32))

        def weights():
            whole = proj_ref[xx, t]
            weight_grad = dot(whole, a1_ref[...], 0, 0).astype(BF16)
            for part in range(3):
                for cc in range(2):
                    start = part * 128 + cc * 64
                    place = pl.multiple_of(heads_rows + 192 + t * 192 + part * 64, 64)
                    grad[xx, cc, pl.ds(place, 64), :] = weight_grad[start : start + 64]
            part = dot(whole, wq[xx, t].reshape(3 * 128, width), 1, 0)

            @pl.when(step == 2)
            def _():
                x1_ref[...] = part

            @pl.when(step > 2)
            def _():
                x1_ref[...] += part

        pl.when(step % 3 < 2)(one_row)
        pl.when(step % 3 == 2)(weights)

    def last_norm():
        def one(step, carry):
            where = at_chunk(step)
            hat, inv = norm(x_ref[where, :].astype(F32))
            da1 = x1_ref[where, :]
            add_sum(GAIN1, da1 * hat)
            add_sum(SHIFT1, da1)
            g_ref[where, :] = (da2_ref[where, :] + norm_back(da1, hat, inv, small(0))).astype(BF16)
            return carry

        lax.fori_loop(0, tokens // chunk, one, 0)
        input_copy.start()

    sums_out_copy = pltpu.make_async_copy(sums, sums_out, small_sem.at[9])
    mixed_copy = pltpu.make_async_copy(hat2_ref, mixed_out, local_sem.at[8])
    input_copy = pltpu.make_async_copy(g_ref, input_out, local_sem.at[9])

    def add_into(xx, start, count, other, other_start):
        def one(step, carry):
            mine = pl.ds(pl.multiple_of(start + step * 32, 32), 32)
            theirs = pl.ds(pl.multiple_of(other_start + step * 32, 32), 32)
            grad[xx, c, mine, :] = (grad[xx, c, mine, :].astype(F32) + other[theirs, :].astype(F32)).astype(BF16)
            return carry

        lax.fori_loop(0, count // 32, one, 0)

    def pair_copy(xx, granule, start, count):
        return remote(
            grad.at[xx, nc, pl.ds(start, count)],
            mate_buf.at[granule % 2, pl.ds(0, count)],
            pair_s.at[granule], pair_r.at[granule], mate,
        )

    def x_copy(unit):
        where = pl.ds(multiple(unit * UNIT, UNIT), UNIT)
        return remote(grad.at[nx, c, where], x_buf.at[where], ex_s.at[unit], ex_r.at[unit], x_peer)

    def granule_add(xx, granule, start, count):
        pair_copy(xx, granule, start, count).wait_recv()
        add_into(xx, start, count, mate_buf.at[granule % 2], 0)

    def tile_start(index):
        return multiple(index * 2 * UNIT, 2 * UNIT)

    def pair_send(pair):
        xx, index = pair_place(pair)
        pair_copy(xx, pair, tile_start(index), 2 * UNIT).start()

    def pair_add(pair):
        xx, index = pair_place(pair)
        granule_add(xx, pair, tile_start(index), 2 * UNIT)

        if FAR_PAIRS[pair]:
            x_copy(2 * index).start()
            x_copy(2 * index + 1).start()

    def heads_start(number):
        return multiple(heads_rows + number * UNIT, UNIT)

    def far_send(number):
        pair_copy(nx, 6 + number, heads_start(number), UNIT).start()

    def far_add(number):
        granule_add(nx, 6 + number, heads_start(number), UNIT)
        x_copy(6 + number).start()

    def near_send(number):
        pair_copy(x, 9 + number, heads_start(number), UNIT).start()

    def near_add(number):
        granule_add(x, 9 + number, heads_start(number), UNIT)

    half = UNIT // 2
    share = half // 2

    def y_copy(unit):
        return remote(
            grad.at[x, c, pl.ds(pl.multiple_of(unit * UNIT + ny * half, half), half)],
            y_buf.at[pl.ds(multiple(unit * half, half), half)],
            ey_s.at[unit], ey_r.at[unit], y_peer,
        )

    def share_rows(unit, part):
        return pl.ds(pl.multiple_of(unit * UNIT + y * half + part * share, share), share)

    def slot_rows(unit):
        return pl.ds(multiple(unit * share, share), share)

    def pair_z_copy(unit):
        return remote(
            grad.at[x, c, share_rows(unit, 1 - zb)], z_buf.at[0, slot_rows(unit)], ez_s.at[unit], ez_r.at[unit], z_pair
        )

    def far_z_copy(unit):
        return remote(
            grad.at[x, c, share_rows(unit, zb)], z_buf.at[1, slot_rows(unit)], ew_s.at[unit], ew_r.at[unit], z_far
        )

    def back_z_copy(unit):
        where = share_rows(unit, zb)
        return remote(x_buf.at[where], x_buf.at[where], fz_s.at[unit], fz_r.at[unit], z_pair)

    def back_y_copy(unit):
        where = pl.ds(pl.multiple_of(unit * UNIT + y * half, half), half)
        return remote(x_buf.at[where], x_buf.at[where], fy_s.at[unit], fy_r.at[unit], y_peer)

    def add_x(unit):
        x_copy(unit).wait_recv()
        start = multiple(unit * UNIT, UNIT)
        add_into(x, start, UNIT, x_buf, start)
        y_copy(unit).start()

    def add_y(unit):
        y_copy(unit).wait_recv()
        add_into(x, pl.multiple_of(unit * UNIT + y * half, half), half, y_buf, multiple(unit * half, half))
        pair_z_copy(unit).start()

    def add_z(unit):
        pair_z_copy(unit).wait_recv()
        start = pl.multiple_of(unit * UNIT + y * half + zb * share, share)
        add_into(x, start, share, z_buf.at[0], multiple(unit * share, share))
        far_z_copy(unit).start()

    def add_far(unit):
        far_z_copy(unit).wait_recv()
        where = share_rows(unit, zb)
        total = grad[x, c, where, :].astype(F32) + z_buf[1, slot_rows(unit), :].astype(F32)
        x_buf[where, :] = total.astype(BF16)
        back_z_copy(unit).start()

    def give_y(unit):
        back_z_copy(unit).wait_recv()
        back_y_copy(unit).start()

    def out_copy(unit):
        where = pl.ds(multiple(unit * UNIT, UNIT), UNIT)
        return pltpu.make_async_copy(x_buf.at[where], grads_out.at[where], local_sem.at[10 + unit])

    def finish(unit):
        back_y_copy(unit).wait_recv()
        out_copy(unit).start()

    def sums_copy(slot, source, peer):
        return remote(sums_recv.at[6 + source], sums_recv.at[slot], sums_s.at[slot], sums_r.at[slot], peer)

    small_peers = [(i, i, peer) for i, peer in enumerate((mate, x_peer, y_peer, z_pair, z_far))]

    def sums_step(number):
        if number > 0:
            sums_copy(*small_peers[number - 1]).wait_recv()
            sums_recv[6 + number] = sums_recv[5 + number] + sums_recv[number - 1]
        else:
            sums_recv[6] = sums[...]
        if number < 5:
            sums_copy(*small_peers[number]).start()
        else:
            total = sums_recv[11]
            sums[...] = total
            own_up = sums[pl.ds(UPB + mp, 1), :]
            pairs = jnp.where(x == 0, total[:, :384], total[:, 384:])
            spread = jnp.where(placed, 1.0, 0.0)
            own_qv = lax.dot_general(
                pairs, spread, (((1,), (1,)), ((), ())), precision=lax.Precision.HIGHEST, preferred_element_type=F32
            )
            own_qv = jnp.concatenate([own_qv, jnp.zeros((16, width - own_qv.shape[1]), F32)], axis=1)
            total = jnp.where(tile_row == OWN_UP, own_up, total)
            total = jnp.where(tile_row == OWN_QV, own_qv[QUERYB : QUERYB + 1], total)
            sums[...] = jnp.where(tile_row == OWN_QV + 1, own_qv[VALUEB : VALUEB + 1], total)
            sums_out_copy.start()

    events = {
        "pair_add": pair_add, "far_add": far_add, "near_add": near_add,
        "pair_send": pair_send, "far_send": far_send, "near_send": near_send,
        "bias_done": bias_done, "pass_x": pass_x, "pass_z": pass_z, "pass_y": pass_y, "pass_done": pass_done, "mate_done": mate_done,
        "add_x": add_x, "add_y": add_y, "add_z": add_z, "add_far": add_far, "give_y": give_y, "finish": finish,
        "sums": sums_step,
    }

    def run_due(due):
        for name, number in due:
            events[name](number)

    def due_now(step, plan):
        for at, due in enumerate(plan):
            if due:
                pl.when(step == at)(lambda due=due: run_due(due))

    lax.fori_loop(0, tokens // chunk, first_norm, 0)

    def forward_step(step, carry):
        due_now(step, PLAN_FORWARD)
        attend_forward(step)

        return carry

    lax.fori_loop(0, 6, forward_step, 0)
    run_due(PLAN_SECOND)
    lax.fori_loop(0, tokens // 256, second_norm, 0)
    sums[...] = jnp.zeros_like(sums)
    locals_[7].wait()

    def main_step(step, carry):
        due_now(step, PLAN_MAIN)
        pl.when(step < BETWEEN)(lambda: expert_tile(step))
        pl.when(step == BETWEEN)(between_norm)
        pl.when(step == BETWEEN + 1)(between_out)
        pl.when(step == BETWEEN + 2)(between_back)
        pl.when(jnp.logical_and(step >= FIRST_HEADS, step < LAST_NORM))(
            lambda: attend_backward(step - FIRST_HEADS)
        )
        pl.when(step == LAST_NORM)(last_norm)
        return carry

    lax.fori_loop(0, LAST_NORM + 1, main_step, 0)
    run_due(PLAN_DRAIN)

    mixed_copy.wait()
    input_copy.wait()
    sums_out_copy.wait()
    for copy in biases:
        copy.wait_send()

    def piece_sends(number):
        def run(kind, index):
            to_mate(number, kind, index).wait_send()
            to_x(number, kind, index).wait_send()
            on_z(number, kind, index, part_x).wait_send()
            on_y(number, kind, index, part_x).wait_send()
            forward(number, kind, index).wait_send()

        kinds(number, run)

    def last_waits(unit, carry):
        x_copy(unit).wait_send()
        y_copy(unit).wait_send()
        pair_z_copy(unit).wait_send()
        far_z_copy(unit).wait_send()
        back_z_copy(unit).wait_send()
        back_y_copy(unit).wait_send()
        out_copy(unit).wait()
        pl.when(unit < 7)(lambda: piece_sends(unit))
        @pl.when(unit < 6)
        def _():
            xx, index = pair_place(unit)
            pair_copy(xx, unit, tile_start(index), 2 * UNIT).wait_send()

        @pl.when(unit < 3)
        def _():
            pair_copy(nx, 6 + unit, heads_start(unit), UNIT).wait_send()
            pair_copy(x, 9 + unit, heads_start(unit), UNIT).wait_send()

        return carry

    lax.fori_loop(0, 9, last_waits, 0)
    for slot, source, peer in small_peers:
        sums_copy(slot, source, peer).wait_send()


def tail_kernel(
    mixed_in, input_in, grads_in, sums_in,
    mixed_out, input_out, qkv_out, wout_out, up_out, down_out,
    qv_out, gain1_out, shift1_out, outb_out, gain2_out, shift2_out, downb_out, upb_out,
    mixed, inputs, grads, qkv, wout, up, down, sums_ref, qv_ref, in_sem, out_sem, small_sem, *vectors,
):
    tiles = down.shape[0]
    heads = qkv.shape[1]
    copies = [
        pltpu.make_async_copy(mixed_in, mixed, in_sem.at[0]),
        pltpu.make_async_copy(input_in, inputs, in_sem.at[1]),
    ]
    loads = []
    for index in range(tiles + 1):
        rows = pl.ds(index * 2 * UNIT, 2 * UNIT if index < tiles else 3 * UNIT)
        loads.append(pltpu.make_async_copy(grads_in.at[rows], grads.at[rows], in_sem.at[2 + index]))
    sums_copy = pltpu.make_async_copy(sums_in, sums_ref, small_sem.at[8])
    for copy in copies + loads + [sums_copy]:
        copy.start()
    stores = [
        pltpu.make_async_copy(mixed, mixed_out, out_sem.at[2 * tiles + 2]),
        pltpu.make_async_copy(inputs, input_out, out_sem.at[2 * tiles + 3]),
    ]
    for copy, store in zip(copies, stores):
        copy.wait()
        store.start()
    for index in range(tiles):
        loads[index].wait()
        start = index * 2 * UNIT
        down[index] = grads[start + UNIT : start + 2 * UNIT, :].astype(F32)
        stores.append(pltpu.make_async_copy(down.at[index], down_out.at[index], out_sem.at[2 * index]))
        stores[-1].start()
        lanes = pl.ds(index * UNIT, UNIT)
        up[:, lanes] = grads[start : start + UNIT, :].astype(F32).T
        stores.append(pltpu.make_async_copy(up.at[:, lanes], up_out.at[:, lanes], out_sem.at[2 * index + 1]))
        stores[-1].start()
    loads[tiles].wait()
    start = 2 * tiles * UNIT
    wout[...] = grads[start : start + heads * HEAD, :].astype(F32)
    stores.append(pltpu.make_async_copy(wout, wout_out, out_sem.at[2 * tiles]))
    stores[-1].start()
    start += heads * HEAD
    for head in range(heads):
        for part in range(3):
            row = start + (head * 3 + part) * HEAD
            qkv[part, head] = grads[row : row + HEAD, :].astype(F32)
    stores.append(pltpu.make_async_copy(qkv, qkv_out, out_sem.at[2 * tiles + 1]))
    stores[-1].start()
    sums_copy.wait()
    for index, (row, out) in enumerate((
        (GAIN1, gain1_out), (SHIFT1, shift1_out), (OUTB, outb_out), (GAIN2, gain2_out), (SHIFT2, shift2_out),
        (DOWNB, downb_out), (OWN_UP, upb_out),
    )):
        vectors[index][...] = sums_ref[row, :]
        stores.append(pltpu.make_async_copy(vectors[index], out, small_sem.at[index]))
        stores[-1].start()
    qv_ref[...] = sums_ref[OWN_QV : OWN_QV + 2, : qv_ref.shape[1]]
    stores.append(pltpu.make_async_copy(qv_ref, qv_out, small_sem.at[7]))
    stores[-1].start()
    for copy in stores:
        copy.wait()


def on_device(
    tokens, segment_ids, cotangent, norm1_gain, norm1_shift, w_qkv, qv_bias, w_out, out_bias,
    norm2_gain, norm2_shift, w_up, up_bias, w_down, down_bias,
):
    rows, seq, width = tokens.shape
    count = rows * seq
    shard = w_up.shape[1]
    heads = w_out.shape[0] // HEAD
    tiles = shard // UNIT
    units = 2 * tiles + 3
    qkv_rows = jnp.transpose(w_qkv, (1, 2, 0)).reshape(3, heads, HEAD, width)

    any_space = pl.BlockSpec(memory_space=pl.ANY)
    dma = pltpu.SemaphoreType.DMA
    vm = pltpu.VMEM
    mixed, input_grad, grads, sums = pl.pallas_call(
        functools.partial(kernel, rows=rows, seq=seq),
        out_shape=(
            jax.ShapeDtypeStruct((count, width), BF16),
            jax.ShapeDtypeStruct((count, width), BF16),
            jax.ShapeDtypeStruct((units * UNIT, width), BF16),
            jax.ShapeDtypeStruct((16, width), F32),
        ),
        in_specs=[any_space] * 15,
        out_specs=(any_space,) * 4,
        scratch_shapes=[
            vm((2, heads, 3, 2, HEAD, width), BF16),
            vm((2, heads, 2, HEAD, width), BF16),
            vm((2, 2, tiles, 2 * UNIT, width), BF16),
            vm((2, 2, 16, width), BF16),
            vm((2, 2, units * UNIT, width), BF16),
            vm((2, 2 * UNIT, width), BF16),
            vm((units * UNIT, width), BF16),
            vm((units * UNIT // 2, width), BF16),
            vm((2, units * UNIT // 4, width), BF16),
            vm((count, width), BF16),
            vm((count, width), BF16),
            vm((count, width), BF16),
            vm((2, heads, count, 3 * 128), BF16),
            vm((count, width), BF16),
            vm((count, width), F32),
            vm((count, width), BF16),
            vm((count, width), BF16),
            vm((count, width), F32),
            vm((count, UNIT), BF16),
            vm((count, UNIT), BF16),
            vm((count, 128), F32),
            vm((count, 128), BF16),
            vm((count, 128), BF16),
            vm((16, width), F32),
            vm((12, 16, width), F32),
            vm((rows, seq), jnp.int32),
            *[vm((width,), BF16)] * 7,
            vm((2, heads * HEAD), BF16),
            dma((10,)),
            dma((10 + units,)),
            dma((7,)), dma((7,)), dma((7,)), dma((7,)), dma((7,)), dma((7,)),
            dma((7,)), dma((7,)), dma((7,)), dma((7,)), dma((3,)), dma((3,)),
            dma((12,)), dma((12,)),
            dma((units,)), dma((units,)), dma((units,)), dma((units,)),
            dma((units,)), dma((units,)), dma((units,)), dma((units,)), dma((units,)), dma((units,)),
            dma((units,)), dma((units,)), dma((6,)), dma((6,)),
        ],
        compiler_params=pltpu.CompilerParams(
            collective_id=0, has_side_effects=True, vmem_limit_bytes=64 * 2**20 - 2**16
        ),
    )(
        tokens.reshape(count, width), cotangent.reshape(count, width), segment_ids,
        norm1_gain, norm1_shift, out_bias, norm2_gain, norm2_shift, down_bias, up_bias, qv_bias,
        qkv_rows, w_out.reshape(heads, HEAD, width), w_up, w_down.reshape(tiles, UNIT, width),
    )

    groups = lax.axis_size("dp") // 8
    if groups > 1:
        grads, sums = lax.psum((grads.astype(F32) * 0.125, sums * 0.125), "dp")
    whole = [jax.ShapeDtypeStruct((width,), F32)] * 7
    results = pl.pallas_call(
        tail_kernel,
        out_shape=(
            mixed, input_grad,
            jax.ShapeDtypeStruct((3, heads, HEAD, width), F32), jax.ShapeDtypeStruct((heads * HEAD, width), F32),
            jax.ShapeDtypeStruct((width, shard), F32), jax.ShapeDtypeStruct((tiles, UNIT, width), F32),
            jax.ShapeDtypeStruct((2, heads * HEAD), F32), *whole,
        ),
        in_specs=[any_space] * 4,
        out_specs=(any_space,) * 14,
        scratch_shapes=[
            vm((count, width), BF16), vm((count, width), BF16), vm(grads.shape, grads.dtype),
            vm((3, heads, HEAD, width), F32), vm((heads * HEAD, width), F32),
            vm((width, shard), F32), vm((tiles, UNIT, width), F32),
            vm((16, width), F32), vm((2, heads * HEAD), F32),
            dma((2 + tiles + 1,)), dma((2 * tiles + 4,)), dma((9,)),
            *[vm((width,), F32)] * 7,
        ],
        compiler_params=pltpu.CompilerParams(vmem_limit_bytes=63 * 2**20),
    )(mixed, input_grad, grads, sums)
    mixed, input_grad, grad_qkv, grad_out, grad_up, grad_down, grad_qv, *vectors = results
    gain1, shift1, outb, gain2, shift2, downb, upb = vectors
    return (
        mixed.reshape(rows, seq, width),
        input_grad.reshape(rows, seq, width),
        gain1,
        shift1,
        jnp.transpose(grad_qkv.reshape(3, heads * HEAD, width), (2, 0, 1)),
        grad_qv,
        grad_out,
        outb,
        gain2,
        shift2,
        grad_up,
        upb,
        grad_down.reshape(shard, width),
        downb,
    )


def solution(mesh):
    tall = P(("dp", "mp"), None, None)
    return jax.shard_map(
        on_device,
        mesh=mesh,
        in_specs=(
            tall, P(("dp", "mp"), None), tall, P(), P(), P(None, None, "mp"), P(None, "mp"), P("mp", None),
            P(), P(), P(), P(None, "mp"), P("mp"), P("mp", None), P(),
        ),
        out_specs=(
            tall, tall, P(), P(), P(None, None, "mp"), P(None, "mp"), P("mp", None), P(), P(), P(),
            P(None, "mp"), P("mp"), P("mp", None), P(),
        ),
        check_vma=False,
    )
```

```python
import functools

import jax
import jax.numpy as jnp
from jax import lax
from jax.experimental import pallas as pl
from jax.experimental.pallas import tpu as pltpu
from jax.sharding import PartitionSpec as P

HEAD = 64
EPS = 1e-06
MASKED = -1e30
UNIT = 256
SPLIT = 4
INV_LANE = 32
OWN_UP, OWN_QV = 12, 13
F32, BF16 = jnp.float32, jnp.bfloat16

GAIN1, SHIFT1, OUTB, GAIN2, SHIFT2, DOWNB, QUERYB, VALUEB, UPB = range(9)

UNITS = (
    (0, 256),
    (256, 256),
    (512, 256),
    (768, 256),
    (1024, 256),
    (1280, 256),
    (1536, 192),
    (1728, 192),
    (1920, 192),
    (2112, 128),
    (2240, 64),
)
GRANULES = (
    (0, 0, 512, (0, 1)),
    (1, 0, 512, (0, 1)),
    (1, 512, 512, (2, 3)),
    (0, 512, 512, (2, 3)),
    (0, 1024, 512, (4, 5)),
    (1, 1024, 512, (4, 5)),
    (1, 1536, 192, (6,)),
    (0, 1536, 192, (6,)),
    (1, 1728, 192, (7,)),
    (1, 1920, 192, (8,)),
    (1, 2112, 192, (9, 10)),
    (0, 1728, 192, (7,)),
    (0, 1920, 192, (8,)),
    (0, 2112, 192, (9, 10)),
)
EARLY = (0, 2)
PIECES, AHEAD = 10, 2
FAR_PAIRS = (0, 1, 1, 0, 0, 1)
PAIR_TILES = (0, 0, 1, 1, 2, 2)
BETWEEN, FIRST_HEADS, LAST_NORM = 12, 15, 33
(
    BIAS_DONE, MATE_DONE, PASS_X, PASS_Y, PASS_DONE, CORE_ADD, CORE_SEND, EARLY_X, EARLY_Y, EARLY_Z,
    ADD_X, ADD_Y, ADD_Z, ADD_FAR, GIVE_Y, FINISH, SUMS, SETTLE,
) = range(18)
PLAN_FORWARD = (
    ((MATE_DONE, 0), (BIAS_DONE, 0),),
    ((PASS_X, 0),),
    ((PASS_X, 1),),
    ((MATE_DONE, 1),),
    (),
    ((PASS_X, 2),),
    ((MATE_DONE, 2),),
    ((PASS_X, 3), (PASS_Y, 0),),
    (),
    ((PASS_DONE, 0), (BIAS_DONE, 1), (BIAS_DONE, 2),),
    ((PASS_X, 4), (PASS_Y, 1),),
    ((PASS_X, 5),),
    ((PASS_DONE, 1),),
    ((PASS_Y, 2),),
    ((PASS_X, 6),),
    ((PASS_DONE, 2),),
    ((PASS_X, 7), (PASS_Y, 3),),
    (),
)
PLAN_SECOND = (
    ((PASS_X, 8), (MATE_DONE, 3), (PASS_DONE, 3),),
    (),
    ((PASS_X, 9), (PASS_Y, 4),),
    (),
)
PLAN_MAIN = (
    ((MATE_DONE, 4), (MATE_DONE, 5),),
    ((PASS_Y, 5), (CORE_SEND, 0),),
    ((PASS_Y, 6), (PASS_DONE, 4), (PASS_DONE, 5),),
    ((CORE_ADD, 0), (CORE_SEND, 1),),
    ((PASS_Y, 7), (CORE_ADD, 1), (PASS_DONE, 6), (PASS_DONE, 7),),
    ((PASS_Y, 8), (CORE_SEND, 2),),
    ((PASS_Y, 9), (MATE_DONE, 6), (MATE_DONE, 7),),
    ((CORE_ADD, 2), (CORE_SEND, 3), (EARLY_Y, 0), (ADD_X, 1),),
    ((CORE_ADD, 3), (EARLY_X, 0), (MATE_DONE, 8), (MATE_DONE, 9),),
    ((CORE_SEND, 4), (EARLY_X, 2), (ADD_Y, 1),),
    ((CORE_ADD, 4), (EARLY_Y, 2), (ADD_X, 3), (PASS_DONE, 8), (PASS_DONE, 9),),
    ((CORE_SEND, 5), (ADD_Z, 1),),
    ((CORE_ADD, 5), (EARLY_Z, 0), (ADD_Y, 3),),
    ((EARLY_Z, 2), (ADD_FAR, 1),),
    ((CORE_SEND, 6), (ADD_Z, 0), (ADD_Z, 3),),
    ((CORE_ADD, 6), (CORE_SEND, 7), (ADD_Z, 2), (GIVE_Y, 1),),
    ((CORE_ADD, 7), (ADD_X, 4),),
    ((ADD_FAR, 0),),
    ((CORE_SEND, 8),),
    ((CORE_ADD, 8), (FINISH, 1),),
    ((ADD_FAR, 3),),
    ((CORE_SEND, 9), (ADD_X, 5), (ADD_Y, 4),),
    ((CORE_ADD, 9), (ADD_FAR, 2), (GIVE_Y, 0), (GIVE_Y, 3),),
    ((ADD_Z, 4),),
    ((CORE_SEND, 10), (ADD_X, 6), (ADD_Y, 5),),
    ((CORE_ADD, 10), (GIVE_Y, 2),),
    ((FINISH, 0),),
    ((CORE_SEND, 11), (ADD_FAR, 4),),
    ((CORE_ADD, 11), (ADD_X, 7), (ADD_Z, 5), (FINISH, 3),),
    ((ADD_Y, 6),),
    ((CORE_SEND, 12), (FINISH, 2),),
    ((CORE_ADD, 12), (ADD_X, 8), (ADD_Y, 7), (GIVE_Y, 4),),
    ((ADD_FAR, 5),),
    ((CORE_SEND, 13), (ADD_Z, 6),),
    ((CORE_ADD, 13), (ADD_X, 9), (ADD_X, 10), (ADD_Y, 8), (ADD_Z, 7),),
    ((GIVE_Y, 5),),
    ((ADD_FAR, 6), (FINISH, 4),),
)
PLAN_DRAIN = (
    (ADD_Z, 8),
    (SUMS, 0),
    (ADD_Y, 9),
    (SETTLE, 0),
    (SETTLE, 1),
    (SETTLE, 2),
    (SETTLE, 3),
    (ADD_FAR, 7),
    (ADD_Y, 10),
    (SETTLE, 4),
    (SETTLE, 5),
    (SETTLE, 6),
    (SETTLE, 7),
    (GIVE_Y, 6),
    (SUMS, 1),
    (SETTLE, 8),
    (SETTLE, 9),
    (SETTLE, 10),
    (SETTLE, 12),
    (SETTLE, 13),
    (SETTLE, 14),
    (SETTLE, 15),
    (SETTLE, 16),
    (SETTLE, 17),
    (SETTLE, 18),
    (ADD_Z, 9),
    (SUMS, 2),
    (ADD_FAR, 8),
    (FINISH, 5),
    (GIVE_Y, 7),
    (SETTLE, 19),
    (ADD_Z, 10),
    (SUMS, 3),
    (FINISH, 6),
    (ADD_FAR, 9),
    (GIVE_Y, 8),
    (SETTLE, 20),
    (SUMS, 4),
    (ADD_FAR, 10),
    (FINISH, 7),
    (GIVE_Y, 9),
    (SUMS, 5),
    (GIVE_Y, 10),
    (SETTLE, 21),
    (SETTLE, 11),
    (SETTLE, 22),
    (FINISH, 8),
    (FINISH, 9),
    (FINISH, 10),
)

def dot(left, right, left_dim, right_dim):
    return lax.dot_general(
        left, right, (((left_dim,), (right_dim,)), ((), ())), preferred_element_type=F32
    )


def column_sum(values):
    return jnp.sum(values, axis=0, keepdims=True)


def gelu_parts(pre):
    cumul = 0.5 + 0.5 * lax.erf(pre * 0.7071067811865476)
    return cumul, jnp.exp(-0.5 * pre * pre) * 0.3989422804014327


def kernel(
    x_in, g_in, seg_in, gain1_in, shift1_in, outb_in, gain2_in, shift2_in, downb_in, upb_in, qvb_in,
    qkv_in, out_in, up_in, down_in,
    mixed_out, input_out, grads_out, sums_out,
    wq, wo, wm, wb, grad, mate_buf, early_buf, x_buf, y_buf, z_buf,
    x_ref, g_ref, a1_ref, proj_ref, o_ref, x1_ref, hat2_ref, a2_ref, da2_ref,
    hid_ref, low_ref, lse_ref, aug_q, aug_k, sums, sums_recv,
    seg_ref, gain1_ref, shift1_ref, outb_ref, gain2_ref, shift2_ref, downb_ref, upb_ref, qvb_ref, small_sem,
    local_sem, wm_s, wm_r, wx_s, wx_r, wy_s, wy_r, wz_s, wz_r, wd_s, wd_r, wf_s, wf_r, wb_s, wb_r,
    core_s, core_r, early_s, early_r, ex_s, ex_r, ey_s, ey_r, ez_s, ez_r, ew_s, ew_r, fz_s, fz_r, fy_s, fy_r, sums_s, sums_r,
    *, rows, seq,
):
    tokens, width = x_ref.shape
    dp, mp = lax.axis_index("dp"), lax.axis_index("mp")
    c, x = mp % 2, mp // 2
    y, z = dp % 2, (dp // 2) % 4
    block = dp - dp % 8
    zb = z % 2
    nx, nc, ny = 1 - x, 1 - c, 1 - y

    def device(zz, yy, xx, cc):
        return (block + zz * 2 + yy, xx * 2 + cc)

    mate = device(z, y, x, nc)
    x_peer = device(z, y, nx, c)
    y_peer = device(z, ny, x, c)
    z_far = device((z + 2) % 4, y, x, c)
    z_pair = device(z + 1 - 2 * zb, y, x, c)
    cross = device(z, y, nx, nc)
    corner = device(z + 1 - 2 * zb, ny, x, c)

    def remote(src, dst, send, recv, where):
        return pltpu.make_async_remote_copy(
            src_ref=src, dst_ref=dst, send_sem=send, recv_sem=recv,
            device_id=where, device_id_type=pl.DeviceIdType.MESH,
        )

    barrier = pltpu.get_barrier_semaphore()
    everyone = [mate, x_peer, cross, y_peer, z_pair, z_far, corner]
    for peer in everyone:
        pl.semaphore_signal(barrier, inc=1, device_id=peer, device_id_type=pl.DeviceIdType.MESH)

    up_stage = grad.at[0, 0, pl.ds(0, width)]
    locals_ = [
        pltpu.make_async_copy(qkv_in.at[:, 0], wq.at[x, 0, :, c], local_sem.at[0]),
        pltpu.make_async_copy(qkv_in.at[:, 1], wq.at[x, 1, :, c], local_sem.at[1]),
        pltpu.make_async_copy(qkv_in.at[:, 2], wq.at[x, 2, :, c], local_sem.at[2]),
        pltpu.make_async_copy(x_in, x_ref, local_sem.at[3]),
        pltpu.make_async_copy(out_in, wo.at[x, :, c], local_sem.at[4]),
        pltpu.make_async_copy(up_in, up_stage, local_sem.at[5]),
        pltpu.make_async_copy(down_in, wm.at[x, c, :, pl.ds(UNIT, UNIT)], local_sem.at[6]),
        pltpu.make_async_copy(g_in, g_ref, local_sem.at[7]),
    ]
    small_copies = [
        pltpu.make_async_copy(src, dst, small_sem.at[i])
        for i, (src, dst) in enumerate((
            (seg_in, seg_ref), (upb_in, upb_ref), (qvb_in, qvb_ref), (gain1_in, gain1_ref), (shift1_in, shift1_ref),
            (outb_in, outb_ref), (gain2_in, gain2_ref), (shift2_in, shift2_ref), (downb_in, downb_ref),
        ))
    ]
    for copy in small_copies + locals_:
        copy.start()
    for copy in small_copies:
        copy.wait()

    from_lane = lax.broadcasted_iota(jnp.int32, (qvb_ref.shape[1], 384), 0)
    to_lane = lax.broadcasted_iota(jnp.int32, (qvb_ref.shape[1], 384), 1)
    placed = jnp.logical_and(
        from_lane == (to_lane // 128) * 64 + to_lane % 64, (to_lane // 64) % 2 == c
    )
    place = jnp.where(placed, 1.0, 0.0).astype(BF16)
    qv_rows = dot(qvb_ref[...], place, 1, 0)
    qv_rows = jnp.concatenate([qv_rows, jnp.zeros((2, width - 384), F32)], axis=1)
    tile_row = lax.broadcasted_iota(jnp.int32, (16, width), 0)
    wb[x, c] = jnp.where(
        tile_row == 0,
        upb_ref[...].astype(F32).reshape(1, width),
        jnp.where(tile_row == 1, qv_rows[0:1], jnp.where(tile_row == 2, qv_rows[1:2], 0.0)),
    ).astype(BF16)
    lane = lax.broadcasted_iota(jnp.int32, (seq, 128), 1)
    for row in range(rows):
        ids = jnp.broadcast_to(seg_ref[row : row + 1, :].astype(F32), (128, seq)).T
        spot = lane % 64
        same = spot == ids.astype(jnp.int32)
        inside = spot < 32
        where = pl.ds(row * seq, seq)
        aug_q[where, :] = jnp.where(same, 1.0, 0.0).astype(BF16)
        aug_k[where, :] = jnp.where(jnp.logical_and(inside, jnp.logical_not(same)), MASKED, 0.0).astype(BF16)
    lse_ref[...] = jnp.zeros_like(lse_ref)
    for number in (0, 1, 2, 4):
        locals_[number].wait()
    pl.semaphore_wait(barrier, len(everyone))

    def piece(kind, index, xx, cc, part=None):
        if kind == "q":
            return wq.at[xx, index, :, cc, some(HEAD, part)]
        if kind == "o":
            return wo.at[xx, :, cc, some(HEAD, part)]
        return wm.at[xx, cc, index // 2, some(UNIT, part, (index % 2) * UNIT)]

    def some(count, part, start=0):
        if part is None:
            return pl.ds(start, count)
        return pl.ds(pl.multiple_of(start + part * (count // 4), 16), count // 4)

    quarter = y * 2 + zb

    def kinds(number, run):
        run("q" if number < 3 else "o" if number == 3 else "m", number - 4 if number > 3 else number)

    def to_mate(number, kind, index):
        own = piece(kind, index, x, c)
        return remote(own, own, wm_s.at[number], wm_r.at[number], mate)

    def to_x(number, kind, index):
        own = piece(kind, index, x, c, quarter)
        return remote(own, own, wx_s.at[number], wx_r.at[number], x_peer)

    def to_square(number, kind, index):
        held = piece(kind, index, nx, c, quarter)
        return [
            remote(held, held, send.at[number], recv.at[number], peer)
            for send, recv, peer in ((wy_s, wy_r, y_peer), (wz_s, wz_r, z_pair), (wd_s, wd_r, corner))
        ]

    def forward(number, kind, index):
        held = piece(kind, index, nx, c)
        return remote(held, held, wf_s.at[number], wf_r.at[number], mate)

    def mate_done(number):
        kinds(number, lambda kind, index: to_mate(number, kind, index).wait_recv())

    def start_x(number):
        kinds(number, lambda kind, index: to_x(number, kind, index).start())

    def pass_x(number):
        def run(kind, index):
            to_x(number, kind, index).wait_recv()
            for copy in to_square(number, kind, index):
                copy.start()

        kinds(number, run)
        if number + AHEAD < PIECES:
            start_x(number + AHEAD)

    def pass_y(number):
        def run(kind, index):
            for copy in to_square(number, kind, index):
                copy.wait_recv()
            forward(number, kind, index).start()

        kinds(number, run)

    def bias_done(number):
        biases[number].wait_recv()

    def pass_done(number):
        kinds(number, lambda kind, index: forward(number, kind, index).wait_recv())

    biases = [
        remote(wb.at[x, c], wb.at[x, c], wb_s.at[i], wb_r.at[i], peer)
        for i, peer in enumerate((mate, x_peer, cross))
    ]
    for copy in biases:
        copy.start()
    for number in range(AHEAD):
        start_x(number)
        if number < 3:
            kinds(number, lambda kind, index: to_mate(number, kind, index).start())
    for number in range(min(AHEAD, 3), 4):
        kinds(number, lambda kind, index: to_mate(number, kind, index).start())
    locals_[5].wait()
    locals_[6].wait()
    tiles = up_stage.shape[1] // UNIT
    for index in range(tiles):
        wm[x, c, index, pl.ds(0, UNIT), :] = up_stage[:, index * UNIT : (index + 1) * UNIT].T
    for number in range(4, PIECES):
        kinds(number, lambda kind, index: to_mate(number, kind, index).start())

    chunk = 128
    locals_[3].wait()
    small_refs = (gain1_ref, shift1_ref, outb_ref, gain2_ref, shift2_ref, downb_ref)

    def small(row):
        return small_refs[row][...].astype(F32).reshape(1, width)

    def norm(values):
        centred = values - jnp.mean(values, axis=-1, keepdims=True)
        inv = lax.rsqrt(jnp.mean(centred * centred, axis=-1, keepdims=True) + EPS)
        return centred * inv, inv

    def at_chunk(step):
        return pl.ds(pl.multiple_of(step * chunk, chunk), chunk)

    def first_norm(step, carry):
        where = at_chunk(step)
        hat, _ = norm(x_ref[where, :].astype(F32))
        a1_ref[where, :] = (small(0) * hat + small(1)).astype(BF16)
        return carry

    even = lane < 64

    def pick(values, others):
        return jnp.where(even, values, others), jnp.where(even, others, values)

    def part_lanes(group, part, count=1):
        return pl.ds(pl.multiple_of(group * 384 + part * 128, 128), count * 128)

    def project(step):
        xx, t = jnp.where(step < 9, x, nx), (step // 3) % 3
        group = xx * 3 + t
        weights = wq[xx, t].reshape(3 * 128, width)
        biasq = wb[xx, 0, 1:2, :].astype(F32) + wb[xx, 1, 1:2, :].astype(F32)
        biasv = wb[xx, 0, 2:3, :].astype(F32) + wb[xx, 1, 2:3, :].astype(F32)
        pq = jnp.where(t == 0, biasq[:, :128], jnp.where(t == 1, biasq[:, 128:256], biasq[:, 256:384]))
        pv = jnp.where(t == 0, biasv[:, :128], jnp.where(t == 1, biasv[:, 128:256], biasv[:, 256:384]))
        for row in range(rows):
            where = pl.ds(row * seq, seq)
            value = dot(a1_ref[where, :], weights, 1, 1)
            proj_ref[where, part_lanes(group, 0)] = ((value[:, :128] + pq).astype(BF16) * 0.125).astype(BF16)
            proj_ref[where, part_lanes(group, 1)] = value[:, 128:256].astype(BF16)
            proj_ref[where, part_lanes(group, 2)] = (value[:, 256:] + pv).astype(BF16)

    def attend_forward(step):
        xx, t = jnp.where(step < 9, x, nx), (step // 3) % 3
        group = xx * 3 + t
        row = step % 3 - 1
        where = pl.ds(pl.multiple_of(row * seq, seq), seq)
        qs = pick(proj_ref[where, part_lanes(group, 0)], aug_q[where, :])
        ks = pick(proj_ref[where, part_lanes(group, 1)], aug_k[where, :])
        vs = pick(proj_ref[where, part_lanes(group, 2)], jnp.ones((seq, 128), BF16))
        scores = [dot(q, k, 1, 1) for q, k in zip(qs, ks)]
        highest = [jnp.max(item, axis=-1, keepdims=True) for item in scores]
        result = [
            dot(jnp.exp(item - top).astype(BF16), v, 1, 0) for item, top, v in zip(scores, highest, vs)
        ]
        total = pltpu.roll(jnp.where(even, result[1], result[0]), 64, 1)
        mixed = jnp.where(even, result[0], result[1]) / total
        o_ref[where, pl.ds(pl.multiple_of(group * 128, 128), 128)] = mixed.astype(BF16)
        log_total = jnp.where(even, highest[0], highest[1]) + jnp.log(total)
        lse_ref[where, :] = jnp.where(lane % 64 == group, log_total, lse_ref[where, :])

    def second_norm(step, carry):
        due_now(step, PLAN_SECOND)
        where = pl.ds(pl.multiple_of(step * 256, 256), 256)
        value = x_ref[where, :].astype(F32) + dot(o_ref[where, :], wo[...].reshape(width, width), 1, 0) + small(2)
        hat, inv = norm(value)
        hat2_ref[where, :] = hat.astype(BF16)
        spot = lax.broadcasted_iota(jnp.int32, (256, 128), 1)
        lse_ref[where, :] = jnp.where(spot == INV_LANE, inv, lse_ref[where, :])
        a2_ref[where, :] = (small(3) * hat + small(4)).astype(BF16)
        x1_ref[where, :] = value + small(5)
        da2_ref[where, :] = jnp.zeros_like(value)
        return carry

    def pair_place(pair):
        far = sum(jnp.where(pair == p, 1, 0) for p, flag in enumerate(FAR_PAIRS) if flag)
        tile = sum(jnp.where(pair == p, index, 0) for p, index in enumerate(PAIR_TILES))
        return jnp.where(far == 1, nx, x), tile

    def expert_tile(step):
        xx, index = pair_place(step // 2)
        cc = jnp.where(step % 2 == 0, nc, c)
        w_up = wm[xx, cc, index, pl.ds(0, UNIT), :]
        w_down = wm[xx, cc, index, pl.ds(UNIT, UNIT), :]
        lanes = pl.ds(pl.multiple_of(index * UNIT, UNIT), UNIT)
        bias = wb[xx, cc, 0:1, lanes].astype(F32)
        upb_sum = None
        part_rows = tokens // SPLIT
        for part in range(SPLIT):
            where = pl.ds(part * part_rows, part_rows)
            pre = dot(a2_ref[where, :], w_up, 1, 1) + bias
            back = dot(g_ref[where, :], w_down, 1, 1)
            cumul, density = gelu_parts(pre)
            hidden = (pre * cumul).astype(BF16)
            low = (back * (cumul + pre * density)).astype(BF16)
            hid_ref[where, :] = hidden
            low_ref[where, :] = low
            one = column_sum(low.astype(F32))
            upb_sum = one if upb_sum is None else upb_sum + one
        sums[pl.ds(UPB + xx * 2 + cc, 1), lanes] = upb_sum
        base = pl.multiple_of(index * 2 * UNIT, UNIT)
        grad[xx, cc, pl.ds(base, UNIT), :] = dot(low_ref[...], a2_ref[...], 0, 0).astype(BF16)
        grad[xx, cc, pl.ds(base + UNIT, UNIT), :] = dot(hid_ref[...], g_ref[...], 0, 0).astype(BF16)
        x1_ref[...] += dot(hid_ref[...], w_down, 1, 0)
        da2_ref[...] += dot(low_ref[...], w_up, 1, 0)

    def norm_back(grad_in, hat, inv, gain):
        scaled = grad_in * gain
        return inv * (
            scaled
            - jnp.mean(scaled, axis=-1, keepdims=True)
            - hat * jnp.mean(scaled * hat, axis=-1, keepdims=True)
        )

    def add_sum(row, values):
        sums[row : row + 1, :] += column_sum(values)

    heads_rows = 6 * UNIT

    def between_norm():
        def one(step, carry):
            where = at_chunk(step)
            da2, hat = da2_ref[where, :], hat2_ref[where, :].astype(F32)
            top = g_ref[where, :].astype(F32)
            add_sum(GAIN2, da2 * hat)
            add_sum(SHIFT2, da2)
            add_sum(DOWNB, top)
            middle = top + norm_back(da2, hat, lse_ref[where, INV_LANE : INV_LANE + 1], small(3))
            da2_ref[where, :] = middle
            low = middle.astype(BF16)
            add_sum(OUTB, low.astype(F32))
            a2_ref[where, :] = low
            hat2_ref[where, :] = x1_ref[where, :].astype(BF16)
            return carry

        lax.fori_loop(0, tokens // chunk, one, 0)
        mixed_copy.start()

    def between_out():
        for xx in range(2):
            half = dot(o_ref[:, xx * 384 : (xx + 1) * 384], a2_ref[...], 0, 0).astype(BF16)
            for t in range(3):
                for cc in range(2):
                    start = (t * 2 + cc) * 64
                    grad[xx, cc, pl.ds(heads_rows + t * 64, 64), :] = half[start : start + 64]

    def between_back():
        def back(step, carry):
            where = pl.ds(pl.multiple_of(step * 256, 256), 256)
            a2_ref[where, :] = dot(a2_ref[where, :], wo[...].reshape(width, width), 1, 1).astype(BF16)
            return carry

        lax.fori_loop(0, tokens // 256, back, 0)

    def attend_backward(step):
        xx, t = jnp.where(step < 9, nx, x), (step // 3) % 3
        group = xx * 3 + t
        lanes = pl.ds(pl.multiple_of(group * 128, 128), 128)

        def one_row():
            where = pl.ds(pl.multiple_of((step % 3) * seq, seq), seq)
            query, key, value = (proj_ref[where, part_lanes(group, i)] for i in range(3))
            out, back = o_ref[where, lanes], a2_ref[where, lanes]
            none = jnp.zeros((seq, 128), BF16)
            product = out.astype(F32) * back.astype(F32)
            log_total = lse_ref[where, :]
            tops = [
                jnp.sum(jnp.where(lane == group + shift, log_total, 0.0), axis=-1, keepdims=True)
                for shift in (0, 64)
            ]
            deltas = [jnp.sum(item, axis=-1, keepdims=True) for item in pick(product, jnp.zeros_like(product))]
            q_aug, k_aug = pick(query, aug_q[where, :]), pick(key, aug_k[where, :])
            q_own, k_own, b_own = pick(query, none), pick(key, none), pick(back, none)
            v_own = pick(value, none)
            d_query = d_key = d_value = None
            for i in range(2):
                prob = jnp.exp(dot(q_aug[i], k_aug[i], 1, 1) - tops[i])
                low = prob.astype(BF16)
                inner = dot(b_own[i], v_own[i], 1, 1) - deltas[i]
                d_score = (prob * inner).astype(BF16)
                parts = (dot(d_score, k_own[i], 1, 0), dot(d_score, q_own[i], 0, 0), dot(low, b_own[i], 0, 0))
                if i == 0:
                    d_query, d_key, d_value = parts
                else:
                    d_query, d_key, d_value = d_query + parts[0], d_key + parts[1], d_value + parts[2]
            low_query = (d_query * 0.125).astype(BF16)
            low_value = d_value.astype(BF16)
            proj_ref[where, part_lanes(group, 0)] = low_query
            proj_ref[where, part_lanes(group, 1)] = d_key.astype(BF16)
            proj_ref[where, part_lanes(group, 2)] = low_value
            sums[QUERYB : QUERYB + 1, lanes] += column_sum(low_query.astype(F32))
            sums[VALUEB : VALUEB + 1, lanes] += column_sum(low_value.astype(F32))

        def weights():
            weight_grad = dot(proj_ref[:, part_lanes(group, 0, 3)], a1_ref[...], 0, 0).astype(BF16)
            for part in range(3):
                for cc in range(2):
                    start = part * 128 + cc * 64
                    place = pl.multiple_of(heads_rows + 192 + t * 192 + part * 64, 64)
                    grad[xx, cc, pl.ds(place, 64), :] = weight_grad[start : start + 64]
        pl.when(step % 3 < 2)(one_row)
        pl.when(step % 3 == 2)(weights)

    def last_norm(step):
        where = pl.ds(pl.multiple_of(step * 256, 256), 256)
        hat, inv = norm(x_ref[where, :].astype(F32))
        da1 = dot(proj_ref[where, :], wq[...].reshape(3 * width, width), 1, 0)
        add_sum(GAIN1, da1 * hat)
        add_sum(SHIFT1, da1)
        g_ref[where, :] = (da2_ref[where, :] + norm_back(da1, hat, inv, small(0))).astype(BF16)
        pl.when(step == tokens // 256 - 1)(lambda: input_copy.start())

    sums_out_copy = pltpu.make_async_copy(sums, sums_out, small_sem.at[9])
    mixed_copy = pltpu.make_async_copy(hat2_ref, mixed_out, local_sem.at[8])
    input_copy = pltpu.make_async_copy(g_ref, input_out, local_sem.at[9])

    def add_into(xx, start, count, other, other_start):
        size = next(size for size in (64, 48, 32, 16) if count % size == 0)

        def one(step, carry):
            mine = pl.ds(pl.multiple_of(start + step * size, 16), size)
            theirs = pl.ds(pl.multiple_of(other_start + step * size, 16), size)
            grad[xx, c, mine, :] = grad[xx, c, mine, :] + other[theirs, :]
            return carry

        if count == size:
            one(0, 0)
        else:
            lax.fori_loop(0, count // size, one, 0)

    def core_copy(granule):
        far, start, count, _ = GRANULES[granule]
        return remote(
            grad.at[nx if far else x, nc, pl.ds(start, count)],
            mate_buf.at[granule % 2, pl.ds(0, count)],
            core_s.at[granule], core_r.at[granule], mate,
        )

    def core_send(granule):
        core_copy(granule).start()

    def core_add(granule):
        far, start, count, units = GRANULES[granule]
        core_copy(granule).wait_recv()
        add_into(nx if far else x, start, count, mate_buf.at[granule % 2], 0)
        for unit in units:
            if unit in EARLY:
                (early_copy if far else outer_copy)(unit).start()
            elif far:
                x_copy(unit).start()

    def outer(unit):
        return (zb, z_pair) if unit in EARLY else (y, y_peer)

    def inner(unit):
        return (y, y_peer) if unit in EARLY else (zb, z_pair)

    def x_copy(unit):
        where = half_rows(unit, outer(unit)[0]) if unit in EARLY else pl.ds(*UNITS[unit])
        return remote(grad.at[nx, c, where], x_buf.at[where], ex_s.at[unit], ex_r.at[unit], x_peer)

    def half_rows(unit, part):
        start, count = UNITS[unit]
        return pl.ds(pl.multiple_of(start + part * (count // 2), 32), count // 2)

    def share_rows(unit, part):
        start, count = UNITS[unit]
        return pl.ds(pl.multiple_of(start + outer(unit)[0] * (count // 2) + part * (count // 4), 16), count // 4)

    def half_slot(unit):
        return pl.ds(UNITS[unit][0] // 2, UNITS[unit][1] // 2)

    def share_slot(unit):
        return pl.ds(UNITS[unit][0] // 4, UNITS[unit][1] // 4)

    def outer_copy(unit):
        part, peer = outer(unit)
        return remote(
            grad.at[x, c, half_rows(unit, 1 - part)], y_buf.at[half_slot(unit)], ey_s.at[unit], ey_r.at[unit], peer
        )

    def early_copy(unit):
        index = EARLY.index(unit)
        where = pl.ds(index * UNIT // 2, UNIT // 2)
        part, peer = outer(unit)
        return remote(
            grad.at[nx, c, half_rows(unit, 1 - part)], early_buf.at[where], early_s.at[index], early_r.at[index], peer
        )

    def inner_copy(unit):
        part, peer = inner(unit)
        return remote(
            grad.at[x, c, share_rows(unit, 1 - part)], z_buf.at[0, share_slot(unit)], ez_s.at[unit], ez_r.at[unit], peer
        )

    def across_copy(unit):
        return remote(
            grad.at[x, c, share_rows(unit, inner(unit)[0])], z_buf.at[1, share_slot(unit)],
            ew_s.at[unit], ew_r.at[unit], z_far,
        )

    def back_inner_copy(unit):
        part, peer = inner(unit)
        where = share_rows(unit, part)
        return remote(x_buf.at[where], x_buf.at[where], fz_s.at[unit], fz_r.at[unit], peer)

    def back_outer_copy(unit):
        part, peer = outer(unit)
        where = half_rows(unit, part)
        return remote(x_buf.at[where], x_buf.at[where], fy_s.at[unit], fy_r.at[unit], peer)

    def early_x(unit):
        early_copy(unit).wait_recv()
        start = EARLY.index(unit) * UNIT // 2
        add_into(nx, half_rows(unit, outer(unit)[0]).start, UNIT // 2, early_buf, start)
        x_copy(unit).start()

    def early_y(unit):
        outer_copy(unit).wait_recv()
        add_into(x, half_rows(unit, outer(unit)[0]).start, UNIT // 2, y_buf, half_slot(unit).start)

    def early_z(unit):
        x_copy(unit).wait_recv()
        start = half_rows(unit, outer(unit)[0]).start
        add_into(x, start, UNIT // 2, x_buf, start)
        inner_copy(unit).start()

    def add_x(unit):
        x_copy(unit).wait_recv()
        start, count = UNITS[unit]
        add_into(x, start, count, x_buf, start)
        outer_copy(unit).start()

    def add_y(unit):
        outer_copy(unit).wait_recv()
        add_into(x, half_rows(unit, outer(unit)[0]).start, UNITS[unit][1] // 2, y_buf, half_slot(unit).start)
        inner_copy(unit).start()

    def add_z(unit):
        inner_copy(unit).wait_recv()
        start = share_rows(unit, inner(unit)[0]).start
        add_into(x, start, UNITS[unit][1] // 4, z_buf.at[0], share_slot(unit).start)
        across_copy(unit).start()

    def add_far(unit):
        across_copy(unit).wait_recv()
        where = share_rows(unit, inner(unit)[0])
        x_buf[where, :] = grad[x, c, where, :] + z_buf[1, share_slot(unit), :]
        back_inner_copy(unit).start()

    def give_y(unit):
        back_inner_copy(unit).wait_recv()
        back_outer_copy(unit).start()

    def out_copy(unit):
        where = pl.ds(*UNITS[unit])
        return pltpu.make_async_copy(x_buf.at[where], grads_out.at[where], local_sem.at[10 + unit])

    def finish(unit):
        back_outer_copy(unit).wait_recv()
        out_copy(unit).start()

    def sums_copy(slot, source, peer):
        return remote(sums_recv.at[6 + source], sums_recv.at[slot], sums_s.at[slot], sums_r.at[slot], peer)

    small_peers = [(i, i, peer) for i, peer in enumerate((mate, x_peer, y_peer, z_pair, z_far))]

    def sums_step(number):
        if number > 0:
            sums_copy(*small_peers[number - 1]).wait_recv()
            sums_recv[6 + number] = sums_recv[5 + number] + sums_recv[number - 1]
        else:
            sums_recv[6] = sums[...]
        if number < 5:
            sums_copy(*small_peers[number]).start()
        else:
            total = sums_recv[11]
            sums[...] = total
            own_up = sums[pl.ds(UPB + mp, 1), :]
            pairs = jnp.where(x == 0, total[:, :384], total[:, 384:])
            spread = jnp.where(placed, 1.0, 0.0)
            own_qv = lax.dot_general(
                pairs, spread, (((1,), (1,)), ((), ())), precision=lax.Precision.HIGHEST, preferred_element_type=F32
            )
            own_qv = jnp.concatenate([own_qv, jnp.zeros((16, width - own_qv.shape[1]), F32)], axis=1)
            total = jnp.where(tile_row == OWN_UP, own_up, total)
            total = jnp.where(tile_row == OWN_QV, own_qv[QUERYB : QUERYB + 1], total)
            sums[...] = jnp.where(tile_row == OWN_QV + 1, own_qv[VALUEB : VALUEB + 1], total)
            sums_out_copy.start()

    def piece_sends(number, kind, index):
        to_mate(number, kind, index).wait_send()
        to_x(number, kind, index).wait_send()
        for copy in to_square(number, kind, index):
            copy.wait_send()
        forward(number, kind, index).wait_send()

    def settle(number):
        if number < PIECES:
            kinds(number, functools.partial(piece_sends, number))
        elif number == PIECES:
            for granule in range(len(GRANULES)):
                core_copy(granule).wait_send()
        elif number == PIECES + 1:
            mixed_copy.wait()
            input_copy.wait()
            sums_out_copy.wait()
            for copy in biases:
                copy.wait_send()
            for slot, source, peer in small_peers:
                sums_copy(slot, source, peer).wait_send()
        else:
            unit = number - PIECES - 2
            for copy in (x_copy, outer_copy, inner_copy, across_copy, back_inner_copy):
                copy(unit).wait_send()
            if unit in EARLY:
                early_copy(unit).wait_send()

    events = {
        BIAS_DONE: bias_done,
        MATE_DONE: mate_done,
        PASS_X: pass_x,
        PASS_Y: pass_y,
        PASS_DONE: pass_done,
        CORE_ADD: core_add,
        CORE_SEND: core_send,
        EARLY_X: early_x,
        EARLY_Y: early_y,
        EARLY_Z: early_z,
        ADD_X: add_x,
        ADD_Y: add_y,
        ADD_Z: add_z,
        ADD_FAR: add_far,
        GIVE_Y: give_y,
        FINISH: finish,
        SUMS: sums_step,
        SETTLE: settle,
    }

    def run_due(due):
        for name, number in due:
            events[name](number)

    def due_now(step, plan):
        def among(low, high):
            if high - low == 1:
                run_due(plan[low])
                return
            middle = (low + high) // 2
            for first, last, here in ((low, middle, step < middle), (middle, high, step >= middle)):
                if any(plan[first:last]):
                    pl.when(here)(functools.partial(among, first, last))

        among(0, len(plan))

    lax.fori_loop(0, tokens // chunk, first_norm, 0)

    def forward_step(step, carry):
        due_now(step, PLAN_FORWARD)
        pl.when(step % 3 == 0)(lambda: project(step))
        pl.when(step % 3 > 0)(lambda: attend_forward(step))
        return carry

    lax.fori_loop(0, 18, forward_step, 0)
    lax.fori_loop(0, tokens // 256, second_norm, 0)
    sums[...] = jnp.zeros_like(sums)
    locals_[7].wait()

    def main_step(step, carry):
        due_now(step, PLAN_MAIN)
        pl.when(step < BETWEEN)(lambda: expert_tile(step))
        pl.when(step == BETWEEN)(between_norm)
        pl.when(step == BETWEEN + 1)(between_out)
        pl.when(step == BETWEEN + 2)(between_back)
        pl.when(jnp.logical_and(step >= FIRST_HEADS, step < LAST_NORM))(
            lambda: attend_backward(step - FIRST_HEADS)
        )
        pl.when(step >= LAST_NORM)(lambda: last_norm(step - LAST_NORM))
        return carry

    lax.fori_loop(0, LAST_NORM + tokens // 256, main_step, 0)
    run_due(PLAN_DRAIN)


    for unit in range(len(UNITS)):
        back_outer_copy(unit).wait_send()
        out_copy(unit).wait()


def tail_kernel(
    mixed_in, input_in, grads_in, sums_in,
    mixed_out, input_out, qkv_out, wout_out, up_out, down_out,
    qv_out, gain1_out, shift1_out, outb_out, gain2_out, shift2_out, downb_out, upb_out,
    mixed, inputs, grads, qkv, wout, up, down, sums_ref, qv_ref, in_sem, out_sem, small_sem, *vectors,
):
    tiles = down.shape[0]
    heads = qkv.shape[1]
    copies = [
        pltpu.make_async_copy(mixed_in, mixed, in_sem.at[0]),
        pltpu.make_async_copy(input_in, inputs, in_sem.at[1]),
    ]
    loads = []
    for index in range(tiles + 1):
        rows = pl.ds(index * 2 * UNIT, 2 * UNIT if index < tiles else 3 * UNIT)
        loads.append(pltpu.make_async_copy(grads_in.at[rows], grads.at[rows], in_sem.at[2 + index]))
    sums_copy = pltpu.make_async_copy(sums_in, sums_ref, small_sem.at[8])
    for copy in copies + loads + [sums_copy]:
        copy.start()
    stores = [
        pltpu.make_async_copy(mixed, mixed_out, out_sem.at[2 * tiles + 2]),
        pltpu.make_async_copy(inputs, input_out, out_sem.at[2 * tiles + 3]),
    ]
    for copy, store in zip(copies, stores):
        copy.wait()
        store.start()
    for index in range(tiles):
        loads[index].wait()
        start = index * 2 * UNIT
        down[index] = grads[start + UNIT : start + 2 * UNIT, :].astype(F32)
        stores.append(pltpu.make_async_copy(down.at[index], down_out.at[index], out_sem.at[2 * index]))
        stores[-1].start()
        lanes = pl.ds(index * UNIT, UNIT)
        up[:, lanes] = grads[start : start + UNIT, :].astype(F32).T
        stores.append(pltpu.make_async_copy(up.at[:, lanes], up_out.at[:, lanes], out_sem.at[2 * index + 1]))
        stores[-1].start()
    loads[tiles].wait()
    start = 2 * tiles * UNIT
    wout[...] = grads[start : start + heads * HEAD, :].astype(F32)
    stores.append(pltpu.make_async_copy(wout, wout_out, out_sem.at[2 * tiles]))
    stores[-1].start()
    start += heads * HEAD
    for head in range(heads):
        for part in range(3):
            row = start + (head * 3 + part) * HEAD
            qkv[part, head] = grads[row : row + HEAD, :].astype(F32)
    stores.append(pltpu.make_async_copy(qkv, qkv_out, out_sem.at[2 * tiles + 1]))
    stores[-1].start()
    sums_copy.wait()
    for index, (row, out) in enumerate((
        (GAIN1, gain1_out), (SHIFT1, shift1_out), (OUTB, outb_out), (GAIN2, gain2_out), (SHIFT2, shift2_out),
        (DOWNB, downb_out), (OWN_UP, upb_out),
    )):
        vectors[index][...] = sums_ref[row, :]
        stores.append(pltpu.make_async_copy(vectors[index], out, small_sem.at[index]))
        stores[-1].start()
    qv_ref[...] = sums_ref[OWN_QV : OWN_QV + 2, : qv_ref.shape[1]]
    stores.append(pltpu.make_async_copy(qv_ref, qv_out, small_sem.at[7]))
    stores[-1].start()
    for copy in stores:
        copy.wait()


def on_device(
    tokens, segment_ids, cotangent, norm1_gain, norm1_shift, w_qkv, qv_bias, w_out, out_bias,
    norm2_gain, norm2_shift, w_up, up_bias, w_down, down_bias,
):
    rows, seq, width = tokens.shape
    count = rows * seq
    shard = w_up.shape[1]
    heads = w_out.shape[0] // HEAD
    tiles = shard // UNIT
    units = 2 * tiles + 3
    qkv_rows = jnp.transpose(w_qkv, (1, 2, 0)).reshape(3, heads, HEAD, width)

    any_space = pl.BlockSpec(memory_space=pl.ANY)
    dma = pltpu.SemaphoreType.DMA
    vm = pltpu.VMEM
    mixed, input_grad, grads, sums = pl.pallas_call(
        functools.partial(kernel, rows=rows, seq=seq),
        out_shape=(
            jax.ShapeDtypeStruct((count, width), BF16),
            jax.ShapeDtypeStruct((count, width), BF16),
            jax.ShapeDtypeStruct((units * UNIT, width), BF16),
            jax.ShapeDtypeStruct((16, width), F32),
        ),
        in_specs=[any_space] * 15,
        out_specs=(any_space,) * 4,
        scratch_shapes=[
            vm((2, heads, 3, 2, HEAD, width), BF16),
            vm((2, heads, 2, HEAD, width), BF16),
            vm((2, 2, tiles, 2 * UNIT, width), BF16),
            vm((2, 2, 16, width), BF16),
            vm((2, 2, units * UNIT, width), BF16),
            vm((2, 2 * UNIT, width), BF16),
            vm((len(EARLY) * UNIT // 2, width), BF16),
            vm((units * UNIT, width), BF16),
            vm((units * UNIT // 2, width), BF16),
            vm((2, units * UNIT // 4, width), BF16),
            vm((count, width), BF16),
            vm((count, width), BF16),
            vm((count, width), BF16),
            vm((count, 2 * heads * 3 * 128), BF16),
            vm((count, width), BF16),
            vm((count, width), F32),
            vm((count, width), BF16),
            vm((count, width), BF16),
            vm((count, width), F32),
            vm((count, UNIT), BF16),
            vm((count, UNIT), BF16),
            vm((count, 128), F32),
            vm((count, 128), BF16),
            vm((count, 128), BF16),
            vm((16, width), F32),
            vm((12, 16, width), F32),
            vm((rows, seq), jnp.int32),
            *[vm((width,), BF16)] * 7,
            vm((2, heads * HEAD), BF16),
            dma((10,)),
            dma((10 + len(UNITS),)),
            *[dma((PIECES,))] * 12, dma((3,)), dma((3,)),
            dma((len(GRANULES),)), dma((len(GRANULES),)), dma((len(EARLY),)), dma((len(EARLY),)),
            *[dma((len(UNITS),))] * 12,
            dma((6,)), dma((6,)),
        ],
        compiler_params=pltpu.CompilerParams(
            collective_id=0, has_side_effects=True, vmem_limit_bytes=64 * 2**20 - 2**16
        ),
    )(
        tokens.reshape(count, width), cotangent.reshape(count, width), segment_ids,
        norm1_gain, norm1_shift, out_bias, norm2_gain, norm2_shift, down_bias, up_bias, qv_bias,
        qkv_rows, w_out.reshape(heads, HEAD, width), w_up, w_down.reshape(tiles, UNIT, width),
    )

    groups = lax.axis_size("dp") // 8
    if groups > 1:
        grads, sums = lax.psum((grads.astype(F32) * 0.125, sums * 0.125), "dp")
    whole = [jax.ShapeDtypeStruct((width,), F32)] * 7
    results = pl.pallas_call(
        tail_kernel,
        out_shape=(
            mixed, input_grad,
            jax.ShapeDtypeStruct((3, heads, HEAD, width), F32), jax.ShapeDtypeStruct((heads * HEAD, width), F32),
            jax.ShapeDtypeStruct((width, shard), F32), jax.ShapeDtypeStruct((tiles, UNIT, width), F32),
            jax.ShapeDtypeStruct((2, heads * HEAD), F32), *whole,
        ),
        in_specs=[any_space] * 4,
        out_specs=(any_space,) * 14,
        scratch_shapes=[
            vm((count, width), BF16), vm((count, width), BF16), vm(grads.shape, grads.dtype),
            vm((3, heads, HEAD, width), F32), vm((heads * HEAD, width), F32),
            vm((width, shard), F32), vm((tiles, UNIT, width), F32),
            vm((16, width), F32), vm((2, heads * HEAD), F32),
            dma((2 + tiles + 1,)), dma((2 * tiles + 4,)), dma((9,)),
            *[vm((width,), F32)] * 7,
        ],
        compiler_params=pltpu.CompilerParams(vmem_limit_bytes=63 * 2**20),
    )(mixed, input_grad, grads, sums)
    mixed, input_grad, grad_qkv, grad_out, grad_up, grad_down, grad_qv, *vectors = results
    gain1, shift1, outb, gain2, shift2, downb, upb = vectors
    return (
        mixed.reshape(rows, seq, width),
        input_grad.reshape(rows, seq, width),
        gain1,
        shift1,
        jnp.transpose(grad_qkv.reshape(3, heads * HEAD, width), (2, 0, 1)),
        grad_qv,
        grad_out,
        outb,
        gain2,
        shift2,
        grad_up,
        upb,
        grad_down.reshape(shard, width),
        downb,
    )


def solution(mesh):
    tall = P(("dp", "mp"), None, None)
    return jax.shard_map(
        on_device,
        mesh=mesh,
        in_specs=(
            tall, P(("dp", "mp"), None), tall, P(), P(), P(None, None, "mp"), P(None, "mp"), P("mp", None),
            P(), P(), P(), P(None, "mp"), P("mp"), P("mp", None), P(),
        ),
        out_specs=(
            tall, tall, P(), P(), P(None, None, "mp"), P(None, "mp"), P("mp", None), P(), P(), P(),
            P(None, "mp"), P("mp"), P("mp", None), P(),
        ),
        check_vma=False,
    )
```

```python
import functools

import jax
import jax.numpy as jnp
from jax import lax
from jax.experimental import pallas as pl
from jax.experimental.pallas import tpu as pltpu
from jax.sharding import PartitionSpec as P

HEAD = 64
EPS = 1e-06
MASKED = -1e30
UNIT = 256
SPLIT = 4
INV_LANE = 32
OWN_UP, OWN_QV = 12, 13
F32, BF16 = jnp.float32, jnp.bfloat16

GAIN1, SHIFT1, OUTB, GAIN2, SHIFT2, DOWNB, QUERYB, VALUEB, UPB = range(9)

KINDS = 16
(
    TO_MATE, TO_X, TO_Y, TO_Z, TO_CORNER, FORWARD, BIAS, CORE, EARLY_OUT, X_OUT, OUTER, INNER, ACROSS, BACK_INNER,
    BACK_OUTER, SUMS_OUT,
) = range(KINDS)

UNITS = (
    (0, 128),
    (128, 128),
    (256, 128),
    (384, 128),
    (512, 128),
    (640, 128),
    (768, 128),
    (896, 128),
    (1024, 128),
    (1152, 128),
    (1280, 128),
    (1408, 128),
    (1536, 192),
    (1728, 192),
    (1920, 128),
    (2048, 64),
    (2112, 64),
    (2176, 64),
    (2240, 64),
)
GRANULES = (
    (0, 0, 512, (0, 1, 2, 3)),
    (1, 0, 512, (0, 1, 2, 3)),
    (0, 512, 512, (4, 5, 6, 7)),
    (1, 512, 512, (4, 5, 6, 7)),
    (0, 1024, 512, (8, 9, 10, 11)),
    (1, 1024, 512, (8, 9, 10, 11)),
    (1, 1536, 192, (12,)),
    (0, 1536, 192, (12,)),
    (1, 1728, 192, (13,)),
    (1, 1920, 192, (14, 15)),
    (1, 2112, 192, (16, 17, 18)),
    (0, 1728, 192, (13,)),
    (0, 1920, 192, (14, 15)),
    (0, 2112, 192, (16, 17, 18)),
)
EARLY = (0, 1, 4, 5)
PIECES, AHEAD = 10, 3
FAR_PAIRS = (0, 1, 0, 1, 0, 1)
PAIR_TILES = (0, 0, 1, 1, 2, 2)
BETWEEN, FIRST_HEADS, LAST_NORM = 12, 15, 33
(
    BIAS_DONE, MATE_DONE, PASS_X, PASS_Y, PASS_DONE, CORE_ADD, CORE_SEND, EARLY_X, EARLY_Y, EARLY_Z,
    ADD_X, ADD_Y, ADD_Z, ADD_FAR, GIVE_Y, FINISH, SUMS,
) = range(17)
PLAN_FORWARD = (
    ((MATE_DONE, 0), (BIAS_DONE, 0),),
    ((PASS_X, 0),),
    (),
    ((PASS_X, 1), (MATE_DONE, 1),),
    ((PASS_X, 2),),
    (),
    ((PASS_X, 3), (MATE_DONE, 2),),
    ((PASS_Y, 0),),
    ((PASS_X, 4),),
    ((PASS_DONE, 0), (BIAS_DONE, 1), (BIAS_DONE, 2),),
    ((PASS_X, 5), (PASS_Y, 1),),
    (),
    ((PASS_X, 6), (PASS_DONE, 1),),
    ((PASS_Y, 2),),
    ((PASS_X, 7),),
    ((PASS_DONE, 2),),
    ((PASS_X, 8), (PASS_Y, 3),),
    (),
)
PLAN_SECOND = (
    ((PASS_X, 9), (MATE_DONE, 3), (PASS_DONE, 3),),
    (),
    (),
    ((PASS_Y, 4),),
)
PLAN_MAIN = (
    ((MATE_DONE, 4), (MATE_DONE, 5),),
    ((PASS_Y, 5), (CORE_SEND, 0),),
    ((PASS_DONE, 4), (PASS_DONE, 5),),
    ((PASS_Y, 6), (CORE_ADD, 0), (CORE_SEND, 1),),
    ((PASS_Y, 7), (MATE_DONE, 6), (MATE_DONE, 7),),
    ((PASS_Y, 8), (CORE_ADD, 1), (CORE_SEND, 2),),
    ((PASS_DONE, 6), (PASS_DONE, 7),),
    ((EARLY_Y, 0), (PASS_Y, 9), (CORE_ADD, 2), (CORE_SEND, 3), (ADD_X, 2),),
    ((EARLY_Y, 1), (EARLY_X, 0), (MATE_DONE, 8), (MATE_DONE, 9),),
    ((ADD_Y, 2), (CORE_ADD, 3), (EARLY_Y, 4), (CORE_SEND, 4), (ADD_X, 3), (EARLY_X, 1),),
    ((EARLY_Z, 0), (EARLY_Y, 5), (ADD_Z, 2), (CORE_ADD, 4), (PASS_DONE, 8), (PASS_DONE, 9),),
    ((ADD_Y, 3), (ADD_Z, 0), (CORE_SEND, 5), (ADD_X, 6), (EARLY_X, 4), (EARLY_X, 5),),
    ((ADD_FAR, 2), (ADD_Z, 3), (CORE_ADD, 5), (ADD_X, 7),),
    ((ADD_Y, 6), (ADD_FAR, 0), (EARLY_Z, 1), (GIVE_Y, 2), (EARLY_Z, 4),),
    ((ADD_Y, 7), (ADD_FAR, 3), (EARLY_Z, 5), (CORE_SEND, 6),),
    ((ADD_Z, 1), (ADD_Z, 6), (CORE_ADD, 6), (CORE_SEND, 7), (GIVE_Y, 0),),
    ((FINISH, 2), (ADD_Z, 7), (ADD_Z, 4), (CORE_ADD, 7), (ADD_X, 8), (GIVE_Y, 3),),
    ((ADD_FAR, 1), (ADD_Z, 5),),
    ((CORE_SEND, 8), (ADD_X, 9), (FINISH, 0),),
    ((ADD_Y, 8), (ADD_FAR, 6), (CORE_ADD, 8),),
    ((FINISH, 3), (ADD_FAR, 7), (ADD_X, 10), (ADD_FAR, 4), (GIVE_Y, 1),),
    ((ADD_Z, 8), (CORE_SEND, 9), (ADD_Y, 9), (GIVE_Y, 6),),
    ((ADD_FAR, 5), (CORE_ADD, 9), (ADD_X, 11), (ADD_Y, 10), (GIVE_Y, 7),),
    ((FINISH, 1), (ADD_FAR, 8), (GIVE_Y, 4),),
    ((FINISH, 6), (ADD_Z, 9), (CORE_SEND, 10),),
    ((ADD_Z, 10), (CORE_ADD, 10), (ADD_X, 12), (GIVE_Y, 5), (GIVE_Y, 8), (ADD_Y, 11),),
    ((FINISH, 4), (FINISH, 7), (ADD_FAR, 9),),
    ((CORE_SEND, 11),),
    ((ADD_Y, 12), (ADD_FAR, 10), (FINISH, 5), (CORE_ADD, 11), (ADD_X, 13),),
    ((FINISH, 8), (ADD_Z, 11), (GIVE_Y, 9),),
    ((CORE_SEND, 12), (ADD_Z, 12),),
    ((ADD_Y, 13), (CORE_ADD, 12), (ADD_X, 14), (ADD_X, 15), (GIVE_Y, 10),),
    ((FINISH, 9), (ADD_FAR, 11),),
    ((CORE_SEND, 13), (ADD_Z, 13),),
    ((ADD_Y, 14), (ADD_FAR, 12), (ADD_Y, 15), (CORE_ADD, 13), (ADD_X, 16), (ADD_X, 17), (ADD_X, 18), (GIVE_Y, 11),),
    ((FINISH, 10),),
    ((ADD_Y, 16), (ADD_Z, 14), (ADD_FAR, 13), (GIVE_Y, 12), (ADD_Y, 17),),
)
PLAN_DRAIN = (
    (ADD_Y, 18),
    (ADD_Z, 15),
    (SUMS, 0),
    (ADD_Z, 16),
    (FINISH, 11),
    (SUMS, 1),
    (ADD_FAR, 14),
    (GIVE_Y, 13),
    (ADD_Z, 17),
    (ADD_Z, 18),
    (ADD_FAR, 15),
    (FINISH, 12),
    (ADD_FAR, 16),
    (SUMS, 2),
    (GIVE_Y, 14),
    (ADD_FAR, 17),
    (GIVE_Y, 15),
    (SUMS, 3),
    (GIVE_Y, 16),
    (FINISH, 13),
    (ADD_FAR, 18),
    (GIVE_Y, 17),
    (SUMS, 4),
    (FINISH, 14),
    (GIVE_Y, 18),
    (FINISH, 15),
    (FINISH, 16),
    (SUMS, 5),
    (FINISH, 17),
    (FINISH, 18),
)

def dot(left, right, left_dim, right_dim):
    return lax.dot_general(
        left, right, (((left_dim,), (right_dim,)), ((), ())), preferred_element_type=F32
    )


def column_sum(values):
    return jnp.sum(values, axis=0, keepdims=True)


def gelu_parts(pre):
    cumul = 0.5 + 0.5 * lax.erf(pre * 0.7071067811865476)
    return cumul, jnp.exp(-0.5 * pre * pre) * 0.3989422804014327


def kernel(
    x_in, g_in, seg_in, gain1_in, shift1_in, outb_in, gain2_in, shift2_in, downb_in, upb_in, qvb_in,
    qkv_in, out_in, up_in, down_in,
    mixed_out, input_out, grads_out, sums_out,
    wq, wo, wm, wb, grad, mate_buf, early_buf, x_buf, y_buf, z_buf,
    x_ref, g_ref, a1_ref, proj_ref, o_ref, x1_ref, hat2_ref, a2_ref, da2_ref,
    hid_ref, low_ref, lse_ref, aug_q, aug_k, sums, sums_recv,
    seg_ref, gain1_ref, shift1_ref, outb_ref, gain2_ref, shift2_ref, downb_ref, upb_ref, qvb_ref, small_sem,
    local_sem, sent, wm_r, wx_r, wy_r, wz_r, wd_r, wf_r, wb_r,
    core_r, early_r, ex_r, ey_r, ez_r, ew_r, fz_r, fy_r, sums_r,
    *, rows, seq,
):
    tokens, width = x_ref.shape
    dp, mp = lax.axis_index("dp"), lax.axis_index("mp")
    c, x = mp % 2, mp // 2
    y, z = dp % 2, (dp // 2) % 4
    block = dp - dp % 8
    zb = z % 2
    nx, nc, ny = 1 - x, 1 - c, 1 - y

    def device(zz, yy, xx, cc):
        return (block + zz * 2 + yy, xx * 2 + cc)

    mate = device(z, y, x, nc)
    x_peer = device(z, y, nx, c)
    y_peer = device(z, ny, x, c)
    z_far = device((z + 2) % 4, y, x, c)
    z_pair = device(z + 1 - 2 * zb, y, x, c)
    cross = device(z, y, nx, nc)
    corner = device(z + 1 - 2 * zb, ny, x, c)

    def remote(src, dst, send, recv, where):
        return pltpu.make_async_remote_copy(
            src_ref=src, dst_ref=dst, send_sem=send, recv_sem=recv,
            device_id=where, device_id_type=pl.DeviceIdType.MESH,
        )

    barrier = pltpu.get_barrier_semaphore()
    everyone = [mate, x_peer, cross, y_peer, z_pair, z_far, corner]
    for peer in everyone:
        pl.semaphore_signal(barrier, inc=1, device_id=peer, device_id_type=pl.DeviceIdType.MESH)

    up_stage = grad.at[0, 0, pl.ds(0, width)]
    locals_ = [
        pltpu.make_async_copy(qkv_in.at[:, 0], wq.at[x, 0, :, c], local_sem.at[0]),
        pltpu.make_async_copy(qkv_in.at[:, 1], wq.at[x, 1, :, c], local_sem.at[1]),
        pltpu.make_async_copy(qkv_in.at[:, 2], wq.at[x, 2, :, c], local_sem.at[2]),
        pltpu.make_async_copy(x_in, x_ref, local_sem.at[3]),
        pltpu.make_async_copy(out_in, wo.at[x, :, c], local_sem.at[4]),
        pltpu.make_async_copy(up_in, up_stage, local_sem.at[5]),
        pltpu.make_async_copy(down_in, wm.at[x, c, :, pl.ds(UNIT, UNIT)], local_sem.at[6]),
        pltpu.make_async_copy(g_in, g_ref, local_sem.at[7]),
    ]
    small_copies = [
        pltpu.make_async_copy(src, dst, small_sem.at[i])
        for i, (src, dst) in enumerate((
            (seg_in, seg_ref), (upb_in, upb_ref), (qvb_in, qvb_ref), (gain1_in, gain1_ref), (shift1_in, shift1_ref),
            (outb_in, outb_ref), (gain2_in, gain2_ref), (shift2_in, shift2_ref), (downb_in, downb_ref),
        ))
    ]
    for copy in small_copies + locals_:
        copy.start()
    for copy in small_copies:
        copy.wait()

    from_lane = lax.broadcasted_iota(jnp.int32, (qvb_ref.shape[1], 384), 0)
    to_lane = lax.broadcasted_iota(jnp.int32, (qvb_ref.shape[1], 384), 1)
    placed = jnp.logical_and(
        from_lane == (to_lane // 128) * 64 + to_lane % 64, (to_lane // 64) % 2 == c
    )
    place = jnp.where(placed, 1.0, 0.0).astype(BF16)
    qv_rows = dot(qvb_ref[...], place, 1, 0)
    qv_rows = jnp.concatenate([qv_rows, jnp.zeros((2, width - 384), F32)], axis=1)
    tile_row = lax.broadcasted_iota(jnp.int32, (16, width), 0)
    wb[x, c] = jnp.where(
        tile_row == 0,
        upb_ref[...].astype(F32).reshape(1, width),
        jnp.where(tile_row == 1, qv_rows[0:1], jnp.where(tile_row == 2, qv_rows[1:2], 0.0)),
    ).astype(BF16)
    lane = lax.broadcasted_iota(jnp.int32, (seq, 128), 1)
    for row in range(rows):
        ids = jnp.broadcast_to(seg_ref[row : row + 1, :].astype(F32), (128, seq)).T
        spot = lane % 64
        same = spot == ids.astype(jnp.int32)
        inside = spot < 32
        where = pl.ds(row * seq, seq)
        aug_q[where, :] = jnp.where(same, 1.0, 0.0).astype(BF16)
        aug_k[where, :] = jnp.where(jnp.logical_and(inside, jnp.logical_not(same)), MASKED, 0.0).astype(BF16)
    lse_ref[...] = jnp.zeros_like(lse_ref)
    for number in (0, 1, 2, 4):
        locals_[number].wait()
    pl.semaphore_wait(barrier, len(everyone))

    def piece(kind, index, xx, cc, part=None):
        if kind == "q":
            return wq.at[xx, index, :, cc, some(HEAD, part)]
        if kind == "o":
            return wo.at[xx, :, cc, some(HEAD, part)]
        return wm.at[xx, cc, index // 2, some(UNIT, part, (index % 2) * UNIT)]

    def some(count, part, start=0):
        if part is None:
            return pl.ds(start, count)
        return pl.ds(pl.multiple_of(start + part * (count // 4), 16), count // 4)

    quarter = y * 2 + zb

    def kinds(number, run):
        run("q" if number < 3 else "o" if number == 3 else "m", number - 4 if number > 3 else number)

    def to_mate(number, kind, index):
        own = piece(kind, index, x, c)
        return remote(own, own, sent.at[TO_MATE], wm_r.at[number], mate)

    def to_x(number, kind, index):
        own = piece(kind, index, x, c, quarter)
        return remote(own, own, sent.at[TO_X], wx_r.at[number], x_peer)

    def to_square(number, kind, index):
        held = piece(kind, index, nx, c, quarter)
        return [
            remote(held, held, sent.at[send], recv.at[number], peer)
            for send, recv, peer in ((TO_Y, wy_r, y_peer), (TO_Z, wz_r, z_pair), (TO_CORNER, wd_r, corner))
        ]

    def forward(number, kind, index):
        held = piece(kind, index, nx, c)
        return remote(held, held, sent.at[FORWARD], wf_r.at[number], mate)

    def mate_done(number):
        kinds(number, lambda kind, index: to_mate(number, kind, index).wait_recv())

    def start_x(number):
        kinds(number, lambda kind, index: to_x(number, kind, index).start())

    def pass_x(number):
        def run(kind, index):
            to_x(number, kind, index).wait_recv()
            for copy in to_square(number, kind, index):
                copy.start()

        kinds(number, run)
        if number + AHEAD < PIECES:
            start_x(number + AHEAD)

    def pass_y(number):
        def run(kind, index):
            for copy in to_square(number, kind, index):
                copy.wait_recv()
            forward(number, kind, index).start()

        kinds(number, run)

    def bias_done(number):
        biases[number].wait_recv()

    def pass_done(number):
        kinds(number, lambda kind, index: forward(number, kind, index).wait_recv())

    biases = [
        remote(wb.at[x, c], wb.at[x, c], sent.at[BIAS], wb_r.at[i], peer)
        for i, peer in enumerate((mate, x_peer, cross))
    ]
    for copy in biases:
        copy.start()
    for number in range(AHEAD):
        start_x(number)
        if number < 3:
            kinds(number, lambda kind, index: to_mate(number, kind, index).start())
    for number in range(min(AHEAD, 3), 4):
        kinds(number, lambda kind, index: to_mate(number, kind, index).start())
    locals_[5].wait()
    locals_[6].wait()
    tiles = up_stage.shape[1] // UNIT
    for index in range(tiles):
        wm[x, c, index, pl.ds(0, UNIT), :] = up_stage[:, index * UNIT : (index + 1) * UNIT].T
    for number in range(4, PIECES):
        kinds(number, lambda kind, index: to_mate(number, kind, index).start())

    chunk = 128
    locals_[3].wait()
    small_refs = (gain1_ref, shift1_ref, outb_ref, gain2_ref, shift2_ref, downb_ref)

    def small(row):
        return small_refs[row][...].astype(F32).reshape(1, width)

    def norm(values):
        centred = values - jnp.mean(values, axis=-1, keepdims=True)
        inv = lax.rsqrt(jnp.mean(centred * centred, axis=-1, keepdims=True) + EPS)
        return centred * inv, inv

    def at_chunk(step):
        return pl.ds(pl.multiple_of(step * chunk, chunk), chunk)

    def first_norm(step, carry):
        where = at_chunk(step)
        hat, _ = norm(x_ref[where, :].astype(F32))
        a1_ref[where, :] = (small(0) * hat + small(1)).astype(BF16)
        return carry

    even = lane < 64

    def pick(values, others):
        return jnp.where(even, values, others), jnp.where(even, others, values)

    def part_lanes(group, part, count=1):
        return pl.ds(pl.multiple_of(group * 384 + part * 128, 128), count * 128)

    def project(step):
        xx, t = jnp.where(step < 9, x, nx), (step // 3) % 3
        group = xx * 3 + t
        weights = wq[xx, t].reshape(3 * 128, width)
        biasq = wb[xx, 0, 1:2, :].astype(F32) + wb[xx, 1, 1:2, :].astype(F32)
        biasv = wb[xx, 0, 2:3, :].astype(F32) + wb[xx, 1, 2:3, :].astype(F32)
        pq = jnp.where(t == 0, biasq[:, :128], jnp.where(t == 1, biasq[:, 128:256], biasq[:, 256:384]))
        pv = jnp.where(t == 0, biasv[:, :128], jnp.where(t == 1, biasv[:, 128:256], biasv[:, 256:384]))
        for row in range(rows):
            where = pl.ds(row * seq, seq)
            value = dot(a1_ref[where, :], weights, 1, 1)
            proj_ref[where, part_lanes(group, 0)] = ((value[:, :128] + pq).astype(BF16) * 0.125).astype(BF16)
            proj_ref[where, part_lanes(group, 1)] = value[:, 128:256].astype(BF16)
            proj_ref[where, part_lanes(group, 2)] = (value[:, 256:] + pv).astype(BF16)

    def attend_forward(step):
        xx, t = jnp.where(step < 9, x, nx), (step // 3) % 3
        group = xx * 3 + t
        row = step % 3 - 1
        where = pl.ds(pl.multiple_of(row * seq, seq), seq)
        qs = pick(proj_ref[where, part_lanes(group, 0)], aug_q[where, :])
        ks = pick(proj_ref[where, part_lanes(group, 1)], aug_k[where, :])
        vs = pick(proj_ref[where, part_lanes(group, 2)], jnp.ones((seq, 128), BF16))
        scores = [dot(q, k, 1, 1) for q, k in zip(qs, ks)]
        highest = [jnp.max(item, axis=-1, keepdims=True) for item in scores]
        result = [
            dot(jnp.exp(item - top).astype(BF16), v, 1, 0) for item, top, v in zip(scores, highest, vs)
        ]
        total = pltpu.roll(jnp.where(even, result[1], result[0]), 64, 1)
        mixed = jnp.where(even, result[0], result[1]) / total
        o_ref[where, pl.ds(pl.multiple_of(group * 128, 128), 128)] = mixed.astype(BF16)
        log_total = jnp.where(even, highest[0], highest[1]) + jnp.log(total)
        lse_ref[where, :] = jnp.where(lane % 64 == group, log_total, lse_ref[where, :])

    def second_norm(step, carry):
        due_now(step, PLAN_SECOND)
        where = pl.ds(pl.multiple_of(step * 256, 256), 256)
        value = x_ref[where, :].astype(F32) + dot(o_ref[where, :], wo[...].reshape(width, width), 1, 0) + small(2)
        hat, inv = norm(value)
        hat2_ref[where, :] = hat.astype(BF16)
        spot = lax.broadcasted_iota(jnp.int32, (256, 128), 1)
        lse_ref[where, :] = jnp.where(spot == INV_LANE, inv, lse_ref[where, :])
        a2_ref[where, :] = (small(3) * hat + small(4)).astype(BF16)
        x1_ref[where, :] = value + small(5)
        da2_ref[where, :] = jnp.zeros_like(value)
        return carry

    def pair_place(pair):
        far = sum(jnp.where(pair == p, 1, 0) for p, flag in enumerate(FAR_PAIRS) if flag)
        tile = sum(jnp.where(pair == p, index, 0) for p, index in enumerate(PAIR_TILES))
        return jnp.where(far == 1, nx, x), tile

    def expert_tile(step):
        xx, index = pair_place(step // 2)
        cc = jnp.where(step % 2 == 0, nc, c)
        w_up = wm[xx, cc, index, pl.ds(0, UNIT), :]
        w_down = wm[xx, cc, index, pl.ds(UNIT, UNIT), :]
        lanes = pl.ds(pl.multiple_of(index * UNIT, UNIT), UNIT)
        bias = wb[xx, cc, 0:1, lanes].astype(F32)
        upb_sum = None
        part_rows = tokens // SPLIT
        for part in range(SPLIT):
            where = pl.ds(part * part_rows, part_rows)
            pre = dot(a2_ref[where, :], w_up, 1, 1) + bias
            back = dot(g_ref[where, :], w_down, 1, 1)
            cumul, density = gelu_parts(pre)
            hidden = (pre * cumul).astype(BF16)
            low = (back * (cumul + pre * density)).astype(BF16)
            hid_ref[where, :] = hidden
            low_ref[where, :] = low
            one = column_sum(low.astype(F32))
            upb_sum = one if upb_sum is None else upb_sum + one
        sums[pl.ds(UPB + xx * 2 + cc, 1), lanes] = upb_sum
        base = pl.multiple_of(index * 2 * UNIT, UNIT)
        grad[xx, cc, pl.ds(base, UNIT), :] = dot(low_ref[...], a2_ref[...], 0, 0).astype(BF16)
        grad[xx, cc, pl.ds(base + UNIT, UNIT), :] = dot(hid_ref[...], g_ref[...], 0, 0).astype(BF16)
        x1_ref[...] += dot(hid_ref[...], w_down, 1, 0)
        da2_ref[...] += dot(low_ref[...], w_up, 1, 0)

    def norm_back(grad_in, hat, inv, gain):
        scaled = grad_in * gain
        return inv * (
            scaled
            - jnp.mean(scaled, axis=-1, keepdims=True)
            - hat * jnp.mean(scaled * hat, axis=-1, keepdims=True)
        )

    def add_sum(row, values):
        sums[row : row + 1, :] += column_sum(values)

    heads_rows = 6 * UNIT

    def between_norm():
        def one(step, carry):
            where = at_chunk(step)
            da2, hat = da2_ref[where, :], hat2_ref[where, :].astype(F32)
            top = g_ref[where, :].astype(F32)
            add_sum(GAIN2, da2 * hat)
            add_sum(SHIFT2, da2)
            add_sum(DOWNB, top)
            middle = top + norm_back(da2, hat, lse_ref[where, INV_LANE : INV_LANE + 1], small(3))
            da2_ref[where, :] = middle
            low = middle.astype(BF16)
            add_sum(OUTB, low.astype(F32))
            a2_ref[where, :] = low
            hat2_ref[where, :] = x1_ref[where, :].astype(BF16)
            return carry

        lax.fori_loop(0, tokens // chunk, one, 0)
        mixed_copy.start()

    def between_out():
        for xx in range(2):
            half = dot(o_ref[:, xx * 384 : (xx + 1) * 384], a2_ref[...], 0, 0).astype(BF16)
            for t in range(3):
                for cc in range(2):
                    start = (t * 2 + cc) * 64
                    grad[xx, cc, pl.ds(heads_rows + t * 64, 64), :] = half[start : start + 64]

    def between_back():
        def back(step, carry):
            where = pl.ds(pl.multiple_of(step * 256, 256), 256)
            a2_ref[where, :] = dot(a2_ref[where, :], wo[...].reshape(width, width), 1, 1).astype(BF16)
            return carry

        lax.fori_loop(0, tokens // 256, back, 0)

    def attend_backward(step):
        xx, t = jnp.where(step < 9, nx, x), (step // 3) % 3
        group = xx * 3 + t
        lanes = pl.ds(pl.multiple_of(group * 128, 128), 128)

        def one_row():
            where = pl.ds(pl.multiple_of((step % 3) * seq, seq), seq)
            query, key, value = (proj_ref[where, part_lanes(group, i)] for i in range(3))
            out, back = o_ref[where, lanes], a2_ref[where, lanes]
            none = jnp.zeros((seq, 128), BF16)
            product = out.astype(F32) * back.astype(F32)
            log_total = lse_ref[where, :]
            tops = [
                jnp.sum(jnp.where(lane == group + shift, log_total, 0.0), axis=-1, keepdims=True)
                for shift in (0, 64)
            ]
            deltas = [jnp.sum(item, axis=-1, keepdims=True) for item in pick(product, jnp.zeros_like(product))]
            q_aug, k_aug = pick(query, aug_q[where, :]), pick(key, aug_k[where, :])
            q_own, k_own, b_own = pick(query, none), pick(key, none), pick(back, none)
            v_own = pick(value, none)
            d_query = d_key = d_value = None
            for i in range(2):
                prob = jnp.exp(dot(q_aug[i], k_aug[i], 1, 1) - tops[i])
                low = prob.astype(BF16)
                inner = dot(b_own[i], v_own[i], 1, 1) - deltas[i]
                d_score = (prob * inner).astype(BF16)
                parts = (dot(d_score, k_own[i], 1, 0), dot(d_score, q_own[i], 0, 0), dot(low, b_own[i], 0, 0))
                if i == 0:
                    d_query, d_key, d_value = parts
                else:
                    d_query, d_key, d_value = d_query + parts[0], d_key + parts[1], d_value + parts[2]
            low_query = (d_query * 0.125).astype(BF16)
            low_value = d_value.astype(BF16)
            proj_ref[where, part_lanes(group, 0)] = low_query
            proj_ref[where, part_lanes(group, 1)] = d_key.astype(BF16)
            proj_ref[where, part_lanes(group, 2)] = low_value
            sums[QUERYB : QUERYB + 1, lanes] += column_sum(low_query.astype(F32))
            sums[VALUEB : VALUEB + 1, lanes] += column_sum(low_value.astype(F32))

        def weights():
            weight_grad = dot(proj_ref[:, part_lanes(group, 0, 3)], a1_ref[...], 0, 0).astype(BF16)
            for part in range(3):
                for cc in range(2):
                    start = part * 128 + cc * 64
                    place = pl.multiple_of(heads_rows + 192 + t * 192 + part * 64, 64)
                    grad[xx, cc, pl.ds(place, 64), :] = weight_grad[start : start + 64]
        pl.when(step % 3 < 2)(one_row)
        pl.when(step % 3 == 2)(weights)

    def last_norm(step):
        where = pl.ds(pl.multiple_of(step * 256, 256), 256)
        hat, inv = norm(x_ref[where, :].astype(F32))
        da1 = dot(proj_ref[where, :], wq[...].reshape(3 * width, width), 1, 0)
        add_sum(GAIN1, da1 * hat)
        add_sum(SHIFT1, da1)
        g_ref[where, :] = (da2_ref[where, :] + norm_back(da1, hat, inv, small(0))).astype(BF16)
        pl.when(step == tokens // 256 - 1)(lambda: input_copy.start())

    sums_out_copy = pltpu.make_async_copy(sums, sums_out, small_sem.at[9])
    mixed_copy = pltpu.make_async_copy(hat2_ref, mixed_out, local_sem.at[8])
    input_copy = pltpu.make_async_copy(g_ref, input_out, local_sem.at[9])

    def add_into(xx, start, count, other, other_start):
        size = next(size for size in (64, 48, 32, 16) if count % size == 0)

        def one(step, carry):
            mine = pl.ds(pl.multiple_of(start + step * size, 16), size)
            theirs = pl.ds(pl.multiple_of(other_start + step * size, 16), size)
            grad[xx, c, mine, :] = grad[xx, c, mine, :] + other[theirs, :]
            return carry

        if count == size:
            one(0, 0)
        else:
            lax.fori_loop(0, count // size, one, 0)

    def core_copy(granule):
        far, start, count, _ = GRANULES[granule]
        return remote(
            grad.at[nx if far else x, nc, pl.ds(start, count)],
            mate_buf.at[granule % 2, pl.ds(0, count)],
            sent.at[CORE], core_r.at[granule], mate,
        )

    def core_send(granule):
        core_copy(granule).start()

    def core_add(granule):
        far, start, count, units = GRANULES[granule]
        core_copy(granule).wait_recv()
        add_into(nx if far else x, start, count, mate_buf.at[granule % 2], 0)
        for unit in units:
            if unit in EARLY:
                (early_copy if far else outer_copy)(unit).start()
            elif far:
                x_copy(unit).start()

    def outer(unit):
        return (zb, z_pair) if unit in EARLY else (y, y_peer)

    def inner(unit):
        return (y, y_peer) if unit in EARLY else (zb, z_pair)

    def x_copy(unit):
        where = half_rows(unit, outer(unit)[0]) if unit in EARLY else pl.ds(*UNITS[unit])
        return remote(grad.at[nx, c, where], x_buf.at[where], sent.at[X_OUT], ex_r.at[unit], x_peer)

    def half_rows(unit, part):
        start, count = UNITS[unit]
        return pl.ds(pl.multiple_of(start + part * (count // 2), 32), count // 2)

    def share_rows(unit, part):
        start, count = UNITS[unit]
        return pl.ds(pl.multiple_of(start + outer(unit)[0] * (count // 2) + part * (count // 4), 16), count // 4)

    def half_slot(unit):
        return pl.ds(UNITS[unit][0] // 2, UNITS[unit][1] // 2)

    def share_slot(unit):
        return pl.ds(UNITS[unit][0] // 4, UNITS[unit][1] // 4)

    def outer_copy(unit):
        part, peer = outer(unit)
        return remote(
            grad.at[x, c, half_rows(unit, 1 - part)], y_buf.at[half_slot(unit)], sent.at[OUTER], ey_r.at[unit], peer
        )

    def early_slot(unit):
        count = UNITS[unit][1] // 2
        return pl.ds(EARLY.index(unit) * count, count)

    def early_copy(unit):
        index = EARLY.index(unit)
        part, peer = outer(unit)
        return remote(
            grad.at[nx, c, half_rows(unit, 1 - part)], early_buf.at[early_slot(unit)], sent.at[EARLY_OUT], early_r.at[index], peer
        )

    def inner_copy(unit):
        part, peer = inner(unit)
        return remote(
            grad.at[x, c, share_rows(unit, 1 - part)], z_buf.at[0, share_slot(unit)], sent.at[INNER], ez_r.at[unit], peer
        )

    def across_copy(unit):
        return remote(
            grad.at[x, c, share_rows(unit, inner(unit)[0])], z_buf.at[1, share_slot(unit)],
            sent.at[ACROSS], ew_r.at[unit], z_far,
        )

    def back_inner_copy(unit):
        part, peer = inner(unit)
        where = share_rows(unit, part)
        return remote(x_buf.at[where], x_buf.at[where], sent.at[BACK_INNER], fz_r.at[unit], peer)

    def back_outer_copy(unit):
        part, peer = outer(unit)
        where = half_rows(unit, part)
        return remote(x_buf.at[where], x_buf.at[where], sent.at[BACK_OUTER], fy_r.at[unit], peer)

    def early_x(unit):
        early_copy(unit).wait_recv()
        add_into(nx, half_rows(unit, outer(unit)[0]).start, UNITS[unit][1] // 2, early_buf, early_slot(unit).start)
        x_copy(unit).start()

    def early_y(unit):
        outer_copy(unit).wait_recv()
        add_into(x, half_rows(unit, outer(unit)[0]).start, UNITS[unit][1] // 2, y_buf, half_slot(unit).start)

    def early_z(unit):
        x_copy(unit).wait_recv()
        start = half_rows(unit, outer(unit)[0]).start
        add_into(x, start, UNITS[unit][1] // 2, x_buf, start)
        inner_copy(unit).start()

    def add_x(unit):
        x_copy(unit).wait_recv()
        start, count = UNITS[unit]
        add_into(x, start, count, x_buf, start)
        outer_copy(unit).start()

    def add_y(unit):
        outer_copy(unit).wait_recv()
        add_into(x, half_rows(unit, outer(unit)[0]).start, UNITS[unit][1] // 2, y_buf, half_slot(unit).start)
        inner_copy(unit).start()

    def add_z(unit):
        inner_copy(unit).wait_recv()
        start = share_rows(unit, inner(unit)[0]).start
        add_into(x, start, UNITS[unit][1] // 4, z_buf.at[0], share_slot(unit).start)
        across_copy(unit).start()

    def add_far(unit):
        across_copy(unit).wait_recv()
        where = share_rows(unit, inner(unit)[0])
        x_buf[where, :] = grad[x, c, where, :] + z_buf[1, share_slot(unit), :]
        back_inner_copy(unit).start()

    def give_y(unit):
        back_inner_copy(unit).wait_recv()
        back_outer_copy(unit).start()

    def out_copy(unit):
        where = pl.ds(*UNITS[unit])
        return pltpu.make_async_copy(x_buf.at[where], grads_out.at[where], local_sem.at[10])

    def finish(unit):
        back_outer_copy(unit).wait_recv()
        out_copy(unit).start()

    def sums_copy(slot, source, peer):
        return remote(sums_recv.at[6 + source], sums_recv.at[slot], sent.at[SUMS_OUT], sums_r.at[slot], peer)

    small_peers = [(i, i, peer) for i, peer in enumerate((mate, x_peer, y_peer, z_pair, z_far))]

    def sums_step(number):
        if number > 0:
            sums_copy(*small_peers[number - 1]).wait_recv()
            sums_recv[6 + number] = sums_recv[5 + number] + sums_recv[number - 1]
        else:
            sums_recv[6] = sums[...]
        if number < 5:
            sums_copy(*small_peers[number]).start()
        else:
            total = sums_recv[11]
            sums[...] = total
            own_up = sums[pl.ds(UPB + mp, 1), :]
            pairs = jnp.where(x == 0, total[:, :384], total[:, 384:])
            spread = jnp.where(placed, 1.0, 0.0)
            own_qv = lax.dot_general(
                pairs, spread, (((1,), (1,)), ((), ())), precision=lax.Precision.HIGHEST, preferred_element_type=F32
            )
            own_qv = jnp.concatenate([own_qv, jnp.zeros((16, width - own_qv.shape[1]), F32)], axis=1)
            total = jnp.where(tile_row == OWN_UP, own_up, total)
            total = jnp.where(tile_row == OWN_QV, own_qv[QUERYB : QUERYB + 1], total)
            sums[...] = jnp.where(tile_row == OWN_QV + 1, own_qv[VALUEB : VALUEB + 1], total)
            sums_out_copy.start()

    events = {
        BIAS_DONE: bias_done,
        MATE_DONE: mate_done,
        PASS_X: pass_x,
        PASS_Y: pass_y,
        PASS_DONE: pass_done,
        CORE_ADD: core_add,
        CORE_SEND: core_send,
        EARLY_X: early_x,
        EARLY_Y: early_y,
        EARLY_Z: early_z,
        ADD_X: add_x,
        ADD_Y: add_y,
        ADD_Z: add_z,
        ADD_FAR: add_far,
        GIVE_Y: give_y,
        FINISH: finish,
        SUMS: sums_step,
    }

    def run_due(due):
        for name, number in due:
            events[name](number)

    def due_now(step, plan):
        def among(low, high):
            if high - low == 1:
                run_due(plan[low])
                return
            middle = (low + high) // 2
            for first, last, here in ((low, middle, step < middle), (middle, high, step >= middle)):
                if any(plan[first:last]):
                    pl.when(here)(functools.partial(among, first, last))

        among(0, len(plan))

    lax.fori_loop(0, tokens // chunk, first_norm, 0)

    def forward_step(step, carry):
        due_now(step, PLAN_FORWARD)
        pl.when(step % 3 == 0)(lambda: project(step))
        pl.when(step % 3 > 0)(lambda: attend_forward(step))
        return carry

    lax.fori_loop(0, 18, forward_step, 0)
    lax.fori_loop(0, tokens // 256, second_norm, 0)
    sums[...] = jnp.zeros_like(sums)
    locals_[7].wait()

    def main_step(step, carry):
        due_now(step, PLAN_MAIN)
        pl.when(step < BETWEEN)(lambda: expert_tile(step))
        pl.when(step == BETWEEN)(between_norm)
        pl.when(step == BETWEEN + 1)(between_out)
        pl.when(step == BETWEEN + 2)(between_back)
        pl.when(jnp.logical_and(step >= FIRST_HEADS, step < LAST_NORM))(
            lambda: attend_backward(step - FIRST_HEADS)
        )
        pl.when(step >= LAST_NORM)(lambda: last_norm(step - LAST_NORM))
        return carry

    lax.fori_loop(0, LAST_NORM + tokens // 256, main_step, 0)
    run_due(PLAN_DRAIN)

    shard_rows = grad.shape[2]
    own = grad.at[0, 0]
    rows_sent = {
        TO_MATE: shard_rows, TO_X: shard_rows // 4, TO_Y: shard_rows // 4, TO_Z: shard_rows // 4,
        TO_CORNER: shard_rows // 4, FORWARD: shard_rows, BIAS: 3 * 16,
        EARLY_OUT: sum(UNITS[unit][1] for unit in EARLY) // 2,
        X_OUT: sum(count // 2 if unit in EARLY else count for unit, (_, count) in enumerate(UNITS)),
        OUTER: shard_rows // 2, INNER: shard_rows // 4, ACROSS: shard_rows // 4, BACK_INNER: shard_rows // 4,
        BACK_OUTER: shard_rows // 2,
    }
    for kind, count in rows_sent.items():
        all_rows = own.at[pl.ds(0, count)]
        remote(all_rows, all_rows, sent.at[kind], wb_r.at[0], mate).wait_send()
    remote(grad.at[0], grad.at[0], sent.at[CORE], wb_r.at[0], mate).wait_send()
    all_sums = sums_recv.at[pl.ds(0, 5)]
    remote(all_sums, all_sums, sent.at[SUMS_OUT], wb_r.at[0], mate).wait_send()
    mixed_copy.wait()
    input_copy.wait()
    sums_out_copy.wait()
    pltpu.make_async_copy(x_buf, grads_out, local_sem.at[10]).wait()


def tail_kernel(
    mixed_in, input_in, grads_in, sums_in,
    mixed_out, input_out, qkv_out, wout_out, up_out, down_out,
    qv_out, gain1_out, shift1_out, outb_out, gain2_out, shift2_out, downb_out, upb_out,
    mixed, inputs, grads, qkv, wout, up, down, sums_ref, qv_ref, in_sem, out_sem, small_sem, *vectors,
):
    tiles = down.shape[0]
    heads = qkv.shape[1]
    copies = [
        pltpu.make_async_copy(mixed_in, mixed, in_sem.at[0]),
        pltpu.make_async_copy(input_in, inputs, in_sem.at[1]),
    ]
    loads = []
    for index in range(tiles + 1):
        rows = pl.ds(index * 2 * UNIT, 2 * UNIT if index < tiles else 3 * UNIT)
        loads.append(pltpu.make_async_copy(grads_in.at[rows], grads.at[rows], in_sem.at[2 + index]))
    sums_copy = pltpu.make_async_copy(sums_in, sums_ref, small_sem.at[8])
    for copy in copies + loads + [sums_copy]:
        copy.start()
    stores = [
        pltpu.make_async_copy(mixed, mixed_out, out_sem.at[2 * tiles + 2]),
        pltpu.make_async_copy(inputs, input_out, out_sem.at[2 * tiles + 3]),
    ]
    for copy, store in zip(copies, stores):
        copy.wait()
        store.start()
    for index in range(tiles):
        loads[index].wait()
        start = index * 2 * UNIT
        down[index] = grads[start + UNIT : start + 2 * UNIT, :].astype(F32)
        stores.append(pltpu.make_async_copy(down.at[index], down_out.at[index], out_sem.at[2 * index]))
        stores[-1].start()
        lanes = pl.ds(index * UNIT, UNIT)
        up[:, lanes] = grads[start : start + UNIT, :].astype(F32).T
        stores.append(pltpu.make_async_copy(up.at[:, lanes], up_out.at[:, lanes], out_sem.at[2 * index + 1]))
        stores[-1].start()
    loads[tiles].wait()
    start = 2 * tiles * UNIT
    wout[...] = grads[start : start + heads * HEAD, :].astype(F32)
    stores.append(pltpu.make_async_copy(wout, wout_out, out_sem.at[2 * tiles]))
    stores[-1].start()
    start += heads * HEAD
    for head in range(heads):
        for part in range(3):
            row = start + (head * 3 + part) * HEAD
            qkv[part, head] = grads[row : row + HEAD, :].astype(F32)
    stores.append(pltpu.make_async_copy(qkv, qkv_out, out_sem.at[2 * tiles + 1]))
    stores[-1].start()
    sums_copy.wait()
    for index, (row, out) in enumerate((
        (GAIN1, gain1_out), (SHIFT1, shift1_out), (OUTB, outb_out), (GAIN2, gain2_out), (SHIFT2, shift2_out),
        (DOWNB, downb_out), (OWN_UP, upb_out),
    )):
        vectors[index][...] = sums_ref[row, :]
        stores.append(pltpu.make_async_copy(vectors[index], out, small_sem.at[index]))
        stores[-1].start()
    qv_ref[...] = sums_ref[OWN_QV : OWN_QV + 2, : qv_ref.shape[1]]
    stores.append(pltpu.make_async_copy(qv_ref, qv_out, small_sem.at[7]))
    stores[-1].start()
    for copy in stores:
        copy.wait()


def on_device(
    tokens, segment_ids, cotangent, norm1_gain, norm1_shift, w_qkv, qv_bias, w_out, out_bias,
    norm2_gain, norm2_shift, w_up, up_bias, w_down, down_bias,
):
    rows, seq, width = tokens.shape
    count = rows * seq
    shard = w_up.shape[1]
    heads = w_out.shape[0] // HEAD
    tiles = shard // UNIT
    units = 2 * tiles + 3
    qkv_rows = jnp.transpose(w_qkv, (1, 2, 0)).reshape(3, heads, HEAD, width)

    any_space = pl.BlockSpec(memory_space=pl.ANY)
    dma = pltpu.SemaphoreType.DMA
    vm = pltpu.VMEM
    mixed, input_grad, grads, sums = pl.pallas_call(
        functools.partial(kernel, rows=rows, seq=seq),
        out_shape=(
            jax.ShapeDtypeStruct((count, width), BF16),
            jax.ShapeDtypeStruct((count, width), BF16),
            jax.ShapeDtypeStruct((units * UNIT, width), BF16),
            jax.ShapeDtypeStruct((16, width), F32),
        ),
        in_specs=[any_space] * 15,
        out_specs=(any_space,) * 4,
        scratch_shapes=[
            vm((2, heads, 3, 2, HEAD, width), BF16),
            vm((2, heads, 2, HEAD, width), BF16),
            vm((2, 2, tiles, 2 * UNIT, width), BF16),
            vm((2, 2, 16, width), BF16),
            vm((2, 2, units * UNIT, width), BF16),
            vm((2, 2 * UNIT, width), BF16),
            vm((sum(UNITS[unit][1] for unit in EARLY) // 2, width), BF16),
            vm((units * UNIT, width), BF16),
            vm((units * UNIT // 2, width), BF16),
            vm((2, units * UNIT // 4, width), BF16),
            vm((count, width), BF16),
            vm((count, width), BF16),
            vm((count, width), BF16),
            vm((count, 2 * heads * 3 * 128), BF16),
            vm((count, width), BF16),
            vm((count, width), F32),
            vm((count, width), BF16),
            vm((count, width), BF16),
            vm((count, width), F32),
            vm((count, UNIT), BF16),
            vm((count, UNIT), BF16),
            vm((count, 128), F32),
            vm((count, 128), BF16),
            vm((count, 128), BF16),
            vm((16, width), F32),
            vm((12, 16, width), F32),
            vm((rows, seq), jnp.int32),
            *[vm((width,), BF16)] * 7,
            vm((2, heads * HEAD), BF16),
            dma((10,)),
            dma((11,)), dma((KINDS,)),
            *[dma((PIECES,))] * 6, dma((3,)),
            dma((len(GRANULES),)), dma((len(EARLY),)), *[dma((len(UNITS),))] * 6, dma((5,)),
        ],
        compiler_params=pltpu.CompilerParams(
            collective_id=0, has_side_effects=True, vmem_limit_bytes=64 * 2**20 - 2**16
        ),
    )(
        tokens.reshape(count, width), cotangent.reshape(count, width), segment_ids,
        norm1_gain, norm1_shift, out_bias, norm2_gain, norm2_shift, down_bias, up_bias, qv_bias,
        qkv_rows, w_out.reshape(heads, HEAD, width), w_up, w_down.reshape(tiles, UNIT, width),
    )

    groups = lax.axis_size("dp") // 8
    if groups > 1:
        grads, sums = lax.psum((grads.astype(F32) * 0.125, sums * 0.125), "dp")
    whole = [jax.ShapeDtypeStruct((width,), F32)] * 7
    results = pl.pallas_call(
        tail_kernel,
        out_shape=(
            mixed, input_grad,
            jax.ShapeDtypeStruct((3, heads, HEAD, width), F32), jax.ShapeDtypeStruct((heads * HEAD, width), F32),
            jax.ShapeDtypeStruct((width, shard), F32), jax.ShapeDtypeStruct((tiles, UNIT, width), F32),
            jax.ShapeDtypeStruct((2, heads * HEAD), F32), *whole,
        ),
        in_specs=[any_space] * 4,
        out_specs=(any_space,) * 14,
        scratch_shapes=[
            vm((count, width), BF16), vm((count, width), BF16), vm(grads.shape, grads.dtype),
            vm((3, heads, HEAD, width), F32), vm((heads * HEAD, width), F32),
            vm((width, shard), F32), vm((tiles, UNIT, width), F32),
            vm((16, width), F32), vm((2, heads * HEAD), F32),
            dma((2 + tiles + 1,)), dma((2 * tiles + 4,)), dma((9,)),
            *[vm((width,), F32)] * 7,
        ],
        compiler_params=pltpu.CompilerParams(vmem_limit_bytes=63 * 2**20),
    )(mixed, input_grad, grads, sums)
    mixed, input_grad, grad_qkv, grad_out, grad_up, grad_down, grad_qv, *vectors = results
    gain1, shift1, outb, gain2, shift2, downb, upb = vectors
    return (
        mixed.reshape(rows, seq, width),
        input_grad.reshape(rows, seq, width),
        gain1,
        shift1,
        jnp.transpose(grad_qkv.reshape(3, heads * HEAD, width), (2, 0, 1)),
        grad_qv,
        grad_out,
        outb,
        gain2,
        shift2,
        grad_up,
        upb,
        grad_down.reshape(shard, width),
        downb,
    )


def solution(mesh):
    tall = P(("dp", "mp"), None, None)
    return jax.shard_map(
        on_device,
        mesh=mesh,
        in_specs=(
            tall, P(("dp", "mp"), None), tall, P(), P(), P(None, None, "mp"), P(None, "mp"), P("mp", None),
            P(), P(), P(), P(None, "mp"), P("mp"), P("mp", None), P(),
        ),
        out_specs=(
            tall, tall, P(), P(), P(None, None, "mp"), P(None, "mp"), P("mp", None), P(), P(), P(),
            P(None, "mp"), P("mp"), P("mp", None), P(),
        ),
        check_vma=False,
    )
```

```python
import functools

import jax
import jax.numpy as jnp
from jax import lax
from jax.experimental import pallas as pl
from jax.experimental.pallas import tpu as pltpu
from jax.sharding import PartitionSpec as P

HEAD = 64
EPS = 1e-06
MASKED = -1e30
UNIT = 256
SPLIT = 4
INV_LANE = 32
OWN_UP, OWN_QV = 12, 13
F32, BF16 = jnp.float32, jnp.bfloat16

GAIN1, SHIFT1, OUTB, GAIN2, SHIFT2, DOWNB, QUERYB, VALUEB, UPB = range(9)

KINDS = 16
(
    TO_MATE, TO_X, TO_Y, TO_Z, TO_CORNER, FORWARD, BIAS, CORE, EARLY_OUT, X_OUT, OUTER, INNER, ACROSS, BACK_INNER,
    BACK_OUTER, SUMS_OUT,
) = range(KINDS)

UNITS = (
    (0, 128),
    (128, 128),
    (256, 128),
    (384, 128),
    (512, 128),
    (640, 128),
    (768, 128),
    (896, 128),
    (1024, 128),
    (1152, 128),
    (1280, 128),
    (1408, 128),
    (1536, 192),
    (1728, 128),
    (1856, 64),
    (1920, 128),
    (2048, 64),
    (2112, 64),
    (2176, 64),
    (2240, 64),
)
GRANULES = (
    (0, 0, 512, (0, 1, 2, 3)),
    (1, 0, 512, (0, 1, 2, 3)),
    (0, 512, 512, (4, 5, 6, 7)),
    (1, 512, 512, (4, 5, 6, 7)),
    (0, 1024, 512, (8, 9, 10, 11)),
    (1, 1024, 512, (8, 9, 10, 11)),
    (1, 1536, 192, (12,)),
    (0, 1536, 192, (12,)),
    (1, 1728, 192, (13, 14)),
    (1, 1920, 192, (15, 16)),
    (1, 2112, 192, (17, 18, 19)),
    (0, 1728, 192, (13, 14)),
    (0, 1920, 192, (15, 16)),
    (0, 2112, 192, (17, 18, 19)),
)
EARLY = (3, 5, 6, 7)
PIECES, AHEAD = 10, 3
FAR_PAIRS = (0, 1, 0, 1, 0, 1)
PAIR_TILES = (0, 0, 1, 1, 2, 2)
BETWEEN, FIRST_HEADS, LAST_NORM, MIX = 12, 15, 33, 37
(
    BIAS_DONE, MATE_DONE, PASS_X, PASS_Y, PASS_DONE, CORE_ADD, CORE_SEND, EARLY_X, EARLY_Y, EARLY_Z,
    ADD_X, ADD_Y, ADD_Z, ADD_FAR, GIVE_Y, FINISH, SUMS,
) = range(17)
PLAN_FORWARD = (
    ((MATE_DONE, 0), (BIAS_DONE, 0),),
    ((PASS_X, 0),),
    (),
    ((PASS_X, 1), (MATE_DONE, 1),),
    ((PASS_X, 2),),
    (),
    ((PASS_X, 3), (MATE_DONE, 2),),
    ((PASS_Y, 0),),
    ((PASS_X, 4),),
    ((PASS_DONE, 0), (BIAS_DONE, 1), (BIAS_DONE, 2),),
    ((PASS_X, 5), (PASS_Y, 1),),
    (),
    ((PASS_X, 6), (PASS_DONE, 1),),
    ((PASS_Y, 2),),
    ((PASS_X, 7),),
    ((PASS_DONE, 2),),
    ((PASS_X, 8),),
    ((PASS_Y, 3),),
)
PLAN_SECOND = (
    ((PASS_X, 9), (MATE_DONE, 3), (PASS_DONE, 3),),
    (),
    ((PASS_Y, 4),),
    (),
)
PLAN_MAIN = (
    ((MATE_DONE, 4), (MATE_DONE, 5),),
    ((PASS_Y, 5), (CORE_SEND, 0),),
    ((PASS_DONE, 4), (PASS_DONE, 5),),
    ((PASS_Y, 6), (CORE_ADD, 0), (CORE_SEND, 1),),
    ((PASS_Y, 7), (MATE_DONE, 6), (MATE_DONE, 7),),
    ((CORE_ADD, 1), (CORE_SEND, 2),),
    ((PASS_Y, 8), (PASS_DONE, 6), (PASS_DONE, 7),),
    ((PASS_Y, 9), (CORE_ADD, 2), (CORE_SEND, 3), (EARLY_Y, 3), (ADD_X, 0),),
    ((EARLY_X, 3), (MATE_DONE, 8), (MATE_DONE, 9),),
    ((ADD_X, 1), (CORE_ADD, 3), (CORE_SEND, 4), (ADD_Y, 0), (EARLY_Y, 5), (EARLY_Y, 6),),
    ((ADD_X, 2), (EARLY_Y, 7), (PASS_DONE, 8), (PASS_DONE, 9),),
    ((EARLY_Z, 3), (CORE_ADD, 4), (CORE_SEND, 5), (ADD_Y, 1), (EARLY_X, 5), (EARLY_X, 6),),
    ((ADD_X, 4), (ADD_Y, 2), (EARLY_X, 7), (CORE_ADD, 5), (ADD_Z, 0), (ADD_Z, 3),),
    ((EARLY_Z, 5), (EARLY_Z, 6), (ADD_Z, 1), (ADD_Z, 2), (ADD_Y, 4),),
    ((EARLY_Z, 7), (CORE_SEND, 6), (ADD_FAR, 0),),
    ((CORE_ADD, 6), (CORE_SEND, 7), (ADD_FAR, 3), (ADD_Z, 5), (ADD_Z, 6),),
    ((ADD_X, 8), (GIVE_Y, 0), (CORE_ADD, 7), (ADD_FAR, 1), (ADD_Z, 4), (ADD_Z, 7),),
    ((GIVE_Y, 3), (ADD_FAR, 2), (ADD_X, 9),),
    ((CORE_SEND, 8), (GIVE_Y, 1), (ADD_FAR, 5),),
    ((CORE_ADD, 8), (ADD_Y, 8), (FINISH, 0), (ADD_FAR, 6),),
    ((ADD_X, 10), (ADD_Y, 9), (GIVE_Y, 2), (FINISH, 3), (ADD_FAR, 4),),
    ((CORE_SEND, 9), (ADD_FAR, 7), (ADD_Z, 8),),
    ((ADD_X, 11), (GIVE_Y, 5), (CORE_ADD, 9), (GIVE_Y, 6), (FINISH, 1), (ADD_Z, 9),),
    ((GIVE_Y, 4), (ADD_Y, 10),),
    ((CORE_SEND, 10), (ADD_FAR, 8),),
    ((ADD_X, 12), (GIVE_Y, 7), (CORE_ADD, 10), (FINISH, 2), (FINISH, 5), (FINISH, 6), (ADD_FAR, 9),),
    ((ADD_Y, 11), (ADD_Z, 10),),
    ((CORE_SEND, 11), (GIVE_Y, 8), (FINISH, 4),),
    ((CORE_ADD, 11), (ADD_X, 13), (ADD_X, 14), (FINISH, 7),),
    ((GIVE_Y, 9), (ADD_Y, 12), (ADD_FAR, 10), (ADD_Z, 11),),
    ((CORE_SEND, 12), (FINISH, 8),),
    ((CORE_ADD, 12), (ADD_X, 15), (ADD_X, 16), (ADD_Y, 13), (ADD_Y, 14), (ADD_Z, 12),),
    ((GIVE_Y, 10), (FINISH, 9), (ADD_FAR, 11),),
    ((CORE_SEND, 13), (ADD_Z, 13),),
    ((ADD_Y, 15), (ADD_Y, 16), (CORE_ADD, 13), (ADD_X, 17), (ADD_X, 18), (ADD_X, 19), (ADD_Z, 14),),
    ((GIVE_Y, 11), (FINISH, 10), (ADD_FAR, 12),),
    ((ADD_Y, 17), (ADD_FAR, 13), (ADD_Z, 15), (ADD_Z, 16),),
    ((SUMS, 0), (GIVE_Y, 12), (ADD_Y, 18), (ADD_Y, 19), (ADD_FAR, 14), (ADD_Z, 17),),
    ((SUMS, 1), (GIVE_Y, 13), (FINISH, 11), (ADD_FAR, 15),),
    ((GIVE_Y, 14), (ADD_FAR, 16), (ADD_Z, 18), (ADD_Z, 19), (SUMS, 2), (FINISH, 12), (ADD_FAR, 17),),
    ((GIVE_Y, 15),),
)
PLAN_DRAIN = (
    (SUMS, 3),
    (GIVE_Y, 16),
    (FINISH, 13),
    (FINISH, 14),
    (ADD_FAR, 18),
    (GIVE_Y, 17),
    (ADD_FAR, 19),
    (SUMS, 4),
    (FINISH, 15),
    (GIVE_Y, 18),
    (FINISH, 16),
    (GIVE_Y, 19),
    (FINISH, 17),
    (SUMS, 5),
    (FINISH, 18),
    (FINISH, 19),
)

def dot(left, right, left_dim, right_dim):
    return lax.dot_general(
        left, right, (((left_dim,), (right_dim,)), ((), ())), preferred_element_type=F32
    )


def column_sum(values):
    return jnp.sum(values, axis=0, keepdims=True)


def gelu_parts(pre):
    cumul = 0.5 + 0.5 * lax.erf(pre * 0.7071067811865476)
    return cumul, jnp.exp(-0.5 * pre * pre) * 0.3989422804014327


def kernel(
    x_in, g_in, seg_in, gain1_in, shift1_in, outb_in, gain2_in, shift2_in, downb_in, upb_in, qvb_in,
    qkv_in, out_in, up_in, down_in,
    mixed_out, input_out, grads_out, sums_out, hid_out,
    wq, wo, wm, wb, grad, mate_buf, early_buf, x_buf, y_buf, z_buf,
    x_ref, g_ref, a1_ref, proj_ref, o_ref, x1_ref, hat2_ref, a2_ref, da2_ref,
    hid_ref, low_ref, lse_ref, aug_q, aug_k, sums, sums_recv,
    seg_ref, gain1_ref, shift1_ref, outb_ref, gain2_ref, shift2_ref, downb_ref, upb_ref, qvb_ref, small_sem,
    local_sem, spill_sem, fetch_sem, sent, wm_r, wx_r, wy_r, wz_r, wd_r, wf_r, wb_r,
    core_r, early_r, ex_r, ey_r, ez_r, ew_r, fz_r, fy_r, sums_r,
    *, rows, seq,
):
    tokens, width = x_ref.shape
    dp, mp = lax.axis_index("dp"), lax.axis_index("mp")
    c, x = mp % 2, mp // 2
    y, z = dp % 2, (dp // 2) % 4
    block = dp - dp % 8
    zb = z % 2
    nx, nc, ny = 1 - x, 1 - c, 1 - y

    def device(zz, yy, xx, cc):
        return (block + zz * 2 + yy, xx * 2 + cc)

    mate = device(z, y, x, nc)
    x_peer = device(z, y, nx, c)
    y_peer = device(z, ny, x, c)
    z_far = device((z + 2) % 4, y, x, c)
    z_pair = device(z + 1 - 2 * zb, y, x, c)
    cross = device(z, y, nx, nc)
    corner = device(z + 1 - 2 * zb, ny, x, c)

    def remote(src, dst, send, recv, where):
        return pltpu.make_async_remote_copy(
            src_ref=src, dst_ref=dst, send_sem=send, recv_sem=recv,
            device_id=where, device_id_type=pl.DeviceIdType.MESH,
        )

    barrier = pltpu.get_barrier_semaphore()
    everyone = [mate, x_peer, cross, y_peer, z_pair, z_far, corner]
    for peer in everyone:
        pl.semaphore_signal(barrier, inc=1, device_id=peer, device_id_type=pl.DeviceIdType.MESH)

    up_stage = grad.at[0, 0, pl.ds(0, width)]
    locals_ = [
        pltpu.make_async_copy(qkv_in.at[:, 0], wq.at[x, 0, :, c], local_sem.at[0]),
        pltpu.make_async_copy(qkv_in.at[:, 1], wq.at[x, 1, :, c], local_sem.at[1]),
        pltpu.make_async_copy(qkv_in.at[:, 2], wq.at[x, 2, :, c], local_sem.at[2]),
        pltpu.make_async_copy(x_in, x_ref, local_sem.at[3]),
        pltpu.make_async_copy(out_in, wo.at[x, :, c], local_sem.at[4]),
        pltpu.make_async_copy(up_in, up_stage, local_sem.at[5]),
        pltpu.make_async_copy(down_in, wm.at[x, c, :, pl.ds(UNIT, UNIT)], local_sem.at[6]),
        pltpu.make_async_copy(g_in, g_ref, local_sem.at[7]),
    ]
    small_copies = [
        pltpu.make_async_copy(src, dst, small_sem.at[i])
        for i, (src, dst) in enumerate((
            (seg_in, seg_ref), (upb_in, upb_ref), (qvb_in, qvb_ref), (gain1_in, gain1_ref), (shift1_in, shift1_ref),
            (outb_in, outb_ref), (gain2_in, gain2_ref), (shift2_in, shift2_ref), (downb_in, downb_ref),
        ))
    ]
    for copy in small_copies + locals_:
        copy.start()
    for copy in small_copies:
        copy.wait()

    from_lane = lax.broadcasted_iota(jnp.int32, (qvb_ref.shape[1], 384), 0)
    to_lane = lax.broadcasted_iota(jnp.int32, (qvb_ref.shape[1], 384), 1)
    placed = jnp.logical_and(
        from_lane == (to_lane // 128) * 64 + to_lane % 64, (to_lane // 64) % 2 == c
    )
    place = jnp.where(placed, 1.0, 0.0).astype(BF16)
    qv_rows = dot(qvb_ref[...], place, 1, 0)
    qv_rows = jnp.concatenate([qv_rows, jnp.zeros((2, width - 384), F32)], axis=1)
    tile_row = lax.broadcasted_iota(jnp.int32, (16, width), 0)
    wb[x, c] = jnp.where(
        tile_row == 0,
        upb_ref[...].astype(F32).reshape(1, width),
        jnp.where(tile_row == 1, qv_rows[0:1], jnp.where(tile_row == 2, qv_rows[1:2], 0.0)),
    ).astype(BF16)
    lane = lax.broadcasted_iota(jnp.int32, (seq, 128), 1)
    for row in range(rows):
        ids = jnp.broadcast_to(seg_ref[row : row + 1, :].astype(F32), (128, seq)).T
        spot = lane % 64
        same = spot == ids.astype(jnp.int32)
        inside = spot < 32
        where = pl.ds(row * seq, seq)
        aug_q[where, :] = jnp.where(same, 1.0, 0.0).astype(BF16)
        aug_k[where, :] = jnp.where(jnp.logical_and(inside, jnp.logical_not(same)), MASKED, 0.0).astype(BF16)
    lse_ref[...] = jnp.zeros_like(lse_ref)
    for number in (0, 1, 2, 4):
        locals_[number].wait()
    pl.semaphore_wait(barrier, len(everyone))

    def piece(kind, index, xx, cc, part=None):
        if kind == "q":
            return wq.at[xx, index, :, cc, some(HEAD, part)]
        if kind == "o":
            return wo.at[xx, :, cc, some(HEAD, part)]
        return wm.at[xx, cc, index // 2, some(UNIT, part, (index % 2) * UNIT)]

    def some(count, part, start=0):
        if part is None:
            return pl.ds(start, count)
        return pl.ds(pl.multiple_of(start + part * (count // 4), 16), count // 4)

    quarter = y * 2 + zb

    def kinds(number, run):
        run("q" if number < 3 else "o" if number == 3 else "m", number - 4 if number > 3 else number)

    def to_mate(number, kind, index):
        own = piece(kind, index, x, c)
        return remote(own, own, sent.at[TO_MATE], wm_r.at[number], mate)

    def to_x(number, kind, index):
        own = piece(kind, index, x, c, quarter)
        return remote(own, own, sent.at[TO_X], wx_r.at[number], x_peer)

    def to_square(number, kind, index):
        held = piece(kind, index, nx, c, quarter)
        return [
            remote(held, held, sent.at[send], recv.at[number], peer)
            for send, recv, peer in ((TO_Y, wy_r, y_peer), (TO_Z, wz_r, z_pair), (TO_CORNER, wd_r, corner))
        ]

    def forward(number, kind, index):
        held = piece(kind, index, nx, c)
        return remote(held, held, sent.at[FORWARD], wf_r.at[number], mate)

    def mate_done(number):
        kinds(number, lambda kind, index: to_mate(number, kind, index).wait_recv())

    def start_x(number):
        kinds(number, lambda kind, index: to_x(number, kind, index).start())

    def pass_x(number):
        def run(kind, index):
            to_x(number, kind, index).wait_recv()
            for copy in to_square(number, kind, index):
                copy.start()

        kinds(number, run)
        if number + AHEAD < PIECES:
            start_x(number + AHEAD)

    def pass_y(number):
        def run(kind, index):
            for copy in to_square(number, kind, index):
                copy.wait_recv()
            forward(number, kind, index).start()

        kinds(number, run)

    def bias_done(number):
        biases[number].wait_recv()

    def pass_done(number):
        kinds(number, lambda kind, index: forward(number, kind, index).wait_recv())

    biases = [
        remote(wb.at[x, c], wb.at[x, c], sent.at[BIAS], wb_r.at[i], peer)
        for i, peer in enumerate((mate, x_peer, cross))
    ]
    for copy in biases:
        copy.start()
    for number in range(AHEAD):
        start_x(number)
        if number < 3:
            kinds(number, lambda kind, index: to_mate(number, kind, index).start())
    for number in range(min(AHEAD, 3), 4):
        kinds(number, lambda kind, index: to_mate(number, kind, index).start())
    locals_[5].wait()
    locals_[6].wait()
    tiles = up_stage.shape[1] // UNIT
    for index in range(tiles):
        wm[x, c, index, pl.ds(0, UNIT), :] = up_stage[:, index * UNIT : (index + 1) * UNIT].T
    for number in range(4, PIECES):
        kinds(number, lambda kind, index: to_mate(number, kind, index).start())

    chunk = 128
    locals_[3].wait()
    small_refs = (gain1_ref, shift1_ref, outb_ref, gain2_ref, shift2_ref, downb_ref)

    def small(row):
        return small_refs[row][...].astype(F32).reshape(1, width)

    def norm(values):
        centred = values - jnp.mean(values, axis=-1, keepdims=True)
        inv = lax.rsqrt(jnp.mean(centred * centred, axis=-1, keepdims=True) + EPS)
        return centred * inv, inv

    def at_chunk(step):
        return pl.ds(pl.multiple_of(step * chunk, chunk), chunk)

    def first_norm(step, carry):
        where = at_chunk(step)
        hat, _ = norm(x_ref[where, :].astype(F32))
        a1_ref[where, :] = (small(0) * hat + small(1)).astype(BF16)
        return carry

    even = lane < 64

    def pick(values, others):
        return jnp.where(even, values, others), jnp.where(even, others, values)

    def part_lanes(group, part, count=1):
        return pl.ds(pl.multiple_of(group * 384 + part * 128, 128), count * 128)

    def project(step):
        xx, t = jnp.where(step < 9, x, nx), (step // 3) % 3
        group = xx * 3 + t
        weights = wq[xx, t].reshape(3 * 128, width)
        biasq = wb[xx, 0, 1:2, :].astype(F32) + wb[xx, 1, 1:2, :].astype(F32)
        biasv = wb[xx, 0, 2:3, :].astype(F32) + wb[xx, 1, 2:3, :].astype(F32)
        pq = jnp.where(t == 0, biasq[:, :128], jnp.where(t == 1, biasq[:, 128:256], biasq[:, 256:384]))
        pv = jnp.where(t == 0, biasv[:, :128], jnp.where(t == 1, biasv[:, 128:256], biasv[:, 256:384]))
        for row in range(rows):
            where = pl.ds(row * seq, seq)
            value = dot(a1_ref[where, :], weights, 1, 1)
            proj_ref[where, part_lanes(group, 0)] = ((value[:, :128] + pq).astype(BF16) * 0.125).astype(BF16)
            proj_ref[where, part_lanes(group, 1)] = value[:, 128:256].astype(BF16)
            proj_ref[where, part_lanes(group, 2)] = (value[:, 256:] + pv).astype(BF16)

    def attend_forward(step):
        xx, t = jnp.where(step < 9, x, nx), (step // 3) % 3
        group = xx * 3 + t
        row = step % 3 - 1
        where = pl.ds(pl.multiple_of(row * seq, seq), seq)
        qs = pick(proj_ref[where, part_lanes(group, 0)], aug_q[where, :])
        ks = pick(proj_ref[where, part_lanes(group, 1)], aug_k[where, :])
        vs = pick(proj_ref[where, part_lanes(group, 2)], jnp.ones((seq, 128), BF16))
        scores = [dot(q, k, 1, 1) for q, k in zip(qs, ks)]
        highest = [jnp.max(item, axis=-1, keepdims=True) for item in scores]
        result = [
            dot(jnp.exp(item - top).astype(BF16), v, 1, 0) for item, top, v in zip(scores, highest, vs)
        ]
        total = pltpu.roll(jnp.where(even, result[1], result[0]), 64, 1)
        mixed = jnp.where(even, result[0], result[1]) / total
        o_ref[where, pl.ds(pl.multiple_of(group * 128, 128), 128)] = mixed.astype(BF16)
        log_total = jnp.where(even, highest[0], highest[1]) + jnp.log(total)
        lse_ref[where, :] = jnp.where(lane % 64 == group, log_total, lse_ref[where, :])

    def second_norm(step, carry):
        due_now(step, PLAN_SECOND)
        where = pl.ds(pl.multiple_of(step * 256, 256), 256)
        value = x_ref[where, :].astype(F32) + dot(o_ref[where, :], wo[...].reshape(width, width), 1, 0) + small(2)
        hat, inv = norm(value)
        hat2_ref[where, :] = hat.astype(BF16)
        spot = lax.broadcasted_iota(jnp.int32, (256, 128), 1)
        lse_ref[where, :] = jnp.where(spot == INV_LANE, inv, lse_ref[where, :])
        a2_ref[where, :] = (small(3) * hat + small(4)).astype(BF16)
        x1_ref[where, :] = value + small(5)
        da2_ref[where, :] = jnp.zeros_like(value)
        return carry

    def pair_place(pair):
        far = sum(jnp.where(pair == p, 1, 0) for p, flag in enumerate(FAR_PAIRS) if flag)
        tile = sum(jnp.where(pair == p, index, 0) for p, index in enumerate(PAIR_TILES))
        return jnp.where(far == 1, nx, x), tile

    def spill(step):
        return pltpu.make_async_copy(hid_ref.at[step % 2], hid_out.at[step], spill_sem.at[step % 2])

    def fetch(tile):
        if tile < 9:
            place = proj_ref.at[:, pl.ds(tile * UNIT, UNIT)]
        else:
            place = a1_ref.at[:, pl.ds((tile - 9) * UNIT, UNIT)]
        return pltpu.make_async_copy(hid_out.at[tile], place, fetch_sem.at[tile])

    def expert_tile(step):
        slot = step % 2
        pl.when(step >= 2)(lambda: spill(step - 2).wait())
        xx, index = pair_place(step // 2)
        cc = jnp.where(step % 2 == 0, nc, c)
        w_up = wm[xx, cc, index, pl.ds(0, UNIT), :]
        w_down = wm[xx, cc, index, pl.ds(UNIT, UNIT), :]
        lanes = pl.ds(pl.multiple_of(index * UNIT, UNIT), UNIT)
        bias = wb[xx, cc, 0:1, lanes].astype(F32)
        upb_sum = None
        part_rows = tokens // SPLIT
        for part in range(SPLIT):
            where = pl.ds(part * part_rows, part_rows)
            pre = dot(a2_ref[where, :], w_up, 1, 1) + bias
            back = dot(g_ref[where, :], w_down, 1, 1)
            cumul, density = gelu_parts(pre)
            hidden = (pre * cumul).astype(BF16)
            low = (back * (cumul + pre * density)).astype(BF16)
            hid_ref[slot, where, :] = hidden
            low_ref[where, :] = low
            one = column_sum(low.astype(F32))
            upb_sum = one if upb_sum is None else upb_sum + one
        sums[pl.ds(UPB + xx * 2 + cc, 1), lanes] = upb_sum
        base = pl.multiple_of(index * 2 * UNIT, UNIT)
        grad[xx, cc, pl.ds(base, UNIT), :] = dot(low_ref[...], a2_ref[...], 0, 0).astype(BF16)
        grad[xx, cc, pl.ds(base + UNIT, UNIT), :] = dot(hid_ref[slot], g_ref[...], 0, 0).astype(BF16)
        spill(step).start()
        da2_ref[...] += dot(low_ref[...], w_up, 1, 0)

    def norm_back(grad_in, hat, inv, gain):
        scaled = grad_in * gain
        return inv * (
            scaled
            - jnp.mean(scaled, axis=-1, keepdims=True)
            - hat * jnp.mean(scaled * hat, axis=-1, keepdims=True)
        )

    def add_sum(row, values):
        sums[row : row + 1, :] += column_sum(values)

    heads_rows = 6 * UNIT

    def between_norm():
        def one(step, carry):
            where = at_chunk(step)
            da2, hat = da2_ref[where, :], hat2_ref[where, :].astype(F32)
            top = g_ref[where, :].astype(F32)
            add_sum(GAIN2, da2 * hat)
            add_sum(SHIFT2, da2)
            add_sum(DOWNB, top)
            middle = top + norm_back(da2, hat, lse_ref[where, INV_LANE : INV_LANE + 1], small(3))
            da2_ref[where, :] = middle
            low = middle.astype(BF16)
            add_sum(OUTB, low.astype(F32))
            a2_ref[where, :] = low
            return carry

        lax.fori_loop(0, tokens // chunk, one, 0)
        for tile in (10, 11):
            spill(tile).wait()

    def between_out():
        for xx in range(2):
            half = dot(o_ref[:, xx * 384 : (xx + 1) * 384], a2_ref[...], 0, 0).astype(BF16)
            for t in range(3):
                for cc in range(2):
                    start = (t * 2 + cc) * 64
                    grad[xx, cc, pl.ds(heads_rows + t * 64, 64), :] = half[start : start + 64]

    def between_back():
        def back(step, carry):
            where = pl.ds(pl.multiple_of(step * 256, 256), 256)
            a2_ref[where, :] = dot(a2_ref[where, :], wo[...].reshape(width, width), 1, 1).astype(BF16)
            return carry

        lax.fori_loop(0, tokens // 256, back, 0)

    def attend_backward(step):
        xx, t = jnp.where(step < 9, nx, x), (step // 3) % 3
        group = xx * 3 + t
        lanes = pl.ds(pl.multiple_of(group * 128, 128), 128)

        def one_row():
            where = pl.ds(pl.multiple_of((step % 3) * seq, seq), seq)
            query, key, value = (proj_ref[where, part_lanes(group, i)] for i in range(3))
            out, back = o_ref[where, lanes], a2_ref[where, lanes]
            none = jnp.zeros((seq, 128), BF16)
            product = out.astype(F32) * back.astype(F32)
            log_total = lse_ref[where, :]
            tops = [
                jnp.sum(jnp.where(lane == group + shift, log_total, 0.0), axis=-1, keepdims=True)
                for shift in (0, 64)
            ]
            deltas = [jnp.sum(item, axis=-1, keepdims=True) for item in pick(product, jnp.zeros_like(product))]
            q_aug, k_aug = pick(query, aug_q[where, :]), pick(key, aug_k[where, :])
            q_own, k_own, b_own = pick(query, none), pick(key, none), pick(back, none)
            v_own = pick(value, none)
            d_query = d_key = d_value = None
            for i in range(2):
                prob = jnp.exp(dot(q_aug[i], k_aug[i], 1, 1) - tops[i])
                low = prob.astype(BF16)
                inner = dot(b_own[i], v_own[i], 1, 1) - deltas[i]
                d_score = (prob * inner).astype(BF16)
                parts = (dot(d_score, k_own[i], 1, 0), dot(d_score, q_own[i], 0, 0), dot(low, b_own[i], 0, 0))
                if i == 0:
                    d_query, d_key, d_value = parts
                else:
                    d_query, d_key, d_value = d_query + parts[0], d_key + parts[1], d_value + parts[2]
            low_query = (d_query * 0.125).astype(BF16)
            low_value = d_value.astype(BF16)
            proj_ref[where, part_lanes(group, 0)] = low_query
            proj_ref[where, part_lanes(group, 1)] = d_key.astype(BF16)
            proj_ref[where, part_lanes(group, 2)] = low_value
            sums[QUERYB : QUERYB + 1, lanes] += column_sum(low_query.astype(F32))
            sums[VALUEB : VALUEB + 1, lanes] += column_sum(low_value.astype(F32))

        def weights():
            weight_grad = dot(proj_ref[:, part_lanes(group, 0, 3)], a1_ref[...], 0, 0).astype(BF16)
            for part in range(3):
                for cc in range(2):
                    start = part * 128 + cc * 64
                    place = pl.multiple_of(heads_rows + 192 + t * 192 + part * 64, 64)
                    grad[xx, cc, pl.ds(place, 64), :] = weight_grad[start : start + 64]
        pl.when(step % 3 < 2)(one_row)
        pl.when(step % 3 == 2)(weights)

    def last_norm(step):
        where = pl.ds(pl.multiple_of(step * 256, 256), 256)
        hat, inv = norm(x_ref[where, :].astype(F32))
        da1 = dot(proj_ref[where, :], wq[...].reshape(3 * width, width), 1, 0)
        add_sum(GAIN1, da1 * hat)
        add_sum(SHIFT1, da1)
        g_ref[where, :] = (da2_ref[where, :] + norm_back(da1, hat, inv, small(0))).astype(BF16)
        pl.when(step == tokens // 256 - 1)(lambda: input_copy.start())

    def mix(step):
        @pl.when(step == 0)
        def _():
            for tile in range(12):
                fetch(tile).start()
            for tile in range(12):
                fetch(tile).wait()

        where = pl.ds(pl.multiple_of(step * 256, 256), 256)
        total = x1_ref[where, :]
        for tile in range(12):
            hidden = proj_ref[where, pl.ds(tile * UNIT, UNIT)] if tile < 9 else a1_ref[where, pl.ds((tile - 9) * UNIT, UNIT)]
            xx = nx if FAR_PAIRS[tile // 2] else x
            cc = c if tile % 2 else nc
            total += dot(hidden, wm[xx, cc, PAIR_TILES[tile // 2], pl.ds(UNIT, UNIT), :], 1, 0)
        hat2_ref[where, :] = total.astype(BF16)
        pl.when(step == tokens // 256 - 1)(lambda: mixed_copy.start())

    sums_out_copy = pltpu.make_async_copy(sums, sums_out, small_sem.at[9])
    mixed_copy = pltpu.make_async_copy(hat2_ref, mixed_out, local_sem.at[8])
    input_copy = pltpu.make_async_copy(g_ref, input_out, local_sem.at[9])

    def add_into(xx, start, count, other, other_start):
        size = next(size for size in (64, 48, 32, 16) if count % size == 0)

        def one(step, carry):
            mine = pl.ds(pl.multiple_of(start + step * size, 16), size)
            theirs = pl.ds(pl.multiple_of(other_start + step * size, 16), size)
            grad[xx, c, mine, :] = grad[xx, c, mine, :] + other[theirs, :]
            return carry

        if count == size:
            one(0, 0)
        else:
            lax.fori_loop(0, count // size, one, 0)

    def core_copy(granule):
        far, start, count, _ = GRANULES[granule]
        return remote(
            grad.at[nx if far else x, nc, pl.ds(start, count)],
            mate_buf.at[granule % 2, pl.ds(0, count)],
            sent.at[CORE], core_r.at[granule], mate,
        )

    def core_send(granule):
        core_copy(granule).start()

    def core_add(granule):
        far, start, count, units = GRANULES[granule]
        core_copy(granule).wait_recv()
        add_into(nx if far else x, start, count, mate_buf.at[granule % 2], 0)
        for unit in units:
            if unit in EARLY:
                (early_copy if far else outer_copy)(unit).start()
            elif far:
                x_copy(unit).start()

    def outer(unit):
        return (zb, z_pair) if unit in EARLY else (y, y_peer)

    def inner(unit):
        return (y, y_peer) if unit in EARLY else (zb, z_pair)

    def x_copy(unit):
        where = half_rows(unit, outer(unit)[0]) if unit in EARLY else pl.ds(*UNITS[unit])
        return remote(grad.at[nx, c, where], x_buf.at[where], sent.at[X_OUT], ex_r.at[unit], x_peer)

    def half_rows(unit, part):
        start, count = UNITS[unit]
        return pl.ds(pl.multiple_of(start + part * (count // 2), 32), count // 2)

    def share_rows(unit, part):
        start, count = UNITS[unit]
        return pl.ds(pl.multiple_of(start + outer(unit)[0] * (count // 2) + part * (count // 4), 16), count // 4)

    def half_slot(unit):
        return pl.ds(UNITS[unit][0] // 2, UNITS[unit][1] // 2)

    def share_slot(unit):
        return pl.ds(UNITS[unit][0] // 4, UNITS[unit][1] // 4)

    def outer_copy(unit):
        part, peer = outer(unit)
        return remote(
            grad.at[x, c, half_rows(unit, 1 - part)], y_buf.at[half_slot(unit)], sent.at[OUTER], ey_r.at[unit], peer
        )

    def early_slot(unit):
        count = UNITS[unit][1] // 2
        return pl.ds(EARLY.index(unit) * count, count)

    def early_copy(unit):
        index = EARLY.index(unit)
        part, peer = outer(unit)
        return remote(
            grad.at[nx, c, half_rows(unit, 1 - part)], early_buf.at[early_slot(unit)], sent.at[EARLY_OUT], early_r.at[index], peer
        )

    def inner_copy(unit):
        part, peer = inner(unit)
        return remote(
            grad.at[x, c, share_rows(unit, 1 - part)], z_buf.at[0, share_slot(unit)], sent.at[INNER], ez_r.at[unit], peer
        )

    def across_copy(unit):
        return remote(
            grad.at[x, c, share_rows(unit, inner(unit)[0])], z_buf.at[1, share_slot(unit)],
            sent.at[ACROSS], ew_r.at[unit], z_far,
        )

    def back_inner_copy(unit):
        part, peer = inner(unit)
        where = share_rows(unit, part)
        return remote(x_buf.at[where], x_buf.at[where], sent.at[BACK_INNER], fz_r.at[unit], peer)

    def back_outer_copy(unit):
        part, peer = outer(unit)
        where = half_rows(unit, part)
        return remote(x_buf.at[where], x_buf.at[where], sent.at[BACK_OUTER], fy_r.at[unit], peer)

    def early_x(unit):
        early_copy(unit).wait_recv()
        add_into(nx, half_rows(unit, outer(unit)[0]).start, UNITS[unit][1] // 2, early_buf, early_slot(unit).start)
        x_copy(unit).start()

    def early_y(unit):
        outer_copy(unit).wait_recv()
        add_into(x, half_rows(unit, outer(unit)[0]).start, UNITS[unit][1] // 2, y_buf, half_slot(unit).start)

    def early_z(unit):
        x_copy(unit).wait_recv()
        start = half_rows(unit, outer(unit)[0]).start
        add_into(x, start, UNITS[unit][1] // 2, x_buf, start)
        inner_copy(unit).start()

    def add_x(unit):
        x_copy(unit).wait_recv()
        start, count = UNITS[unit]
        add_into(x, start, count, x_buf, start)
        outer_copy(unit).start()

    def add_y(unit):
        outer_copy(unit).wait_recv()
        add_into(x, half_rows(unit, outer(unit)[0]).start, UNITS[unit][1] // 2, y_buf, half_slot(unit).start)
        inner_copy(unit).start()

    def add_z(unit):
        inner_copy(unit).wait_recv()
        start = share_rows(unit, inner(unit)[0]).start
        add_into(x, start, UNITS[unit][1] // 4, z_buf.at[0], share_slot(unit).start)
        across_copy(unit).start()

    def add_far(unit):
        across_copy(unit).wait_recv()
        where = share_rows(unit, inner(unit)[0])
        x_buf[where, :] = grad[x, c, where, :] + z_buf[1, share_slot(unit), :]
        back_inner_copy(unit).start()

    def give_y(unit):
        back_inner_copy(unit).wait_recv()
        back_outer_copy(unit).start()

    def out_copy(unit):
        where = pl.ds(*UNITS[unit])
        return pltpu.make_async_copy(x_buf.at[where], grads_out.at[where], local_sem.at[10])

    def finish(unit):
        back_outer_copy(unit).wait_recv()
        out_copy(unit).start()

    def sums_copy(slot, source, peer):
        return remote(sums_recv.at[6 + source], sums_recv.at[slot], sent.at[SUMS_OUT], sums_r.at[slot], peer)

    small_peers = [(i, i, peer) for i, peer in enumerate((mate, x_peer, y_peer, z_pair, z_far))]

    def sums_step(number):
        if number > 0:
            sums_copy(*small_peers[number - 1]).wait_recv()
            sums_recv[6 + number] = sums_recv[5 + number] + sums_recv[number - 1]
        else:
            sums_recv[6] = sums[...]
        if number < 5:
            sums_copy(*small_peers[number]).start()
        else:
            total = sums_recv[11]
            sums[...] = total
            own_up = sums[pl.ds(UPB + mp, 1), :]
            pairs = jnp.where(x == 0, total[:, :384], total[:, 384:])
            spread = jnp.where(placed, 1.0, 0.0)
            own_qv = lax.dot_general(
                pairs, spread, (((1,), (1,)), ((), ())), precision=lax.Precision.HIGHEST, preferred_element_type=F32
            )
            own_qv = jnp.concatenate([own_qv, jnp.zeros((16, width - own_qv.shape[1]), F32)], axis=1)
            total = jnp.where(tile_row == OWN_UP, own_up, total)
            total = jnp.where(tile_row == OWN_QV, own_qv[QUERYB : QUERYB + 1], total)
            sums[...] = jnp.where(tile_row == OWN_QV + 1, own_qv[VALUEB : VALUEB + 1], total)
            sums_out_copy.start()

    events = {
        BIAS_DONE: bias_done,
        MATE_DONE: mate_done,
        PASS_X: pass_x,
        PASS_Y: pass_y,
        PASS_DONE: pass_done,
        CORE_ADD: core_add,
        CORE_SEND: core_send,
        EARLY_X: early_x,
        EARLY_Y: early_y,
        EARLY_Z: early_z,
        ADD_X: add_x,
        ADD_Y: add_y,
        ADD_Z: add_z,
        ADD_FAR: add_far,
        GIVE_Y: give_y,
        FINISH: finish,
        SUMS: sums_step,
    }

    def run_due(due):
        for name, number in due:
            events[name](number)

    def due_now(step, plan):
        def among(low, high):
            if high - low == 1:
                run_due(plan[low])
                return
            middle = (low + high) // 2
            for first, last, here in ((low, middle, step < middle), (middle, high, step >= middle)):
                if any(plan[first:last]):
                    pl.when(here)(functools.partial(among, first, last))

        among(0, len(plan))

    lax.fori_loop(0, tokens // chunk, first_norm, 0)

    def forward_step(step, carry):
        due_now(step, PLAN_FORWARD)
        pl.when(step % 3 == 0)(lambda: project(step))
        pl.when(step % 3 > 0)(lambda: attend_forward(step))
        return carry

    lax.fori_loop(0, 18, forward_step, 0)
    lax.fori_loop(0, tokens // 256, second_norm, 0)
    sums[...] = jnp.zeros_like(sums)
    locals_[7].wait()

    def main_step(step, carry):
        due_now(step, PLAN_MAIN)
        pl.when(step < BETWEEN)(lambda: expert_tile(step))
        pl.when(step == BETWEEN)(between_norm)
        pl.when(step == BETWEEN + 1)(between_out)
        pl.when(step == BETWEEN + 2)(between_back)
        pl.when(jnp.logical_and(step >= FIRST_HEADS, step < LAST_NORM))(
            lambda: attend_backward(step - FIRST_HEADS)
        )
        pl.when(jnp.logical_and(step >= LAST_NORM, step < MIX))(lambda: last_norm(step - LAST_NORM))
        pl.when(step >= MIX)(lambda: mix(step - MIX))
        return carry

    lax.fori_loop(0, MIX + tokens // 256, main_step, 0)
    run_due(PLAN_DRAIN)

    shard_rows = grad.shape[2]
    own = grad.at[0, 0]
    rows_sent = {
        TO_MATE: shard_rows, TO_X: shard_rows // 4, TO_Y: shard_rows // 4, TO_Z: shard_rows // 4,
        TO_CORNER: shard_rows // 4, FORWARD: shard_rows, BIAS: 3 * 16,
        EARLY_OUT: sum(UNITS[unit][1] for unit in EARLY) // 2,
        X_OUT: sum(count // 2 if unit in EARLY else count for unit, (_, count) in enumerate(UNITS)),
        OUTER: shard_rows // 2, INNER: shard_rows // 4, ACROSS: shard_rows // 4, BACK_INNER: shard_rows // 4,
        BACK_OUTER: shard_rows // 2,
    }
    for kind, count in rows_sent.items():
        all_rows = own.at[pl.ds(0, count)]
        remote(all_rows, all_rows, sent.at[kind], wb_r.at[0], mate).wait_send()
    remote(grad.at[0], grad.at[0], sent.at[CORE], wb_r.at[0], mate).wait_send()
    all_sums = sums_recv.at[pl.ds(0, 5)]
    remote(all_sums, all_sums, sent.at[SUMS_OUT], wb_r.at[0], mate).wait_send()
    mixed_copy.wait()
    input_copy.wait()
    sums_out_copy.wait()
    pltpu.make_async_copy(x_buf, grads_out, local_sem.at[10]).wait()


def tail_kernel(
    mixed_in, input_in, grads_in, sums_in,
    mixed_out, input_out, qkv_out, wout_out, up_out, down_out,
    qv_out, gain1_out, shift1_out, outb_out, gain2_out, shift2_out, downb_out, upb_out,
    mixed, inputs, grads, qkv, wout, up, down, sums_ref, qv_ref, in_sem, out_sem, small_sem, *vectors,
):
    tiles = down.shape[0]
    heads = qkv.shape[1]
    copies = [
        pltpu.make_async_copy(mixed_in, mixed, in_sem.at[0]),
        pltpu.make_async_copy(input_in, inputs, in_sem.at[1]),
    ]
    loads = []
    for index in range(tiles + 1):
        rows = pl.ds(index * 2 * UNIT, 2 * UNIT if index < tiles else 3 * UNIT)
        loads.append(pltpu.make_async_copy(grads_in.at[rows], grads.at[rows], in_sem.at[2 + index]))
    sums_copy = pltpu.make_async_copy(sums_in, sums_ref, small_sem.at[8])
    for copy in copies + loads + [sums_copy]:
        copy.start()
    stores = [
        pltpu.make_async_copy(mixed, mixed_out, out_sem.at[2 * tiles + 2]),
        pltpu.make_async_copy(inputs, input_out, out_sem.at[2 * tiles + 3]),
    ]
    for copy, store in zip(copies, stores):
        copy.wait()
        store.start()
    for index in range(tiles):
        loads[index].wait()
        start = index * 2 * UNIT
        down[index] = grads[start + UNIT : start + 2 * UNIT, :].astype(F32)
        stores.append(pltpu.make_async_copy(down.at[index], down_out.at[index], out_sem.at[2 * index]))
        stores[-1].start()
        lanes = pl.ds(index * UNIT, UNIT)
        up[:, lanes] = grads[start : start + UNIT, :].astype(F32).T
        stores.append(pltpu.make_async_copy(up.at[:, lanes], up_out.at[:, lanes], out_sem.at[2 * index + 1]))
        stores[-1].start()
    loads[tiles].wait()
    start = 2 * tiles * UNIT
    wout[...] = grads[start : start + heads * HEAD, :].astype(F32)
    stores.append(pltpu.make_async_copy(wout, wout_out, out_sem.at[2 * tiles]))
    stores[-1].start()
    start += heads * HEAD
    for head in range(heads):
        for part in range(3):
            row = start + (head * 3 + part) * HEAD
            qkv[part, head] = grads[row : row + HEAD, :].astype(F32)
    stores.append(pltpu.make_async_copy(qkv, qkv_out, out_sem.at[2 * tiles + 1]))
    stores[-1].start()
    sums_copy.wait()
    for index, (row, out) in enumerate((
        (GAIN1, gain1_out), (SHIFT1, shift1_out), (OUTB, outb_out), (GAIN2, gain2_out), (SHIFT2, shift2_out),
        (DOWNB, downb_out), (OWN_UP, upb_out),
    )):
        vectors[index][...] = sums_ref[row, :]
        stores.append(pltpu.make_async_copy(vectors[index], out, small_sem.at[index]))
        stores[-1].start()
    qv_ref[...] = sums_ref[OWN_QV : OWN_QV + 2, : qv_ref.shape[1]]
    stores.append(pltpu.make_async_copy(qv_ref, qv_out, small_sem.at[7]))
    stores[-1].start()
    for copy in stores:
        copy.wait()


def on_device(
    tokens, segment_ids, cotangent, norm1_gain, norm1_shift, w_qkv, qv_bias, w_out, out_bias,
    norm2_gain, norm2_shift, w_up, up_bias, w_down, down_bias,
):
    rows, seq, width = tokens.shape
    count = rows * seq
    shard = w_up.shape[1]
    heads = w_out.shape[0] // HEAD
    tiles = shard // UNIT
    units = 2 * tiles + 3
    qkv_rows = jnp.transpose(w_qkv, (1, 2, 0)).reshape(3, heads, HEAD, width)

    any_space = pl.BlockSpec(memory_space=pl.ANY)
    dma = pltpu.SemaphoreType.DMA
    vm = pltpu.VMEM
    mixed, input_grad, grads, sums, _ = pl.pallas_call(
        functools.partial(kernel, rows=rows, seq=seq),
        out_shape=(
            jax.ShapeDtypeStruct((count, width), BF16),
            jax.ShapeDtypeStruct((count, width), BF16),
            jax.ShapeDtypeStruct((units * UNIT, width), BF16),
            jax.ShapeDtypeStruct((16, width), F32),
            jax.ShapeDtypeStruct((4 * tiles, count, UNIT), BF16),
        ),
        in_specs=[any_space] * 15,
        out_specs=(any_space,) * 5,
        scratch_shapes=[
            vm((2, heads, 3, 2, HEAD, width), BF16),
            vm((2, heads, 2, HEAD, width), BF16),
            vm((2, 2, tiles, 2 * UNIT, width), BF16),
            vm((2, 2, 16, width), BF16),
            vm((2, 2, units * UNIT, width), BF16),
            vm((2, 2 * UNIT, width), BF16),
            vm((sum(UNITS[unit][1] for unit in EARLY) // 2, width), BF16),
            vm((units * UNIT, width), BF16),
            vm((units * UNIT // 2, width), BF16),
            vm((2, units * UNIT // 4, width), BF16),
            vm((count, width), BF16),
            vm((count, width), BF16),
            vm((count, width), BF16),
            vm((count, 2 * heads * 3 * 128), BF16),
            vm((count, width), BF16),
            vm((count, width), F32),
            vm((count, width), BF16),
            vm((count, width), BF16),
            vm((count, width), F32),
            vm((2, count, UNIT), BF16),
            vm((count, UNIT), BF16),
            vm((count, 128), F32),
            vm((count, 128), BF16),
            vm((count, 128), BF16),
            vm((16, width), F32),
            vm((12, 16, width), F32),
            vm((rows, seq), jnp.int32),
            *[vm((width,), BF16)] * 7,
            vm((2, heads * HEAD), BF16),
            dma((10,)),
            dma((11,)), dma((2,)), dma((12,)), dma((KINDS,)),
            *[dma((PIECES,))] * 6, dma((3,)),
            dma((len(GRANULES),)), dma((len(EARLY),)), *[dma((len(UNITS),))] * 6, dma((5,)),
        ],
        compiler_params=pltpu.CompilerParams(
            collective_id=0, has_side_effects=True, vmem_limit_bytes=64 * 2**20 - 2**16
        ),
    )(
        tokens.reshape(count, width), cotangent.reshape(count, width), segment_ids,
        norm1_gain, norm1_shift, out_bias, norm2_gain, norm2_shift, down_bias, up_bias, qv_bias,
        qkv_rows, w_out.reshape(heads, HEAD, width), w_up, w_down.reshape(tiles, UNIT, width),
    )

    groups = lax.axis_size("dp") // 8
    if groups > 1:
        grads, sums = lax.psum((grads.astype(F32) * 0.125, sums * 0.125), "dp")
    whole = [jax.ShapeDtypeStruct((width,), F32)] * 7
    results = pl.pallas_call(
        tail_kernel,
        out_shape=(
            mixed, input_grad,
            jax.ShapeDtypeStruct((3, heads, HEAD, width), F32), jax.ShapeDtypeStruct((heads * HEAD, width), F32),
            jax.ShapeDtypeStruct((width, shard), F32), jax.ShapeDtypeStruct((tiles, UNIT, width), F32),
            jax.ShapeDtypeStruct((2, heads * HEAD), F32), *whole,
        ),
        in_specs=[any_space] * 4,
        out_specs=(any_space,) * 14,
        scratch_shapes=[
            vm((count, width), BF16), vm((count, width), BF16), vm(grads.shape, grads.dtype),
            vm((3, heads, HEAD, width), F32), vm((heads * HEAD, width), F32),
            vm((width, shard), F32), vm((tiles, UNIT, width), F32),
            vm((16, width), F32), vm((2, heads * HEAD), F32),
            dma((2 + tiles + 1,)), dma((2 * tiles + 4,)), dma((9,)),
            *[vm((width,), F32)] * 7,
        ],
        compiler_params=pltpu.CompilerParams(vmem_limit_bytes=63 * 2**20),
    )(mixed, input_grad, grads, sums)
    mixed, input_grad, grad_qkv, grad_out, grad_up, grad_down, grad_qv, *vectors = results
    gain1, shift1, outb, gain2, shift2, downb, upb = vectors
    return (
        mixed.reshape(rows, seq, width),
        input_grad.reshape(rows, seq, width),
        gain1,
        shift1,
        jnp.transpose(grad_qkv.reshape(3, heads * HEAD, width), (2, 0, 1)),
        grad_qv,
        grad_out,
        outb,
        gain2,
        shift2,
        grad_up,
        upb,
        grad_down.reshape(shard, width),
        downb,
    )


def solution(mesh):
    tall = P(("dp", "mp"), None, None)
    return jax.shard_map(
        on_device,
        mesh=mesh,
        in_specs=(
            tall, P(("dp", "mp"), None), tall, P(), P(), P(None, None, "mp"), P(None, "mp"), P("mp", None),
            P(), P(), P(), P(None, "mp"), P("mp"), P("mp", None), P(),
        ),
        out_specs=(
            tall, tall, P(), P(), P(None, None, "mp"), P(None, "mp"), P("mp", None), P(), P(), P(),
            P(None, "mp"), P("mp"), P("mp", None), P(),
        ),
        check_vma=False,
    )
```
